32 devices in a mesh: seq: 8 (over z, y), head: 4 (over x, core).
Axes of the slice: x: 2, y: 2, z: 4, core: 2. Of those that a mesh axis runs over, the one named last changes fastest.
Arguments:
- block_input: bfloat16 [3072, 1024], P('seq'), may hold values from -6 to 6
- cotangent: bfloat16 [3072, 1024], P('seq'), may hold values from -6 to 6
- segment_ids: int32 [3072], P('seq'), may hold values from 0 to 98, as said below
- norm_gain: float32 [1024], replicated, may hold values from 0.5 to 1.5
- w_query: bfloat16 [1024, 1024], P(None, 'head'), may hold values from -0.1875 to 0.1875
- w_key: bfloat16 [1024, 1024], P(None, 'head'), may hold values from -0.1875 to 0.1875
- w_value: bfloat16 [1024, 1024], P(None, 'head'), may hold values from -0.1875 to 0.1875
- w_gate: bfloat16 [1024, 1024], P(None, 'head'), may hold values from -0.1875 to 0.1875
- w_beta: bfloat16 [1024, 8], P(None, 'head'), may hold values from -0.1875 to 0.1875
- beta_bias: float32 [8], P('head'), may hold values from -8 to 2
- conv_weight: float32 [3, 4, 1024], P(None, None, 'head'), may hold values from -3 to 3
- head_gain: float32 [128], replicated, may hold values from 0.5 to 1.5
- w_out: bfloat16 [1024, 1024], P('head'), may hold values from -0.375 to 0.375
- ffn_gain: float32 [1024], replicated, may hold values from 0.5 to 1.5
- w_ffn_gate: bfloat16 [1024, 2816], P(None, 'head'), may hold values from -0.1875 to 0.1875
- w_ffn_up: bfloat16 [1024, 2816], P(None, 'head'), may hold values from -0.1875 to 0.1875
- w_ffn_down: bfloat16 [2816, 1024], P('head'), may hold values from -0.21875 to 0.21875
Outputs:
- block_output: bfloat16 [3072, 1024], P('seq')
- input_grad: float32 [3072, 1024], P('seq')
- norm_gain_grad: float32 [1024], replicated
- w_query_grad: float32 [1024, 1024], P('seq', 'head')
- w_key_grad: float32 [1024, 1024], P('seq', 'head')
- w_value_grad: float32 [1024, 1024], P('seq', 'head')
- w_gate_grad: float32 [1024, 1024], P('seq', 'head')
- w_beta_grad: float32 [1024, 8], P('seq', 'head')
- beta_bias_grad: float32 [8], P('head')
- conv_weight_grad: float32 [3, 4, 1024], P(None, None, 'head')
- head_gain_grad: float32 [128], replicated
- w_out_grad: float32 [1024, 1024], P('head', 'seq')
- ffn_gain_grad: float32 [1024], replicated
- w_ffn_gate_grad: float32 [1024, 2816], P('seq', 'head')
- w_ffn_up_grad: float32 [1024, 2816], P('seq', 'head')
- w_ffn_down_grad: float32 [2816, 1024], P('head', 'seq')
The draws below stay inside these ranges and needn't reach their ends.
Inputs may be any that keep to these rules, and one draw needn't show every extreme that they name: `segment_ids`: segment ids start at 0, never fall and rise by at most one from a token to the next; one document starts within the first 384 tokens and reaches into the last 384 tokens; the others have very unequal lengths.
All inputs are finite; a program needn't handle non-finite values.
Results may differ from the reference program's by a relative error of at most 0.04.
Values may be sent and summed in bfloat16 or wider, within the bound.
No kernel may reach another device: no remote copies, remote signals or barrier semaphores. Data moves between devices by JAX's collectives and lax.ppermute only.
A program may use at most 128 MiB of HBM per device.

```python
import math
import jax
import jax.numpy as jnp
from jax import lax

D = 1024
H = 8
HEAD_DIM = 128
FF = 2816
TOK_DEV = 384
SPAN = 64
CONV = 4
TOKENS = 3072
N_HEAD = 4


def draw_segment_ids(key, part):
    key_start, key_end, key_level, key_bits = jax.random.split(key, 4)
    doc_begin = jax.random.randint(key_start, (), TOK_DEV // 2, TOK_DEV)
    doc_finish = jax.random.randint(key_end, (), TOKENS - TOK_DEV + 1, TOKENS - TOK_DEV // 2 + 1)
    levels = jax.random.randint(key_level, (TOKENS // SPAN,), 0, 5)
    level_rows = jnp.repeat(levels, SPAN)
    random_bits = jnp.right_shift(jax.random.randint(key_bits, (TOKENS,), 0, 16384), 2 * level_rows)
    position = jnp.arange(TOKENS, dtype=jnp.int32)
    eligible = (position >= 1) & (position < doc_begin) | (position > doc_finish)
    scores = jnp.where(eligible, random_bits * TOKENS + position, -1)
    picked = lax.top_k(scores, TOK_DEV // 4)[1]
    boundary = jnp.zeros((TOKENS,), jnp.int32).at[picked].set(1)
    boundary = jnp.where((position == doc_begin) | (position == doc_finish), 1, boundary)
    return jnp.cumsum(boundary).astype(jnp.int32)


def draw_beta_bias(key, part):
    key_order, key_slow, key_fast = jax.random.split(jax.random.fold_in(key, 17), 3)
    order = jax.random.permutation(key_order, H)
    slow_count = H // 2
    slow_heads = order < slow_count
    slow_level = jnp.float32(math.log(HEAD_DIM / TOKENS)) + jax.random.uniform(key_slow, (H,), jnp.float32, -0.5, 0.5)
    fast_level = jax.random.uniform(key_fast, (H,), jnp.float32, 0.0, 2.0)
    return jnp.where(slow_heads, slow_level, fast_level).astype(jnp.float32)


def steps_of(key, dims, cuts, least, largest):
    level = 1.0
    for axis_at, blocks in cuts:
        steps = jax.random.uniform(jax.random.fold_in(jax.random.fold_in(key, 6), axis_at), (blocks,), jnp.float32, least / len(cuts), largest / len(cuts))
        level = level * jnp.repeat(jnp.exp(steps), dims[axis_at] // blocks).reshape((-1,) + (1,) * (len(dims) - 1 - axis_at))
    return level


def scatter_about(key, extent, width, limit, pieces=(), kind=jnp.bfloat16):
    values = width * jax.random.normal(key, extent, jnp.float32)
    if pieces:
        values = values * steps_of(key, extent, pieces, -0.22, 0.18)
    return jnp.clip(values, -limit, limit).astype(kind)


def setup_inputs(seed: int = 0) -> dict:
    keys = jax.random.split(jax.random.key(seed), 18)
    block_input = scatter_about(keys[0], (TOKENS, D), 1.0, 6.0, ((0, 8),))
    cotangent = scatter_about(keys[1], (TOKENS, D), 1.0, 6.0, ((0, 8),))
    segment_ids = draw_segment_ids(jax.random.fold_in(keys[17], 71), 0)
    norm_gain = jnp.clip(1.0 + 0.1 * jax.random.normal(keys[3], (D,), jnp.float32), 0.5, 1.5)
    w_query = scatter_about(keys[4], (D, D), D ** -0.5, 0.1875, ((1, 4),))
    w_key = scatter_about(keys[5], (D, D), D ** -0.5, 0.1875, ((1, 4),))
    w_value = scatter_about(keys[6], (D, D), D ** -0.5, 0.1875, ((1, 4),))
    w_gate = scatter_about(keys[7], (D, D), D ** -0.5, 0.1875, ((1, 4),))
    w_beta = scatter_about(keys[8], (D, H), D ** -0.5, 0.1875, ((1, 4),))
    beta_bias = draw_beta_bias(jax.random.fold_in(keys[17], 71), 0)
    conv_weight = scatter_about(keys[10], (3, CONV, D), CONV ** -0.5, 3.0, ((2, 4),), jnp.float32)
    head_gain = jnp.clip(1.0 + 0.1 * jax.random.normal(keys[11], (HEAD_DIM,), jnp.float32), 0.5, 1.5)
    w_out = scatter_about(keys[12], (D, D), (D // 4) ** -0.5, 0.375, ((0, 4),))
    ffn_gain = jnp.clip(1.0 + 0.1 * jax.random.normal(keys[13], (D,), jnp.float32), 0.5, 1.5)
    w_ffn_gate = scatter_about(keys[14], (D, FF), D ** -0.5, 0.1875, ((1, 4),))
    w_ffn_up = scatter_about(keys[15], (D, FF), D ** -0.5, 0.1875, ((1, 4),))
    w_ffn_down = scatter_about(keys[16], (FF, D), (FF // 4) ** -0.5, 0.21875, ((0, 4),))
    return {"block_input": block_input, "cotangent": cotangent, "segment_ids": segment_ids, "norm_gain": norm_gain, "w_query": w_query, "w_key": w_key, "w_value": w_value, "w_gate": w_gate, "w_beta": w_beta, "beta_bias": beta_bias, "conv_weight": conv_weight, "head_gain": head_gain, "w_out": w_out, "ffn_gain": ffn_gain, "w_ffn_gate": w_ffn_gate, "w_ffn_up": w_ffn_up, "w_ffn_down": w_ffn_down}


top_precision = lax.Precision.HIGHEST

@jax.custom_vjp
def low(v):
    return lax.optimization_barrier(v.astype(jnp.bfloat16)).astype(jnp.float32)

@jax.custom_vjp
def low_back(v):
    return v

def low_keep(v):
    return (low(v), None)

def low_pass(kept, grad):
    return (grad,)

def back_keep(v):
    return (v, None)

def back_low(kept, grad):
    return (low(grad),)
low.defvjp(low_keep, low_pass)
low_back.defvjp(back_keep, back_low)

def hdot(left_vals, right_vals):
    return jnp.dot(left_vals, right_vals, precision=top_precision, preferred_element_type=jnp.float32)

def rms_scale(row_vals, gain_vec):
    return row_vals * lax.rsqrt(lax.optimization_barrier(jnp.mean(row_vals * row_vals, axis=-1, keepdims=True)) + 1e-06) * gain_vec

def head_scale(mix_out, gate_raw, gain_vec):
    gate_heads = gate_raw.reshape(mix_out.shape)
    scaled = mix_out * lax.rsqrt(lax.optimization_barrier(jnp.mean(mix_out * mix_out, axis=-1, keepdims=True)) + 1e-05) * gain_vec * jax.nn.silu(gate_heads)
    return scaled.reshape(mix_out.shape[0], mix_out.shape[1] * mix_out.shape[2])

def gated_unit(gate_vals, up_vals):
    return jax.nn.silu(gate_vals) * up_vals

def unit_inverse(matrix):
    size_rows = matrix.shape[0]
    row_ids = lax.broadcasted_iota(jnp.int32, (size_rows, size_rows), 0)
    col_ids = lax.broadcasted_iota(jnp.int32, (size_rows, size_rows), 1)
    inverse = jnp.eye(size_rows, dtype=jnp.float32)
    block_width = 1
    while block_width < size_rows:
        within = (row_ids // (2 * block_width) == col_ids // (2 * block_width)) & (row_ids // block_width != col_ids // block_width)
        coupling = jnp.where(within, matrix, 0.0)
        inverse = inverse - jnp.dot(jnp.dot(inverse, coupling, precision=top_precision), inverse, precision=top_precision)
        block_width = block_width * 2
    return inverse

def span_step(state, query_rows, key_rows, value_rows, beta_vals, seg_rows, prev_seg):
    size_rows = query_rows.shape[0]
    row_ids = lax.broadcasted_iota(jnp.int32, (size_rows, size_rows), 0)
    col_ids = lax.broadcasted_iota(jnp.int32, (size_rows, size_rows), 1)
    same_doc = (seg_rows[:, None] == seg_rows[None, :]).astype(jnp.float32)
    opened = (seg_rows == prev_seg).astype(jnp.float32)
    closing = (seg_rows == seg_rows[size_rows - 1]).astype(jnp.float32)
    kept_flag = opened[size_rows - 1]
    key_inner = jnp.dot(key_rows, key_rows.T, precision=top_precision) * same_doc
    system = jnp.eye(size_rows, dtype=jnp.float32) + jnp.where(row_ids > col_ids, key_inner * beta_vals[:, None], 0.0)
    inverse = unit_inverse(system)
    w_rows = jnp.dot(inverse, beta_vals[:, None] * key_rows, precision=top_precision)
    u_rows = jnp.dot(inverse, beta_vals[:, None] * value_rows, precision=top_precision)
    fresh = u_rows - opened[:, None] * jnp.dot(w_rows, state, precision=top_precision)
    scores = jnp.where(row_ids >= col_ids, jnp.dot(query_rows, key_rows.T, precision=top_precision) * same_doc, 0.0)
    output = opened[:, None] * jnp.dot(query_rows, state, precision=top_precision) + jnp.dot(scores, fresh, precision=top_precision)
    new_state = kept_flag * state + jnp.dot((closing[:, None] * key_rows).T, fresh, precision=top_precision)
    return (new_state, output)

def scan_blocks(queries, key_rows, value_rows, beta_vals, segment_ids, first_prev, start_state):
    block_count = queries.shape[0] // SPAN
    tails = segment_ids[SPAN - 1::SPAN].astype(jnp.int32)
    prev_ids = jnp.concatenate([jnp.reshape(first_prev, (1,)).astype(jnp.int32), tails[:block_count - 1]])

    def blocked(array):
        return array.reshape((block_count, SPAN) + array.shape[1:])
    stepper = jax.vmap(span_step, in_axes=(0, 1, 1, 1, 1, None, None), out_axes=(0, 1))

    def advance(state, inputs):
        q_block, k_block, v_block, b_block, s_block, p_block = inputs
        return stepper(state, q_block, k_block, v_block, b_block, s_block, p_block)
    final_state, outputs = lax.scan(jax.checkpoint(advance), start_state, (blocked(queries), blocked(key_rows), blocked(value_rows), blocked(beta_vals), blocked(segment_ids), prev_ids))
    return (outputs.reshape(queries.shape), final_state)

def conv_mix(pre_vals, halo_rows, tap_rows, segment_ids, halo_ids):
    row_count = pre_vals.shape[0]
    lag_rows = halo_rows.shape[0]
    joined = jnp.concatenate([halo_rows, pre_vals], axis=0)
    joined_ids = jnp.concatenate([halo_ids, segment_ids], axis=0)
    mixed_sum = jnp.zeros_like(pre_vals)
    for lag_step in range(lag_rows + 1):
        offset = lag_rows - lag_step
        match_doc = (joined_ids[offset:offset + row_count] == segment_ids).astype(jnp.float32)
        mixed_sum = mixed_sum + tap_rows[lag_rows - lag_step] * joined[offset:offset + row_count] * match_doc[:, None]
    return jax.nn.silu(mixed_sum)

def unit_heads(mixed_act, heads_here):
    row_count = mixed_act.shape[0]
    part_width = mixed_act.shape[1] // 3
    query_raw = mixed_act[:, :part_width].reshape(row_count, heads_here, HEAD_DIM)
    key_raw = mixed_act[:, part_width:2 * part_width].reshape(row_count, heads_here, HEAD_DIM)
    value_rows = mixed_act[:, 2 * part_width:].reshape(row_count, heads_here, HEAD_DIM)
    queries = query_raw * lax.rsqrt(lax.optimization_barrier(jnp.sum(query_raw * query_raw, axis=-1, keepdims=True)) + 1e-06) * HEAD_DIM ** (-0.5)
    key_rows = key_raw * lax.rsqrt(lax.optimization_barrier(jnp.sum(key_raw * key_raw, axis=-1, keepdims=True)) + 1e-06)
    return (queries, key_rows, value_rows)

def group_sum(left_vals, right_vals):
    part_width = left_vals.shape[1] // N_HEAD
    total_sum = jnp.zeros((left_vals.shape[0], right_vals.shape[1]), jnp.float32)
    for group_index in range(N_HEAD):
        first_col = group_index * part_width
        total_sum = total_sum + low(hdot(left_vals[:, first_col:first_col + part_width], right_vals[first_col:first_col + part_width]))
    return total_sum

def forward(input_vals, gain_one, query_w, key_w, value_w, gate_w, beta_w, bias_beta, conv_w, gain_head, out_w, gain_two, ffn_gate_w, ffn_up_w, ffn_down_w, segment_ids):
    normed_one = low(rms_scale(input_vals, gain_one))
    projected = jnp.concatenate([hdot(normed_one, query_w), hdot(normed_one, key_w), hdot(normed_one, value_w)], axis=1)
    pre_vals = low_back(low(projected))
    gate_raw = low_back(hdot(normed_one, gate_w))
    beta_vals = jax.nn.sigmoid(low_back(hdot(normed_one, beta_w)) + bias_beta)
    tap_rows = jnp.transpose(conv_w, (1, 0, 2)).reshape(CONV, 3 * D)
    mixed_act = conv_mix(pre_vals, jnp.zeros((CONV - 1, 3 * D), jnp.float32), tap_rows, segment_ids, jnp.full((CONV - 1,), -1, jnp.int32))
    queries, key_rows, value_rows = unit_heads(mixed_act, H)
    start_state = jnp.zeros((H, HEAD_DIM, HEAD_DIM), jnp.float32)
    mix_out, final_state = scan_blocks(queries, key_rows, value_rows, beta_vals, segment_ids, jnp.full((), -1, jnp.int32), start_state)
    head_low = low(head_scale(mix_out, gate_raw, gain_head))
    attention = low_back(group_sum(head_low, out_w))
    residual = input_vals + attention
    normed_two = low(rms_scale(residual, gain_two))
    gate_vals = low_back(hdot(normed_two, ffn_gate_w))
    up_vals = low_back(hdot(normed_two, ffn_up_w))
    hidden = low(gated_unit(gate_vals, up_vals))
    ffn_out = low_back(group_sum(hidden, ffn_down_w))
    return residual + ffn_out

def reference(block_input, cotangent, segment_ids, norm_gain, w_query, w_key, w_value, w_gate, w_beta, beta_bias, conv_weight, head_gain, w_out, ffn_gain, w_ffn_gate, w_ffn_up, w_ffn_down):

    def wrapped(input_vals, gain_one, query_w, key_w, value_w, gate_w, beta_w, bias_beta, conv_w, gain_head, out_w, gain_two, ffn_gate_w, ffn_up_w, ffn_down_w):
        return forward(input_vals, gain_one, query_w, key_w, value_w, gate_w, beta_w, bias_beta, conv_w, gain_head, out_w, gain_two, ffn_gate_w, ffn_up_w, ffn_down_w, segment_ids)
    output_vals, pull_back = jax.vjp(wrapped, block_input.astype(jnp.float32), norm_gain, w_query.astype(jnp.float32), w_key.astype(jnp.float32), w_value.astype(jnp.float32), w_gate.astype(jnp.float32), w_beta.astype(jnp.float32), beta_bias, conv_weight, head_gain, w_out.astype(jnp.float32), ffn_gain, w_ffn_gate.astype(jnp.float32), w_ffn_up.astype(jnp.float32), w_ffn_down.astype(jnp.float32))
    grad_list = pull_back(cotangent.astype(jnp.float32))
    return (output_vals.astype(jnp.bfloat16), grad_list[0], grad_list[1], grad_list[2], grad_list[3], grad_list[4], grad_list[5], grad_list[6], grad_list[7], grad_list[8], grad_list[9], grad_list[10], grad_list[11], grad_list[12], grad_list[13], grad_list[14])
```

```python
import functools

import jax
import jax.numpy as jnp
from jax import lax
from jax.experimental import pallas as pl
from jax.experimental.pallas import tpu as pltpu
from jax.sharding import PartitionSpec as P

HEAD_DIM = 128
CHUNK = 128
LANES = 128
SUB = 8
Q_SCALE = HEAD_DIM ** (-0.5)
VMEM_BYTES = 56 * 1024 * 1024

bf16 = jnp.bfloat16
f32 = jnp.float32


def mm(left, right, left_dim=1, right_dim=0):
    return lax.dot_general(
        left.astype(bf16),
        right.astype(bf16),
        (((left_dim,), (right_dim,)), ((), ())),
        preferred_element_type=f32,
    )


def sigmoid(value):
    return 1.0 / (1.0 + jnp.exp(-value))


def kernel_call(body, out_shapes, *args, scratch=(), name, flops=0):
    vmem = pl.BlockSpec(memory_space=pltpu.VMEM)
    smem = pl.BlockSpec(memory_space=pltpu.SMEM)
    moved = sum(a.size * a.dtype.itemsize for a in args)
    moved += sum(o.size * o.dtype.itemsize for o in out_shapes)
    return pl.pallas_call(
        body,
        out_shape=tuple(out_shapes),
        in_specs=[smem] + [vmem] * (len(args) - 1),
        out_specs=tuple([vmem] * len(out_shapes)),
        scratch_shapes=list(scratch),
        compiler_params=pltpu.CompilerParams(vmem_limit_bytes=VMEM_BYTES),
        cost_estimate=pl.CostEstimate(flops=int(flops), bytes_accessed=int(moved), transcendentals=0),
        name=name,
    )(*args)


def shaped(shape, dtype):
    return jax.ShapeDtypeStruct(tuple(shape), dtype)


def swap(value, axis, bit):
    count = lax.axis_size(axis)
    return lax.ppermute(value, axis, [(s, s ^ bit) for s in range(count)])


def shift(value, axis, step):
    count = lax.axis_size(axis)
    return lax.ppermute(
        value, axis, [(s, s + step) for s in range(count) if 0 <= s + step < count]
    )


def bit_of(place_ref, which, bit):
    return lax.rem(lax.shift_right_logical(place_ref[which], bit), 2)


def chosen(flag, when_one, when_zero):
    return jnp.where(flag == 1, when_one, when_zero)


def tri_masks():
    rows = lax.broadcasted_iota(jnp.int32, (CHUNK, CHUNK), 0)
    cols = lax.broadcasted_iota(jnp.int32, (CHUNK, CHUNK), 1)
    return rows, cols


def unit_inverses(lowers):
    rows, cols = tri_masks()
    eye = jnp.where(rows == cols, 1.0, 0.0).astype(f32)
    width = 1
    inverses = None
    while width < CHUNK:
        shift_bits = width.bit_length() - 1
        row_block = lax.shift_right_logical(rows, shift_bits)
        col_block = lax.shift_right_logical(cols, shift_bits)
        within = (
            lax.shift_right_logical(row_block, 1) == lax.shift_right_logical(col_block, 1)
        ) & (row_block != col_block)
        couplings = [jnp.where(within, low, 0.0) for low in lowers]
        if inverses is None:
            inverses = [eye - coupling for coupling in couplings]
        else:
            halves = [mm(inv, coupling) for inv, coupling in zip(inverses, couplings)]
            inverses = [inv - mm(half, inv) for inv, half in zip(inverses, halves)]
        width *= 2
    return inverses


def project_kernel(
    place, x_ref, gain_ref, wq_ref, wk_ref, wv_ref, wg_ref, wb_ref, bias_ref, seg_ref,
    a_ref, p_ref, gate_ref, beta_ref, segc_ref, tail_ref,
):
    rows = x_ref.shape[0]
    head_width = wq_ref.shape[1]
    x = x_ref[...].astype(f32)
    scale = lax.rsqrt(jnp.mean(x * x, axis=-1, keepdims=True) + 1e-06)
    a = (x * scale * gain_ref[...]).astype(bf16)
    a_ref[...] = a
    for part, w_ref in enumerate((wq_ref, wk_ref, wv_ref)):
        value = mm(a, w_ref[...])
        cols = slice(part * head_width, (part + 1) * head_width)
        low = value.astype(bf16)
        p_ref[:, cols] = low
        tail_ref[:, cols] = low.astype(f32)[rows - SUB :, :]
    gate_ref[...] = mm(a, wg_ref[...])
    logits = mm(a, wb_ref[...])
    for head in range(head_width // LANES):
        column = logits[:, head : head + 1] + bias_ref[:, head : head + 1]
        beta_ref[:, head * LANES : (head + 1) * LANES] = sigmoid(
            jnp.broadcast_to(column, (rows, LANES))
        )
    for chunk in range(rows // CHUNK):
        ids = jnp.broadcast_to(seg_ref[chunk : chunk + 1, :], (CHUNK, LANES))
        turned = ids.T
        segc_ref[chunk * CHUNK : (chunk + 1) * CHUNK, :] = turned
        if chunk == rows // CHUNK - 1:
            tail_ref[:, 3 * head_width :] = turned[CHUNK - SUB :, :]


def fill_joined(p_ref, tail_ref, segc_ref, joined, joined_ids):
    width = p_ref.shape[1]
    rows = p_ref.shape[0]
    joined[0:SUB, :] = tail_ref[:, :width]
    joined[SUB : SUB + rows, :] = p_ref[...].astype(f32)
    joined_ids[0:SUB, :] = tail_ref[:, width:]
    joined_ids[SUB : SUB + rows, :] = segc_ref[...]


def lag_masks(joined_ids, segc_ref, lags):
    rows = segc_ref.shape[0]
    ids = segc_ref[...]
    return [None] + [
        jnp.where(joined_ids[SUB - lag : SUB - lag + rows, :] == ids, 1.0, 0.0)
        for lag in range(1, lags + 1)
    ]


def conv_sum(joined, taps_ref, masks, part, head, head_width, rows):
    lags = taps_ref.shape[1] - 1
    col = part * head_width + head * LANES
    tap_cols = slice(head * LANES, (head + 1) * LANES)
    total = taps_ref[part, lags : lags + 1, tap_cols] * joined[SUB : SUB + rows, col : col + LANES]
    for lag in range(1, lags + 1):
        tap = taps_ref[part, lags - lag : lags - lag + 1, tap_cols]
        total = total + tap * joined[SUB - lag : SUB - lag + rows, col : col + LANES] * masks[lag]
    return total


def chunk_flags(joined_ids, segc_ref, seg_ref, chunk):
    start = chunk * CHUNK
    ids = segc_ref[start : start + CHUNK, :]
    same = jnp.where(ids == seg_ref[chunk : chunk + 1, :], 1.0, 0.0)
    before = joined_ids[SUB + start - 1 : SUB + start, :]
    final = joined_ids[SUB + start + CHUNK - 1 : SUB + start + CHUNK, :]
    opened = jnp.where(ids == before, 1.0, 0.0)
    closing = jnp.where(ids == final, 1.0, 0.0)
    kept = jnp.where(final == before, 1.0, 0.0)
    return same, opened, closing, kept


def delta_kernel(
    place, p_ref, tail_ref, taps_ref, seg_ref, segc_ref, beta_ref,
    qkv_ref, w_ref, u_ref, qe_ref, pu_ref, r_ref, s_ref, d_ref, ku_ref, maps_ref,
    joined, joined_ids,
):
    rows, width = p_ref.shape
    head_width = width // 3
    heads = head_width // LANES
    chunks = rows // CHUNK
    fill_joined(p_ref, tail_ref, segc_ref, joined, joined_ids)
    masks = lag_masks(joined_ids, segc_ref, taps_ref.shape[1] - 1)
    for part in range(3):
        for head in range(heads):
            total = conv_sum(joined, taps_ref, masks, part, head, head_width, rows)
            z = total * sigmoid(total)
            if part < 2:
                z = z * lax.rsqrt(jnp.sum(z * z, axis=-1, keepdims=True) + 1e-06)
                if part == 0:
                    z = z * Q_SCALE
            col = part * head_width + head * LANES
            qkv_ref[:, col : col + LANES] = z.astype(bf16)
    row_ids, col_ids = tri_masks()
    flags = [chunk_flags(joined_ids, segc_ref, seg_ref, chunk) for chunk in range(chunks)]
    sets = [(head, chunk) for head in range(heads) for chunk in range(chunks)]

    def tile(ref, head, chunk, part=0):
        col = part * head_width + head * LANES
        return ref[chunk * CHUNK : (chunk + 1) * CHUNK, col : col + LANES]

    lowers = []
    for head, chunk in sets:
        same = flags[chunk][0]
        q, k = tile(qkv_ref, head, chunk, 0), tile(qkv_ref, head, chunk, 1)
        inner = mm(jnp.concatenate([q, k], axis=0), k, 1, 1)
        scores = jnp.where(row_ids >= col_ids, inner[:CHUNK] * same, 0.0)
        s_ref[chunk * CHUNK : (chunk + 1) * CHUNK, head * LANES : (head + 1) * LANES] = (
            scores.astype(bf16)
        )
        lowers.append(
            jnp.where(row_ids > col_ids, inner[CHUNK:] * same * tile(beta_ref, head, chunk), 0.0)
        )
    inverses = unit_inverses(lowers)
    eye = jnp.where(row_ids == col_ids, 1.0, 0.0).astype(f32)
    maps = [
        jnp.concatenate([eye, jnp.zeros((HEAD_DIM, HEAD_DIM), f32)], axis=1) for _ in range(heads)
    ]
    products = []
    for (head, chunk), inverse in zip(sets, inverses):
        beta = tile(beta_ref, head, chunk)
        k = tile(qkv_ref, head, chunk, 1).astype(f32)
        v = tile(qkv_ref, head, chunk, 2).astype(f32)
        both = jnp.concatenate([beta * k, beta * v], axis=1)
        products.append(mm(inverse, both))
    steps = {}
    for (head, chunk), inverse, product in zip(sets, inverses, products):
        same, opened, closing, kept = flags[chunk]
        at = (slice(chunk * CHUNK, (chunk + 1) * CHUNK), slice(head * LANES, (head + 1) * LANES))
        w_rows, u_rows = product[:, :HEAD_DIM], product[:, HEAD_DIM:]
        r_ref[at] = inverse.astype(bf16)
        w_ref[at] = w_rows.astype(bf16)
        u_ref[at] = u_rows.astype(bf16)
        both = jnp.concatenate([opened * w_rows, u_rows], axis=1)
        k = tile(qkv_ref, head, chunk, 1).astype(f32)
        q = tile(qkv_ref, head, chunk, 0).astype(f32)
        step = mm(closing * k, both, 0, 0)
        through = mm(s_ref[at], both)
        qe_ref[at] = (opened * q - through[:, :HEAD_DIM]).astype(bf16)
        pu_ref[at] = through[:, HEAD_DIM:].astype(bf16)
        d_ref[at] = step[:, :HEAD_DIM].astype(bf16)
        ku_ref[at] = step[:, HEAD_DIM:].astype(bf16)
        steps[head, chunk] = step
    for chunk in range(chunks):
        kept = flags[chunk][3]
        kept_wide = jnp.concatenate([kept, kept], axis=1)
        for head in range(heads):
            step = steps[head, chunk]
            pushed = kept_wide * maps[head] - mm(step[:, :HEAD_DIM], maps[head])
            maps[head] = jnp.concatenate(
                [pushed[:, :HEAD_DIM], pushed[:, HEAD_DIM:] + step[:, HEAD_DIM:]], axis=1
            )
    for head in range(heads):
        maps_ref[head * HEAD_DIM : (head + 1) * HEAD_DIM, :] = maps[head][:, :HEAD_DIM].astype(bf16)
        base = (heads + head) * HEAD_DIM
        maps_ref[base : base + HEAD_DIM, :] = maps[head][:, HEAD_DIM:].astype(bf16)


def scan_round_kernel(
    bit, first, place, own_ref, other_ref, prefix_ref, suffix_ref, total_ref, prefix_out, suffix_out
):
    upper = bit_of(place, 0, bit)
    heads = own_ref.shape[0] // (2 * HEAD_DIM)
    for head in range(heads):
        m_at = slice(head * HEAD_DIM, (head + 1) * HEAD_DIM)
        a_at = slice((heads + head) * HEAD_DIM, (heads + head + 1) * HEAD_DIM)
        own_m, own_a = own_ref[m_at, :].astype(f32), own_ref[a_at, :].astype(f32)
        other_m, other_a = other_ref[m_at, :].astype(f32), other_ref[a_at, :].astype(f32)
        high_m, high_a = chosen(upper, own_m, other_m), chosen(upper, own_a, other_a)
        low_m, low_a = chosen(upper, other_m, own_m), chosen(upper, other_a, own_a)
        total = mm(high_m, jnp.concatenate([low_m, low_a], axis=1))
        total_ref[m_at, :] = total[:, :HEAD_DIM].astype(bf16)
        total_ref[a_at, :] = (total[:, HEAD_DIM:] + high_a).astype(bf16)
        if first:
            rows, cols = tri_masks()
            eye = jnp.where(rows == cols, 1.0, 0.0).astype(f32)
            prefix_out[m_at, :] = chosen(upper, other_m, eye).astype(bf16)
            prefix_out[a_at, :] = chosen(upper, other_a, jnp.zeros_like(other_a)).astype(bf16)
            suffix_out[m_at, :] = chosen(upper, eye, other_m.T).astype(bf16)
        else:
            before_m, before_a = prefix_ref[m_at, :].astype(f32), prefix_ref[a_at, :].astype(f32)
            after_m = suffix_ref[m_at, :].astype(f32)
            joint = mm(before_m, jnp.concatenate([other_m, other_a], axis=1))
            prefix_out[m_at, :] = chosen(upper, joint[:, :HEAD_DIM], before_m).astype(bf16)
            prefix_out[a_at, :] = chosen(
                upper, joint[:, HEAD_DIM:] + before_a, before_a
            ).astype(bf16)
            suffix_out[m_at, :] = chosen(upper, after_m, mm(after_m, other_m, 1, 1)).astype(bf16)


def back_round_kernel(
    bit, first, place, own_maps, other_maps, suffix_m, own_ref, other_ref, after_ref,
    total_ref, after_out,
):
    upper = bit_of(place, 0, bit)
    heads = own_ref.shape[0] // HEAD_DIM
    for head in range(heads):
        at = slice(head * HEAD_DIM, (head + 1) * HEAD_DIM)
        own, other = own_ref[at, :].astype(f32), other_ref[at, :].astype(f32)
        low_m = chosen(upper, other_maps[at, :].astype(f32), own_maps[at, :].astype(f32))
        high, low = chosen(upper, own, other), chosen(upper, other, own)
        total_ref[at, :] = (mm(low_m, high, 0, 0) + low).astype(bf16)
        if first:
            after_out[at, :] = chosen(upper, jnp.zeros_like(other), other).astype(bf16)
        else:
            after = after_ref[at, :].astype(f32)
            after_out[at, :] = chosen(upper, after, mm(suffix_m[at, :], other) + after).astype(bf16)


def mixer_kernel(
    last_bit, place, seg_ref, segc_ref, tail_ref, prefix_ref, other_a_ref,
    qe_ref, pu_ref, d_ref, ku_ref, gate_ref, hgain_ref,
    y_ref, o_ref, state_ref, joined_ids,
):
    rows, head_width = qe_ref.shape
    heads = head_width // LANES
    width = tail_ref.shape[1] - LANES
    joined_ids[0:SUB, :] = tail_ref[:, width:]
    joined_ids[SUB : SUB + rows, :] = segc_ref[...]
    upper = bit_of(place, 0, last_bit)
    for head in range(heads):
        m_at = slice(head * HEAD_DIM, (head + 1) * HEAD_DIM)
        a_at = slice((heads + head) * HEAD_DIM, (heads + head + 1) * HEAD_DIM)
        before_m, before_a = prefix_ref[m_at, :], prefix_ref[a_at, :].astype(f32)
        state = chosen(upper, mm(before_m, other_a_ref[m_at, :]) + before_a, before_a)
        cols = slice(head * LANES, (head + 1) * LANES)
        for chunk in range(rows // CHUNK):
            at = (slice(chunk * CHUNK, (chunk + 1) * CHUNK), cols)
            kept = chunk_flags(joined_ids, segc_ref, seg_ref, chunk)[3]
            low = state.astype(bf16)
            state_ref[at] = low
            out = mm(qe_ref[at], low) + pu_ref[at].astype(f32)
            o_ref[at] = out
            state = kept * state - mm(d_ref[at], low) + ku_ref[at].astype(f32)
            gate = gate_ref[at]
            scale = lax.rsqrt(jnp.mean(out * out, axis=-1, keepdims=True) + 1e-05)
            y_ref[at] = (out * scale * hgain_ref[...] * (gate * sigmoid(gate))).astype(bf16)


def ffn_kernel(
    place, x_ref, g_ref, fgain_ref, wg_ref, wu_ref, wd_ref, *rest,
):
    *parts, h_ref, b_ref, hid_ref, dgate_ref, dup_ref, keep_ref, send_ref, whole = rest
    y_refs, wo_refs = parts[: len(parts) // 2], parts[len(parts) // 2 :]
    att = None
    for y_ref, wo_ref in zip(y_refs, wo_refs):
        for piece in range(y_ref.shape[0]):
            part = mm(y_ref[piece], wo_ref[piece])
            att = part if att is None else att + part
    h = x_ref[...].astype(f32) + att
    h_ref[...] = h
    scale = lax.rsqrt(jnp.mean(h * h, axis=-1, keepdims=True) + 1e-06)
    b = (h * scale * fgain_ref[...]).astype(bf16)
    b_ref[...] = b
    gate = mm(b, wg_ref[...])
    up = mm(b, wu_ref[...])
    sg = sigmoid(gate)
    act = gate * sg
    hid_ref[...] = (act * up).astype(bf16)
    dhid = mm(g_ref[...], wd_ref[...], 1, 1)
    dgate = (dhid * up * (sg * (1.0 + gate * (1.0 - sg)))).astype(bf16)
    dup = (dhid * act).astype(bf16)
    dgate_ref[...] = dgate
    dup_ref[...] = dup
    whole[...] = mm(dgate, wg_ref[...], 1, 1) + mm(dup, wu_ref[...], 1, 1)
    split_rows(place, whole, keep_ref, send_ref)


def split_rows(place, whole, keep_ref, send_ref):
    half = keep_ref.shape[0]
    core = bit_of(place, 1, 0)
    keep_ref[...] = whole[pl.ds(pl.multiple_of(core * half, half), half), :].astype(bf16)
    send_ref[...] = whole[pl.ds(pl.multiple_of((1 - core) * half, half), half), :].astype(bf16)


def join_rows(place, mine, theirs, whole):
    half = mine.shape[0]
    core = bit_of(place, 1, 0)
    whole[pl.ds(pl.multiple_of(core * half, half), half), :] = mine
    whole[pl.ds(pl.multiple_of((1 - core) * half, half), half), :] = theirs


def ffn_grads_kernel(place, b_ref, hid_ref, dgate_ref, dup_ref, g_ref, wd_ref,
                     ggate_ref, gup_ref, gdown_ref, keep_ref, send_ref, whole):
    whole[...] = mm(hid_ref[...], wd_ref[...])
    split_rows(place, whole, keep_ref, send_ref)
    ggate_ref[...] = mm(b_ref[...], dgate_ref[...], 0, 0).astype(bf16)
    gup_ref[...] = mm(b_ref[...], dup_ref[...], 0, 0).astype(bf16)
    gdown_ref[...] = mm(g_ref[...], hid_ref[...], 0, 0).astype(bf16)


def residual_back_kernel(
    place, mine_a, mine_b, theirs_a, theirs_b, h_ref, g_ref, fgain_ref, wo_ref, y_ref, o_ref,
    gate_ref, hgain_ref, seg_ref, segc_ref, tail_ref, qe_ref, d_ref,
    dh_ref, gh_ref, do_ref, dgr_ref, pull_ref, sums_ref, whole, joined_ids,
):
    rows, head_width = o_ref.shape
    heads = head_width // LANES
    width = tail_ref.shape[1] - LANES
    joined_ids[0:SUB, :] = tail_ref[:, width:]
    joined_ids[SUB : SUB + rows, :] = segc_ref[...]
    join_rows(
        place,
        mine_a[...].astype(f32) + mine_b[...].astype(f32),
        theirs_a[...].astype(f32) + theirs_b[...].astype(f32),
        whole,
    )
    h = h_ref[...]
    db = whole[...]
    scale = lax.rsqrt(jnp.mean(h * h, axis=-1, keepdims=True) + 1e-06)
    hat = h * scale
    prod = db * hat
    sums_ref[0:1, :] = jnp.sum(prod, axis=0, keepdims=True)
    inner = jnp.mean(prod * fgain_ref[...], axis=-1, keepdims=True)
    dh = g_ref[...].astype(f32) + scale * (db * fgain_ref[...] - hat * inner)
    dh_ref[...] = dh
    gh = dh.astype(bf16)
    gh_ref[...] = gh
    dy_all = mm(gh, wo_ref[...], 1, 1)
    hg_sum = jnp.zeros((1, LANES), f32)
    for head in range(heads):
        cols = slice(head * LANES, (head + 1) * LANES)
        out, gate, dy = o_ref[:, cols], gate_ref[:, cols], dy_all[:, cols]
        norm = lax.rsqrt(jnp.mean(out * out, axis=-1, keepdims=True) + 1e-05)
        hat_o = out * norm
        sg = sigmoid(gate)
        act = gate * sg
        hg_sum = hg_sum + jnp.sum(dy * hat_o * act, axis=0, keepdims=True)
        dgain = dy * hgain_ref[...]
        dgr_ref[:, cols] = (dgain * hat_o * (sg * (1.0 + gate * (1.0 - sg)))).astype(bf16)
        e = dgain * act
        do_ref[:, cols] = (norm * (e - hat_o * jnp.mean(e * hat_o, axis=-1, keepdims=True))).astype(bf16)
    sums_ref[1:2, :] = jnp.concatenate(
        [hg_sum, jnp.zeros((1, sums_ref.shape[1] - LANES), f32)], axis=1
    )
    chunks = rows // CHUNK
    pulls = [None] * heads
    for chunk in range(chunks - 1, -1, -1):
        kept = chunk_flags(joined_ids, segc_ref, seg_ref, chunk)[3]
        for head in range(heads):
            at = (slice(chunk * CHUNK, (chunk + 1) * CHUNK), slice(head * LANES, (head + 1) * LANES))
            local = mm(qe_ref[at], do_ref[at], 0, 0)
            if pulls[head] is not None:
                local = local + kept * pulls[head] - mm(d_ref[at], pulls[head], 0, 0)
            pulls[head] = local
    for head in range(heads):
        pull_ref[head * HEAD_DIM : (head + 1) * HEAD_DIM, :] = pulls[head].astype(bf16)


def delta_back_kernel(
    last_bit, place, p_ref, tail_ref, taps_ref, seg_ref, segc_ref, beta_ref,
    qkv_ref, w_ref, u_ref, r_ref, s_ref, d_ref, qe_ref, state_ref, do_ref,
    suffix_m, after_ref, other_ref,
    gp_ref, last_ref, halo_ref, gb_ref, gtaps_ref, gbias_ref,
    joined, joined_ids, dq_s, du_s, mask_s,
):
    rows, width = p_ref.shape
    head_width = width // 3
    heads = head_width // LANES
    chunks = rows // CHUNK
    lags = taps_ref.shape[1] - 1
    fill_joined(p_ref, tail_ref, segc_ref, joined, joined_ids)
    masks = lag_masks(joined_ids, segc_ref, lags)
    row_ids, col_ids = tri_masks()
    flags = [chunk_flags(joined_ids, segc_ref, seg_ref, chunk) for chunk in range(chunks)]
    upper = bit_of(place, 0, last_bit)
    sets = [(head, chunk) for head in range(heads) for chunk in range(chunks)]

    def at_of(head, chunk, part=0):
        col = part * head_width + head * LANES
        return (slice(chunk * CHUNK, (chunk + 1) * CHUNK), slice(col, col + LANES))

    state_grads = {}
    for head in range(heads):
        at = slice(head * HEAD_DIM, (head + 1) * HEAD_DIM)
        after = after_ref[at, :].astype(f32)
        grad = chosen(upper, after, mm(suffix_m[at, :], other_ref[at, :]) + after)
        for chunk in range(chunks - 1, -1, -1):
            state_grads[head, chunk] = grad
            if chunk:
                tile = at_of(head, chunk)
                low = grad.astype(bf16)
                grad = (
                    flags[chunk][3] * grad
                    - mm(d_ref[tile], low, 0, 0)
                    + mm(qe_ref[tile], do_ref[tile], 0, 0)
                )
    lane_ids = lax.broadcasted_iota(jnp.int32, (CHUNK, LANES), 1)
    gb_cols = [jnp.zeros((CHUNK, LANES), f32) for _ in range(chunks)]
    for head, chunk in sets:
        same, opened, closing, kept = flags[chunk]
        at = at_of(head, chunk)
        q, k, v = (qkv_ref[at_of(head, chunk, part)] for part in range(3))
        kf, vf = k.astype(f32), v.astype(f32)
        beta = beta_ref[at]
        state, do = state_ref[at], do_ref[at]
        scores, w_rows, u_rows, inverse = s_ref[at], w_ref[at], u_ref[at], r_ref[at]
        sgrad = state_grads[head, chunk].astype(bf16)
        fresh = (u_rows.astype(f32) - opened * mm(w_rows, state)).astype(bf16)
        dfresh = mm(scores, do, 0, 0) + mm(closing * kf, sgrad)
        dscore = jnp.where(row_ids >= col_ids, mm(do, fresh, 1, 1) * same, 0.0).astype(bf16)
        dw = -(opened * mm(dfresh, state, 1, 1))
        dx = mm(inverse, jnp.concatenate([dfresh, dw], axis=1), 0, 0)
        dxv, dxk = dx[:, :HEAD_DIM], dx[:, HEAD_DIM:]
        dlow = mm(dx, jnp.concatenate([u_rows, w_rows], axis=1), 1, 1)
        dlow = jnp.where(row_ids > col_ids, -dlow * same, 0.0)
        inner = mm(k, k, 1, 1)
        dbeta = jnp.sum(dxv * vf + dxk * kf + dlow * inner, axis=-1, keepdims=True)
        glow = (dlow * beta).astype(bf16)
        dq_s[at_of(head, chunk, 0)] = opened * mm(do, state, 1, 1) + mm(dscore, k)
        dq_s[at_of(head, chunk, 1)] = (
            beta * dxk
            + mm(dscore, q, 0, 0)
            + closing * mm(fresh, sgrad, 1, 1)
            + mm(glow, k)
            + mm(glow, k, 0, 0)
        )
        dq_s[at_of(head, chunk, 2)] = beta * dxv
        raw = jnp.broadcast_to(dbeta, (CHUNK, LANES)) * beta * (1.0 - beta)
        gb_cols[chunk] = jnp.where(lane_ids == head, raw, gb_cols[chunk])
    bias_sum = jnp.zeros((1, LANES), f32)
    for chunk in range(chunks):
        gb_ref[chunk * CHUNK : (chunk + 1) * CHUNK, :] = gb_cols[chunk].astype(bf16)
        bias_sum = bias_sum + jnp.sum(gb_cols[chunk], axis=0, keepdims=True)
    gbias_ref[...] = bias_sum
    du_s[0:SUB, :] = jnp.zeros((SUB, LANES), f32)
    du_s[SUB + rows :, :] = jnp.zeros((SUB, LANES), f32)
    for lag in range(1, lags + 1):
        mask_s[lag - 1, 0:SUB, :] = jnp.zeros((SUB, LANES), f32)
        mask_s[lag - 1, SUB : SUB + rows, :] = masks[lag]
        mask_s[lag - 1, SUB + rows :, :] = jnp.zeros((SUB, LANES), f32)
    for part in range(3):
        for head in range(heads):
            col = part * head_width + head * LANES
            cols = slice(col, col + LANES)
            tap_cols = slice(head * LANES, (head + 1) * LANES)
            total = conv_sum(joined, taps_ref, masks, part, head, head_width, rows)
            sg = sigmoid(total)
            grad = dq_s[:, cols]
            if part < 2:
                z = total * sg
                norm = lax.rsqrt(jnp.sum(z * z, axis=-1, keepdims=True) + 1e-06)
                hat = z * norm
                grad = norm * (grad - hat * jnp.sum(grad * hat, axis=-1, keepdims=True))
                if part == 0:
                    grad = grad * Q_SCALE
            grad = grad * (sg * (1.0 + total * (1.0 - sg)))
            du_s[SUB : SUB + rows, :] = grad
            dp = taps_ref[part, lags : lags + 1, tap_cols] * grad
            halo = jnp.zeros((SUB, LANES), f32)
            gtaps_ref[part, lags : lags + 1, tap_cols] = jnp.sum(
                grad * joined[SUB : SUB + rows, cols], axis=0, keepdims=True
            )
            for lag in range(1, lags + 1):
                tap = taps_ref[part, lags - lag : lags - lag + 1, tap_cols]
                gtaps_ref[part, lags - lag : lags - lag + 1, tap_cols] = jnp.sum(
                    grad * joined[SUB - lag : SUB - lag + rows, cols] * masks[lag],
                    axis=0,
                    keepdims=True,
                )
                moved = du_s[SUB + lag : SUB + lag + rows, :]
                dp = dp + tap * moved * mask_s[lag - 1, SUB + lag : SUB + lag + rows, :]
                halo = halo + tap * du_s[lag : lag + SUB, :] * mask_s[lag - 1, lag : lag + SUB, :]
            gp_ref[:, cols] = dp.astype(bf16)
            last_ref[:, cols] = dp[rows - 2 * SUB :, :]
            halo_ref[:, cols] = halo


def input_back_kernel(
    place, gp_ref, last_ref, next_ref, dgr_ref, gb_ref, wq_ref, wk_ref, wv_ref, wg_ref, wb_ref,
    x_ref, keep_ref, send_ref, gpf_ref, sums_ref, whole,
):
    rows, width = gp_ref.shape
    head_width = width // 3
    gpf_ref[...] = gp_ref[...]
    last = last_ref[...]
    gpf_ref[rows - 2 * SUB :, :] = jnp.concatenate(
        [last[:SUB], last[SUB:] + next_ref[...]], axis=0
    ).astype(bf16)
    total = mm(dgr_ref[...], wg_ref[...], 1, 1) + mm(gb_ref[...], wb_ref[...], 1, 1)
    for part, w_ref in enumerate((wq_ref, wk_ref, wv_ref)):
        total = total + mm(gpf_ref[:, part * head_width : (part + 1) * head_width], w_ref[...], 1, 1)
    whole[...] = total
    split_rows(place, whole, keep_ref, send_ref)
    x = x_ref[...].astype(f32)
    scale = lax.rsqrt(jnp.mean(x * x, axis=-1, keepdims=True) + 1e-06)
    sums_ref[...] = jnp.sum(total * (x * scale), axis=0, keepdims=True)


def project_grads_kernel(order, place, a_ref, gp_ref, dgr_ref, gb_ref, keep_ref, send_ref, gwb_ref, whole):
    width = gp_ref.shape[1]
    a = a_ref[...]
    whole[:, :width] = mm(a, gp_ref[...], 0, 0).astype(bf16)
    whole[:, width:] = mm(a, dgr_ref[...], 0, 0).astype(bf16)
    gwb_ref[...] = mm(gb_ref[...], a, 0, 0)[: gwb_ref.shape[0]]
    block = whole.shape[0] // (2 * len(order))
    for index, relative in enumerate(order):
        for ref, low_bit in ((keep_ref, 0), (send_ref, 1)):
            owner = lax.bitwise_xor(place[0], jnp.int32(relative | low_bit))
            ref[index * block : (index + 1) * block, :] = whole[
                pl.ds(pl.multiple_of(owner * block, block), block), :
            ]


def input_grad_kernel(place, mine_a, mine_b, theirs_a, theirs_b, x_ref, gain_ref, dh_ref, out_ref, whole):
    join_rows(
        place,
        mine_a[...].astype(f32) + mine_b[...].astype(f32),
        theirs_a[...].astype(f32) + theirs_b[...].astype(f32),
        whole,
    )
    x = x_ref[...].astype(f32)
    scale = lax.rsqrt(jnp.mean(x * x, axis=-1, keepdims=True) + 1e-06)
    hat = x * scale
    grad = whole[...] * gain_ref[...]
    inner = jnp.mean(grad * hat, axis=-1, keepdims=True)
    out_ref[...] = dh_ref[...] + scale * (grad - hat * inner)


def output_kernel(place, mine_a, mine_b, theirs_a, theirs_b, h_ref, out_ref, whole):
    join_rows(
        place,
        mine_a[...].astype(f32) + mine_b[...].astype(f32),
        theirs_a[...].astype(f32) + theirs_b[...].astype(f32),
        whole,
    )
    out_ref[...] = (h_ref[...] + whole[...]).astype(bf16)


def head_sum(keep, send):
    count = lax.axis_size("head")
    mine = keep + swap(send, "head", 1)
    bit = 2
    if bit >= count:
        zero = jnp.zeros_like(mine)
        return mine, zero, swap(mine, "head", 1), zero
    while bit * 2 < count:
        mine = mine + swap(mine, "head", bit)
        bit *= 2
    far = swap(mine, "head", bit)
    return mine, far, swap(mine, "head", 1), swap(far, "head", 1)


def gathered(value):
    count = lax.axis_size("head")
    blocks = value[None]
    bits = []
    bit = 2
    while bit < count:
        bits.append(bit)
        bit *= 2
    bits.append(1)
    for bit in bits:
        blocks = jnp.concatenate([blocks, swap(blocks, "head", bit)], axis=0)
    return blocks


def body(
    block_input, cotangent, segment_ids, norm_gain, w_query, w_key, w_value, w_gate, w_beta,
    beta_bias, conv_weight, head_gain, w_out, ffn_gain, w_ffn_gate, w_ffn_up, w_ffn_down,
):
    rows, model = block_input.shape
    heads = w_beta.shape[1]
    head_width = w_query.shape[1]
    ffn_width = w_ffn_gate.shape[1]
    taps = conv_weight.shape[1]
    seq_count = lax.axis_size("seq")
    rounds = seq_count.bit_length() - 1
    width = 3 * head_width
    chunks = rows // CHUNK

    place = jnp.stack([lax.axis_index("seq"), lax.axis_index("head")]).astype(jnp.int32)
    seg_rows = segment_ids.reshape(chunks, LANES).astype(f32)
    gain_row, fgain_row, hgain_row = norm_gain[None], ffn_gain[None], head_gain[None]
    w_beta_wide = jnp.pad(w_beta, ((0, 0), (0, LANES - heads)))
    bias_row = jnp.pad(beta_bias, (0, LANES - heads))[None]

    w_out_all = gathered(w_out)

    a, p, gate_raw, beta, seg_cols, tail = kernel_call(
        project_kernel,
        (
            shaped((rows, model), bf16),
            shaped((rows, width), bf16),
            shaped((rows, head_width), f32),
            shaped((rows, head_width), f32),
            shaped((rows, LANES), f32),
            shaped((SUB, width + LANES), f32),
        ),
        place, block_input, gain_row, w_query, w_key, w_value, w_gate, w_beta_wide, bias_row, seg_rows,
        name="project",
        flops=2 * rows * model * (4 * head_width + LANES),
    )
    halo = shift(tail, "seq", 1)
    square = (rows, head_width)
    joined = pltpu.VMEM((rows + SUB, width), f32)
    joined_ids = pltpu.VMEM((rows + SUB, LANES), f32)
    qkv, w_rows, u_rows, q_eff, p_u, inverse, scores, d_map, k_u, maps = kernel_call(
        delta_kernel,
        (shaped((rows, width), bf16),)
        + (shaped(square, bf16),) * 8
        + (shaped((2 * heads * HEAD_DIM, HEAD_DIM), bf16),),
        place, p, halo, conv_weight, seg_rows, seg_cols, beta,
        scratch=(joined, joined_ids),
        name="delta",
        flops=2 * heads * chunks * 128**3 * 30,
    )
    half_maps = heads * HEAD_DIM
    prefix = suffix = maps
    round_maps = []
    suffixes = [None]
    for bit in range(rounds - 1):
        other = swap(maps, "seq", 1 << bit)
        round_maps.append((maps, other))
        maps, prefix, suffix = kernel_call(
            functools.partial(scan_round_kernel, bit, bit == 0),
            (shaped(maps.shape, bf16), shaped(maps.shape, bf16), shaped((half_maps, HEAD_DIM), bf16)),
            place, maps, other, prefix, suffix,
            name="scan_round",
            flops=2 * heads * 128**3 * 5,
        )
        suffixes.append(suffix)
    other_a = swap(maps[half_maps:], "seq", 1 << (rounds - 1))
    y, mixed, states = kernel_call(
        functools.partial(mixer_kernel, rounds - 1),
        (shaped(square, bf16), shaped(square, f32), shaped(square, bf16)),
        place, seg_rows, seg_cols, halo, prefix, other_a, q_eff, p_u, d_map, k_u, gate_raw, hgain_row,
        scratch=(joined_ids,),
        name="mixer",
        flops=2 * heads * chunks * 128**3 * 2,
    )
    y_all = gathered(y)
    half = (rows // 2, model)
    h, b, hidden, dgate, dup, db_keep, db_send = kernel_call(
        ffn_kernel,
        (
            shaped((rows, model), f32),
            shaped((rows, model), bf16),
            shaped((rows, ffn_width), bf16),
            shaped((rows, ffn_width), bf16),
            shaped((rows, ffn_width), bf16),
            shaped(half, bf16),
            shaped(half, bf16),
        ),
        place, block_input, cotangent, fgain_row, w_ffn_gate, w_ffn_up, w_ffn_down, y_all, w_out_all,
        scratch=(pltpu.VMEM((rows, model), f32),),
        name="ffn",
        flops=2 * rows * model * (model + 5 * ffn_width),
    )
    db_parts = head_sum(db_keep, db_send)
    grad_gate, grad_up, grad_down, out_keep, out_send = kernel_call(
        ffn_grads_kernel,
        (
            shaped((model, ffn_width), bf16),
            shaped((model, ffn_width), bf16),
            shaped((model, ffn_width), bf16),
            shaped(half, bf16),
            shaped(half, bf16),
        ),
        place, b, hidden, dgate, dup, cotangent, w_ffn_down,
        scratch=(pltpu.VMEM((rows, model), f32),),
        name="ffn_grads",
        flops=2 * rows * model * 4 * ffn_width,
    )
    ffn_share = lax.psum_scatter(
        jnp.concatenate([grad_gate, grad_up], axis=1), "seq", scatter_dimension=0, tiled=True
    ).astype(f32)
    out_parts = head_sum(out_keep, out_send)
    (block_output,) = kernel_call(
        output_kernel,
        (shaped((rows, model), bf16),),
        place, *out_parts, h,
        scratch=(pltpu.VMEM((rows, model), f32),),
        name="output",
    )
    dh, gh, d_out, d_gate_raw, pull, sums_a = kernel_call(
        residual_back_kernel,
        (
            shaped((rows, model), f32),
            shaped((rows, model), bf16),
            shaped(square, bf16),
            shaped(square, bf16),
            shaped((half_maps, HEAD_DIM), bf16),
            shaped((2, model), f32),
        ),
        place, *db_parts, h, cotangent, fgain_row, w_out, y, mixed, gate_raw, hgain_row,
        seg_rows, seg_cols, halo, q_eff, d_map,
        scratch=(pltpu.VMEM((rows, model), f32), joined_ids),
        name="residual_back",
        flops=2 * rows * model * head_width,
    )
    grad_out = jnp.einsum("td,tw->dw", gh, y, preferred_element_type=f32).astype(bf16)
    down_share = lax.psum_scatter(
        jnp.concatenate([grad_down, grad_out], axis=1), "seq", scatter_dimension=0, tiled=True
    ).astype(f32)
    after = pull
    for bit in range(rounds - 1):
        other = swap(pull, "seq", 1 << bit)
        own_maps, other_maps = round_maps[bit]
        pull, after = kernel_call(
            functools.partial(back_round_kernel, bit, bit == 0),
            (shaped(pull.shape, bf16), shaped(pull.shape, bf16)),
            place, own_maps[:half_maps], other_maps[:half_maps],
            suffixes[bit] if bit else own_maps[:half_maps], pull, other, after,
            name="back_round",
            flops=2 * heads * 128**3 * 2,
        )
    other_pull = swap(pull, "seq", 1 << (rounds - 1))
    gp, gp_last, gp_halo, gb, grad_taps, grad_bias = kernel_call(
        functools.partial(delta_back_kernel, rounds - 1),
        (
            shaped((rows, width), bf16),
            shaped((2 * SUB, width), f32),
            shaped((SUB, width), f32),
            shaped((rows, LANES), bf16),
            shaped(conv_weight.shape, f32),
            shaped((1, LANES), f32),
        ),
        place, p, halo, conv_weight, seg_rows, seg_cols, beta, qkv, w_rows, u_rows, inverse, scores,
        d_map, q_eff, states, d_out, suffixes[rounds - 1], after, other_pull,
        scratch=(
            joined,
            joined_ids,
            pltpu.VMEM((rows, width), f32),
            pltpu.VMEM((rows + 2 * SUB, LANES), f32),
            pltpu.VMEM((taps - 1, rows + 2 * SUB, LANES), f32),
        ),
        name="delta_back",
        flops=2 * heads * chunks * 128**3 * 20,
    )
    from_next = shift(gp_halo, "seq", -1)
    da_keep, da_send, gp_full, sums_b = kernel_call(
        input_back_kernel,
        (
            shaped(half, bf16),
            shaped(half, bf16),
            shaped((rows, width), bf16),
            shaped((1, model), f32),
        ),
        place, gp, gp_last, from_next, d_gate_raw, gb, w_query, w_key, w_value, w_gate, w_beta_wide,
        block_input,
        scratch=(pltpu.VMEM((rows, model), f32),),
        name="input_back",
        flops=2 * rows * model * (4 * head_width + LANES),
    )
    da_parts = head_sum(da_keep, da_send)
    order = []
    for index in range(seq_count // 2):
        relative = 0
        for position in range(rounds - 1):
            if index >> (rounds - 2 - position) & 1:
                relative |= 1 << (position + 1)
        order.append(relative)
    share_rows = model // 2
    keep, send, grad_beta_rows = kernel_call(
        functools.partial(project_grads_kernel, tuple(order)),
        (
            shaped((share_rows, 4 * head_width), bf16),
            shaped((share_rows, 4 * head_width), bf16),
            shaped((heads, model), f32),
        ),
        place, a, gp_full, d_gate_raw, gb,
        scratch=(pltpu.VMEM((model, 4 * head_width), bf16),),
        name="project_grads",
        flops=2 * rows * model * (4 * head_width + LANES),
    )
    (input_grad,) = kernel_call(
        input_grad_kernel,
        (shaped((rows, model), f32),),
        place, *da_parts, block_input, gain_row, dh,
        scratch=(pltpu.VMEM((rows, model), f32),),
        name="input_grad",
    )
    both_axes = jnp.concatenate([sums_b[0], sums_a[1, :LANES]])
    seq_only = jnp.concatenate(
        [sums_a[0], grad_taps.reshape(-1), grad_beta_rows.reshape(-1), grad_bias[0]]
    )
    small = jnp.concatenate([both_axes, seq_only])
    short = both_axes.shape[0]
    size = small.shape[0]
    small = jnp.pad(small, (0, -size % 1024)).reshape(-1, LANES)
    for bit in range(rounds):
        got = swap(send, "seq", 1 << bit)
        small = small + swap(small, "seq", 1 << bit)
        if bit < rounds - 1:
            middle = keep.shape[0] // 2
            send = keep[middle:] + got[middle:]
            keep = keep[:middle] + got[:middle]
        else:
            project_share = keep.astype(f32) + got.astype(f32)
    flat = small.reshape(-1)
    both_axes = flat[:short].reshape(-1, LANES)
    bit = 1
    while bit < lax.axis_size("head"):
        both_axes = both_axes + swap(both_axes, "head", bit)
        bit *= 2
    both_axes = both_axes.reshape(-1)
    norm_total, head_gain_total = both_axes[:model], both_axes[model:]
    flat = flat[short:size]
    ffn_gain_total, flat = flat[:model], flat[model:]
    conv_total, flat = flat[: conv_weight.size].reshape(conv_weight.shape), flat[conv_weight.size :]
    beta_rows, flat = flat[: heads * model].reshape(heads, model), flat[heads * model :]
    bias_total = flat[:heads]
    block = model // seq_count
    beta_share = lax.dynamic_slice(
        beta_rows, (0, lax.axis_index("seq") * block), (heads, block)
    ).T
    return (
        block_output,
        input_grad,
        norm_total,
        project_share[:, :head_width],
        project_share[:, head_width : 2 * head_width],
        project_share[:, 2 * head_width : 3 * head_width],
        project_share[:, 3 * head_width :],
        beta_share,
        bias_total,
        conv_total,
        head_gain_total,
        down_share[:, ffn_width:].T,
        ffn_gain_total,
        ffn_share[:, :ffn_width],
        ffn_share[:, ffn_width:],
        down_share[:, :ffn_width].T,
    )


def solution(mesh):
    return jax.shard_map(
        body,
        mesh=mesh,
        in_specs=(
            P("seq", None), P("seq", None), P("seq"), P(),
            P(None, "head"), P(None, "head"), P(None, "head"), P(None, "head"), P(None, "head"),
            P("head"), P(None, None, "head"), P(), P("head", None), P(),
            P(None, "head"), P(None, "head"), P("head", None),
        ),
        out_specs=(
            P("seq", None), P("seq", None), P(),
            P("seq", "head"), P("seq", "head"), P("seq", "head"), P("seq", "head"), P("seq", "head"),
            P("head"), P(None, None, "head"), P(), P("head", "seq"), P(),
            P("seq", "head"), P("seq", "head"), P("head", "seq"),
        ),
        check_vma=False,
    )
```

```python
import functools
import math

import jax
import jax.numpy as jnp
from jax import lax
from jax.experimental import pallas as pl
from jax.experimental.pallas import tpu as pltpu
from jax.sharding import PartitionSpec as P

HEAD_DIM = 128
CHUNK = 128
LANES = 128
SUB = 8
Q_SCALE = HEAD_DIM ** (-0.5)
VMEM_SLACK = 14 * 1024 * 1024

bf16 = jnp.bfloat16
f32 = jnp.float32


def mm(left, right, left_dim=1, right_dim=0):
    return lax.dot_general(
        left.astype(bf16),
        right.astype(bf16),
        (((left_dim,), (right_dim,)), ((), ())),
        preferred_element_type=f32,
    )


def sigmoid(value):
    return 1.0 / (1.0 + jnp.exp(-value))


class Free:
    def __init__(self, value):
        self.value = value


class Held(Free):
    pass


class Far(Free):
    pass


class Place:
    def __getitem__(self, which):
        return lax.axis_index(("seq", "head")[which])


class Direct:
    def __init__(self, shape, dtype):
        self.shape, self.dtype = tuple(shape), dtype


def kernel_call(body, out_shapes, place, *args, scratch=(), name, flops=0, deps=()):
    vmem = pl.BlockSpec(memory_space=pltpu.VMEM)
    smem = pl.BlockSpec(memory_space=pltpu.SMEM)
    anywhere = pl.BlockSpec(memory_space=pl.ANY)
    size_of = lambda a: math.prod(a.shape) * jnp.dtype(a.dtype).itemsize
    held = sum(size_of(s) for s in scratch if hasattr(s, "dtype") and not is_semaphore(s))
    operands, specs, moved = [], [], 0
    here = Place()
    for arg in args:
        if isinstance(arg, Free):
            value = arg.value
            if not type(arg) is Free:
                value = pltpu.with_memory_space_constraint(value, pltpu.HBM)
            operands.append(value)
            specs.append(anywhere if isinstance(arg, Far) else vmem)
            if not isinstance(arg, Far):
                held += size_of(value)
        elif arg.ndim == 1:
            operands.append(arg)
            specs.append(smem)
        else:
            operands.append(pltpu.with_memory_space_constraint(arg, pltpu.VMEM))
            specs.append(vmem)
        moved += size_of(operands[-1])
    count = len(args)
    run = lambda *refs: body(here, *refs[:count], *refs[count + len(deps) :])
    operands += [
        pltpu.with_memory_space_constraint(dep.value, pltpu.HBM)
        if isinstance(dep, Free)
        else pltpu.with_memory_space_constraint(dep, pltpu.VMEM)
        for dep in deps
    ]
    specs += [anywhere] * len(deps)
    results, result_specs = [], []
    for out in out_shapes:
        moved += size_of(out)
        if isinstance(out, Direct):
            results.append(pltpu.HBM(out.shape, out.dtype))
            result_specs.append(anywhere)
        else:
            results.append(out)
            result_specs.append(vmem)
            if isinstance(out, jax.ShapeDtypeStruct) or out.memory_space == pltpu.HBM:
                held += size_of(out)
    return pl.pallas_call(
        run,
        out_shape=tuple(results),
        in_specs=specs,
        out_specs=tuple(result_specs),
        scratch_shapes=list(scratch),
        compiler_params=pltpu.CompilerParams(vmem_limit_bytes=int(held) + VMEM_SLACK),
        cost_estimate=pl.CostEstimate(flops=0, bytes_accessed=0, transcendentals=0),
        name=name,
    )(*operands)


def stored(shape, dtype):
    return pltpu.HBM(tuple(shape), dtype)


def send_out(source, target, sems, index):
    copy = pltpu.make_async_copy(source, target, sems.at[index])
    copy.start()
    return copy


def is_semaphore(scratch):
    return not (
        jnp.issubdtype(scratch.dtype, jnp.floating) or jnp.issubdtype(scratch.dtype, jnp.integer)
    )


def final(shape, dtype):
    return jax.ShapeDtypeStruct(tuple(shape), dtype)


def shaped(shape, dtype):
    return pltpu.VMEM(tuple(shape), dtype)


def swap(value, axis, bit):
    count = lax.axis_size(axis)
    return lax.ppermute(value, axis, [(s, s ^ bit) for s in range(count)])


def shift(value, axis, step):
    count = lax.axis_size(axis)
    return lax.ppermute(
        value, axis, [(s, s + step) for s in range(count) if 0 <= s + step < count]
    )


def bit_of(place_ref, which, bit):
    return lax.rem(lax.shift_right_logical(place_ref[which], bit), 2)


def chosen(flag, when_one, when_zero):
    return jnp.where(flag == 1, when_one, when_zero)


def tri_masks():
    rows = lax.broadcasted_iota(jnp.int32, (CHUNK, CHUNK), 0)
    cols = lax.broadcasted_iota(jnp.int32, (CHUNK, CHUNK), 1)
    return rows, cols


def unit_inverses(lowers):
    rows, cols = tri_masks()
    eye = jnp.where(rows == cols, 1.0, 0.0).astype(f32)
    width = 1
    inverses = None
    while width < CHUNK:
        shift_bits = width.bit_length() - 1
        row_block = lax.shift_right_logical(rows, shift_bits)
        col_block = lax.shift_right_logical(cols, shift_bits)
        within = (
            lax.shift_right_logical(row_block, 1) == lax.shift_right_logical(col_block, 1)
        ) & (row_block != col_block)
        couplings = [jnp.where(within, low, 0.0) for low in lowers]
        if inverses is None:
            inverses = [eye - coupling for coupling in couplings]
        else:
            halves = [mm(inv, coupling) for inv, coupling in zip(inverses, couplings)]
            inverses = [inv - mm(half, inv) for inv, half in zip(inverses, halves)]
        width *= 2
    return inverses


def project_kernel(
    place, x_hbm, wq_hbm, wk_hbm, wv_hbm, wg_hbm, gain_hbm, wb_hbm, bias_hbm, seg_hbm, wo_hbm,
    p_ref, beta_ref, segc_ref, tail_ref, a_hbm, gate_hbm, wb8_hbm, wo_out,
    x_s, weights, gain_s, wb_s, bias_s, seg_s, a_s, gate_s, wb8_s, wo_s, arrived, left,
):
    rows = x_s.shape[0]
    head_width = wq_hbm.shape[1]
    heads = head_width // LANES
    pairs = ((x_hbm, x_s), (gain_hbm, gain_s), (seg_hbm, seg_s), (wb_hbm, wb_s), (bias_hbm, bias_s))
    pairs += ((wo_hbm, wo_s),)
    pairs += tuple(
        (source, weights.at[index]) for index, source in enumerate((wg_hbm, wq_hbm, wk_hbm, wv_hbm))
    )
    copies = [send_out(source, target, arrived, index) for index, (source, target) in enumerate(pairs)]
    for copy in copies[:5]:
        copy.wait()
    wo_copy, *copies = copies[5:]
    segr = seg_s[...].astype(f32)
    wb8_s[...] = jnp.zeros(wb8_s.shape, f32)
    wb8_s[0:heads, :] = wb_s[...].astype(f32)
    leaving = [send_out(wb8_s, wb8_hbm, left, 2)]
    x = x_s[...].astype(f32)
    scale = lax.rsqrt(jnp.mean(x * x, axis=-1, keepdims=True) + 1e-06)
    a = (x * scale * gain_s[...]).astype(bf16)
    a_s[...] = a
    tail_ref[:, 3 * head_width + LANES :] = a.astype(f32)[rows - SUB :, :]
    leaving.append(send_out(a_s, a_hbm, left, 0))
    logits = mm(a, wb8_s[...], 1, 1)
    for head in range(heads):
        column = logits[:, head : head + 1] + bias_s[:, head : head + 1]
        beta_ref[:, head * LANES : (head + 1) * LANES] = sigmoid(
            jnp.broadcast_to(column, (rows, LANES))
        )
    for chunk in range(rows // CHUNK):
        ids = jnp.broadcast_to(segr[chunk : chunk + 1, :], (CHUNK, LANES))
        turned = ids.T
        segc_ref[chunk * CHUNK : (chunk + 1) * CHUNK, :] = turned
        if chunk == rows // CHUNK - 1:
            tail_ref[:, 3 * head_width : 3 * head_width + LANES] = turned[CHUNK - SUB :, :]
    wo_copy.wait()
    leaving.append(send_out(wo_s, wo_out, left, 3))
    copies[0].wait()
    gate_s[...] = mm(a, weights[0])
    leaving.append(send_out(gate_s, gate_hbm, left, 1))
    for part in range(3):
        copies[part + 1].wait()
        value = mm(a, weights[part + 1])
        cols = slice(part * head_width, (part + 1) * head_width)
        low = value.astype(bf16)
        p_ref[:, cols] = low
        tail_ref[:, cols] = low.astype(f32)[rows - SUB :, :]
    for copy in leaving:
        copy.wait()


def lag_masks(joined_ids, lags):
    rows = joined_ids.shape[0] - SUB
    ids = joined_ids[SUB : SUB + rows, :]
    return [None] + [
        jnp.where(joined_ids[SUB - lag : SUB - lag + rows, :] == ids, 1.0, 0.0)
        for lag in range(1, lags + 1)
    ]


def conv_sum(joined, taps_ref, masks, part, head, head_width, rows):
    lags = taps_ref.shape[1] - 1
    col = part * head_width + head * LANES
    tap_cols = slice(head * LANES, (head + 1) * LANES)
    total = taps_ref[part, lags : lags + 1, tap_cols] * joined[SUB : SUB + rows, col : col + LANES]
    for lag in range(1, lags + 1):
        tap = taps_ref[part, lags - lag : lags - lag + 1, tap_cols]
        total = total + tap * joined[SUB - lag : SUB - lag + rows, col : col + LANES] * masks[lag]
    return total


def chunk_flags(joined_ids, chunk):
    start = chunk * CHUNK
    ids = joined_ids[SUB + start : SUB + start + CHUNK, :]
    same = jnp.where(ids == ids.T, 1.0, 0.0)
    before = joined_ids[SUB + start - 1 : SUB + start, :]
    final_id = joined_ids[SUB + start + CHUNK - 1 : SUB + start + CHUNK, :]
    opened = jnp.where(ids == before, 1.0, 0.0)
    closing = jnp.where(ids == final_id, 1.0, 0.0)
    kept = jnp.where(final_id == before, 1.0, 0.0)
    return same, opened, closing, kept


def delta_kernel(
    place, p_ref, tail_ref, taps_ref, segc_ref, beta_ref,
    maps_ref, mix_ref, back_ref, facts_ref, before_ref,
    joined, joined_ids,
):
    rows, width = p_ref.shape
    head_width = width // 3
    heads = head_width // LANES
    chunks = rows // CHUNK
    first = 2 * SUB
    joined[0:SUB, :] = tail_ref[:, :width]
    joined[SUB : SUB + rows, :] = p_ref[...].astype(f32)
    joined_ids[0:SUB, :] = tail_ref[:, width : width + LANES]
    joined_ids[SUB : SUB + rows, :] = segc_ref[...]
    facts_ref[SUB:, 0:head_width] = beta_ref[...]
    facts_ref[0:SUB, 0:head_width] = jnp.zeros((SUB, head_width), f32)
    facts_ref[:, head_width:] = joined_ids[...]
    before_ref[...] = jnp.concatenate(
        [jnp.zeros((SUB, before_ref.shape[1]), f32), tail_ref[:, width + LANES :]], axis=0
    ).astype(bf16)
    back_ref[first:, 0:width] = p_ref[...]
    back_ref[0:first, 0:width] = jnp.concatenate(
        [jnp.zeros((SUB, width), f32), tail_ref[:, :width]], axis=0
    ).astype(bf16)
    back_ref[0:first, width:] = jnp.zeros((first, back_ref.shape[1] - width), bf16)
    masks = lag_masks(joined_ids, taps_ref.shape[1] - 1)
    for part in range(3):
        for head in range(heads):
            total = conv_sum(joined, taps_ref, masks, part, head, head_width, rows)
            z = total * sigmoid(total)
            if part < 2:
                z = z * lax.rsqrt(jnp.sum(z * z, axis=-1, keepdims=True) + 1e-06)
                if part == 0:
                    z = z * Q_SCALE
            col = width + part * head_width + head * LANES
            back_ref[first:, col : col + LANES] = z.astype(bf16)
    row_ids, col_ids = tri_masks()
    flags = [chunk_flags(joined_ids, chunk) for chunk in range(chunks)]
    mix_ref[rows:, :] = jnp.concatenate(
        [jnp.concatenate([flags[min(row, chunks - 1)][3]] * (4 * heads), axis=1) for row in range(2 * SUB)],
        axis=0,
    ).astype(bf16)
    sets = [(head, chunk) for head in range(heads) for chunk in range(chunks)]

    def at_of(head, chunk, part=0):
        col = part * head_width + head * LANES
        return (slice(chunk * CHUNK, (chunk + 1) * CHUNK), slice(col, col + LANES))

    def kept_at(head, chunk, part):
        col = (3 + part) * head_width + head * LANES
        return (slice(first + chunk * CHUNK, first + (chunk + 1) * CHUNK), slice(col, col + LANES))

    lowers = []
    for head, chunk in sets:
        same = flags[chunk][0]
        q, k = back_ref[kept_at(head, chunk, 0)], back_ref[kept_at(head, chunk, 1)]
        inner = mm(jnp.concatenate([q, k], axis=0), k, 1, 1)
        scores = jnp.where(row_ids >= col_ids, inner[:CHUNK] * same, 0.0)
        back_ref[kept_at(head, chunk, 6)] = scores.astype(bf16)
        lowers.append(
            jnp.where(row_ids > col_ids, inner[CHUNK:] * same * beta_ref[at_of(head, chunk)], 0.0)
        )
    inverses = unit_inverses(lowers)
    eye = jnp.where(row_ids == col_ids, 1.0, 0.0).astype(f32)
    maps = [
        jnp.concatenate([eye, jnp.zeros((HEAD_DIM, HEAD_DIM), f32)], axis=1) for _ in range(heads)
    ]
    products = []
    for (head, chunk), inverse in zip(sets, inverses):
        beta = beta_ref[at_of(head, chunk)]
        k = back_ref[kept_at(head, chunk, 1)].astype(f32)
        v = back_ref[kept_at(head, chunk, 2)].astype(f32)
        both = jnp.concatenate([beta * k, beta * v], axis=1)
        products.append(mm(inverse, both))
    steps = {}
    for (head, chunk), inverse, product in zip(sets, inverses, products):
        same, opened, closing, kept = flags[chunk]
        w_rows, u_rows = product[:, :HEAD_DIM], product[:, HEAD_DIM:]
        back_ref[kept_at(head, chunk, 3)] = w_rows.astype(bf16)
        back_ref[kept_at(head, chunk, 4)] = u_rows.astype(bf16)
        back_ref[kept_at(head, chunk, 5)] = inverse.astype(bf16)
        both = jnp.concatenate([opened * w_rows, u_rows], axis=1)
        k = back_ref[kept_at(head, chunk, 1)].astype(f32)
        q = back_ref[kept_at(head, chunk, 0)].astype(f32)
        step = mm(closing * k, both, 0, 0)
        through = mm(back_ref[kept_at(head, chunk, 6)], both)
        mix_ref[at_of(head, chunk, 0)] = (opened * q - through[:, :HEAD_DIM]).astype(bf16)
        mix_ref[at_of(head, chunk, 1)] = step[:, :HEAD_DIM].astype(bf16)
        mix_ref[at_of(head, chunk, 2)] = through[:, HEAD_DIM:].astype(bf16)
        mix_ref[at_of(head, chunk, 3)] = step[:, HEAD_DIM:].astype(bf16)
        steps[head, chunk] = step
    for chunk in range(chunks):
        kept = flags[chunk][3]
        kept_wide = jnp.concatenate([kept, kept], axis=1)
        for head in range(heads):
            step = steps[head, chunk]
            pushed = kept_wide * maps[head] - mm(step[:, :HEAD_DIM], maps[head])
            maps[head] = jnp.concatenate(
                [pushed[:, :HEAD_DIM], pushed[:, HEAD_DIM:] + step[:, HEAD_DIM:]], axis=1
            )
    for head in range(heads):
        maps_ref[head * HEAD_DIM : (head + 1) * HEAD_DIM, :] = maps[head][:, :HEAD_DIM].astype(bf16)
        base = (heads + head) * HEAD_DIM
        maps_ref[base : base + HEAD_DIM, :] = maps[head][:, HEAD_DIM:].astype(bf16)


def park_kernel(count, place, *refs):
    sources, targets, left = refs[:count], refs[count : 2 * count], refs[-1]
    copies = []
    for index, (source, target) in enumerate(zip(sources, targets)):
        if source.shape != target.shape:
            source = source.at[:, 0 : target.shape[1]]
        copies.append(send_out(source, target, left, index))
    for copy in copies:
        copy.wait()


def park(place, *pairs, name, deps=()):
    arrays = [value.value if isinstance(value, Free) else value for value, _ in pairs]
    return kernel_call(
        functools.partial(park_kernel, len(pairs)),
        [
            Direct((array.shape[0], array.shape[1] if cols is None else cols), array.dtype)
            for array, (_, cols) in zip(arrays, pairs)
        ],
        place,
        *[value for value, _ in pairs],
        scratch=(pltpu.SemaphoreType.DMA((len(pairs),)),),
        name=name,
        deps=deps,
    )


def scan_round_kernel(bit, place, own_ref, other_ref, prefix_ref, pack_ref, total_ref, prefix_out, pack_out):
    upper = bit_of(place, 0, bit)
    half = own_ref.shape[0] // 2
    heads = half // HEAD_DIM
    base = 2 * half * bit
    if bit:
        pack_out[0:base, :] = pack_ref[...]
    for head in range(heads):
        m_at = slice(head * HEAD_DIM, (head + 1) * HEAD_DIM)
        a_at = slice((heads + head) * HEAD_DIM, (heads + head + 1) * HEAD_DIM)
        low_at = slice(base + head * HEAD_DIM, base + (head + 1) * HEAD_DIM)
        suffix_at = slice(base + half + head * HEAD_DIM, base + half + (head + 1) * HEAD_DIM)
        own_m, own_a = own_ref[m_at, :].astype(f32), own_ref[a_at, :].astype(f32)
        other_m, other_a = other_ref[m_at, :].astype(f32), other_ref[a_at, :].astype(f32)
        high_m, high_a = chosen(upper, own_m, other_m), chosen(upper, own_a, other_a)
        low_m, low_a = chosen(upper, other_m, own_m), chosen(upper, other_a, own_a)
        pack_out[low_at, :] = low_m.astype(bf16)
        total = mm(high_m, jnp.concatenate([low_m, low_a], axis=1))
        added_part = (total[:, HEAD_DIM:] + high_a).astype(bf16)
        if total_ref.shape[0] == own_ref.shape[0]:
            total_ref[m_at, :] = total[:, :HEAD_DIM].astype(bf16)
            total_ref[a_at, :] = added_part
        else:
            total_ref[m_at, :] = added_part
        if bit == 0:
            rows, cols = tri_masks()
            eye = jnp.where(rows == cols, 1.0, 0.0).astype(f32)
            prefix_out[m_at, :] = chosen(upper, other_m, eye).astype(bf16)
            prefix_out[a_at, :] = chosen(upper, other_a, jnp.zeros_like(other_a)).astype(bf16)
            pack_out[suffix_at, :] = chosen(upper, eye, other_m.T).astype(bf16)
        else:
            before_m, before_a = prefix_ref[m_at, :].astype(f32), prefix_ref[a_at, :].astype(f32)
            at = base - half + head * HEAD_DIM
            after_m = pack_ref[at : at + HEAD_DIM, :].astype(f32)
            joint = mm(before_m, jnp.concatenate([other_m, other_a], axis=1))
            prefix_out[m_at, :] = chosen(upper, joint[:, :HEAD_DIM], before_m).astype(bf16)
            prefix_out[a_at, :] = chosen(
                upper, joint[:, HEAD_DIM:] + before_a, before_a
            ).astype(bf16)
            pack_out[suffix_at, :] = chosen(upper, after_m, mm(after_m, other_m, 1, 1)).astype(bf16)


def back_round_kernel(bit, place, pack_ref, own_ref, other_ref, after_ref, total_ref, after_out):
    upper = bit_of(place, 0, bit)
    half = own_ref.shape[0]
    base = 2 * half * bit
    for head in range(half // HEAD_DIM):
        at = slice(head * HEAD_DIM, (head + 1) * HEAD_DIM)
        own, other = own_ref[at, :].astype(f32), other_ref[at, :].astype(f32)
        high, low = chosen(upper, own, other), chosen(upper, other, own)
        low_m = pack_ref[base + head * HEAD_DIM : base + (head + 1) * HEAD_DIM, :]
        total_ref[at, :] = (mm(low_m, high, 0, 0) + low).astype(bf16)
        if bit == 0:
            after_out[at, :] = chosen(upper, jnp.zeros_like(other), other).astype(bf16)
        else:
            start = base - half + head * HEAD_DIM
            suffix_m = pack_ref[start : start + HEAD_DIM, :]
            after = after_ref[at, :].astype(f32)
            after_out[at, :] = chosen(upper, after, mm(suffix_m, other) + after).astype(bf16)


def mixer_kernel(
    last_bit, place, prefix_ref, other_a_ref, mix_ref, gate_ref, hgain_ref,
    y_ref, o_ref, keep_ref,
):
    rows, head_width = gate_ref.shape
    heads = head_width // LANES
    upper = bit_of(place, 0, last_bit)
    kept_rows = mix_ref[rows:, 0:LANES].astype(f32)
    for head in range(heads):
        m_at = slice(head * HEAD_DIM, (head + 1) * HEAD_DIM)
        a_at = slice((heads + head) * HEAD_DIM, (heads + head + 1) * HEAD_DIM)
        before_m, before_a = prefix_ref[m_at, :], prefix_ref[a_at, :].astype(f32)
        state = chosen(upper, mm(before_m, other_a_ref[m_at, :]) + before_a, before_a)
        for chunk in range(rows // CHUNK):
            chunk_rows = slice(chunk * CHUNK, (chunk + 1) * CHUNK)
            cols = [
                slice(part * head_width + head * LANES, part * head_width + (head + 1) * LANES)
                for part in range(4)
            ]
            at = (chunk_rows, cols[0])
            low = state.astype(bf16)
            keep_ref[at] = low
            out = mm(mix_ref[at], low) + mix_ref[chunk_rows, cols[2]].astype(f32)
            o_ref[at] = out
            state = (
                kept_rows[chunk : chunk + 1, :] * state
                - mm(mix_ref[chunk_rows, cols[1]], low)
                + mix_ref[chunk_rows, cols[3]].astype(f32)
            )
            gate = gate_ref[at]
            scale = lax.rsqrt(jnp.mean(out * out, axis=-1, keepdims=True) + 1e-05)
            y = (out * scale * hgain_ref[...] * (gate * sigmoid(gate))).astype(bf16)
            y_ref[at] = y
            keep_ref[chunk_rows, cols[1]] = y


def ffn_kernel(
    share, place, x_ref, g_ref, fgain_ref, wg_ref, wu_ref, wd_ref, *rest,
):
    *parts, send_ref, h_hbm, grads_hbm, hid_hbm, keep_hbm, h_s, grads_s, hid_s, keep_s, whole, left = rest
    y_refs, wo_refs = parts[: len(parts) // 2], parts[len(parts) // 2 :]
    att = None
    for y_ref, wo_ref in zip(y_refs, wo_refs):
        part = mm(y_ref[...], wo_ref[...])
        att = part if att is None else att + part
    h = x_ref[...].astype(f32) + att
    h_s[...] = h
    leaving = [send_out(h_s, h_hbm, left, 0)]
    scale = lax.rsqrt(jnp.mean(h * h, axis=-1, keepdims=True) + 1e-06)
    b = (h * scale * fgain_ref[...]).astype(bf16)
    gate = mm(b, wg_ref[...], 1, 1)
    up = mm(b, wu_ref[...], 1, 1)
    sg = sigmoid(gate)
    act = gate * sg
    hid = (act * up).astype(bf16)
    hid_s[...] = hid
    leaving.append(send_out(hid_s, hid_hbm, left, 2))
    dhid = mm(g_ref[...], wd_ref[...], 1, 1)
    dgate = (dhid * up * (sg * (1.0 + gate * (1.0 - sg)))).astype(bf16)
    dup = (dhid * act).astype(bf16)
    owners = grads_s.shape[0] // (3 * share)
    for index, (left_side, right_side) in enumerate(((g_ref[...], hid), (b, dgate), (b, dup))):
        grad = mm(left_side, right_side, 0, 0).astype(bf16)
        for owner in range(owners):
            at = (3 * owner + index) * share
            grads_s[at : at + share, :] = grad[owner * share : (owner + 1) * share]
    leaving.append(send_out(grads_s, grads_hbm, left, 1))
    whole[...] = mm(dgate, wg_ref[...]) + mm(dup, wu_ref[...])
    split_rows(place, whole, keep_s, send_ref)
    leaving.append(send_out(keep_s, keep_hbm, left, 3))
    for copy in leaving:
        copy.wait()


def split_rows(place, whole, keep_ref, send_ref):
    half = whole.shape[0] // 2
    core = bit_of(place, 1, 0)
    keep_ref[0:half, :] = whole[pl.ds(pl.multiple_of(core * half, half), half), :].astype(bf16)
    send_ref[0:half, :] = whole[pl.ds(pl.multiple_of((1 - core) * half, half), half), :].astype(bf16)


def join_rows(place, mine, theirs, whole):
    half = whole.shape[0] // 2
    core = bit_of(place, 1, 0)
    mine, theirs = mine[:half], theirs[:half]
    whole[pl.ds(pl.multiple_of(core * half, half), half), :] = mine
    whole[pl.ds(pl.multiple_of((1 - core) * half, half), half), :] = theirs


def emit_shares(place, bits, whole, keep_ref, send_ref):
    order = [0]
    for bit in reversed(bits[1:]):
        order = order + [relative | (1 << bit) for relative in order]
    block = whole.shape[0] // (2 * len(order))
    for index, relative in enumerate(order):
        for ref, first in ((keep_ref, 0), (send_ref, 1 << bits[0])):
            owner = lax.bitwise_xor(place[0], jnp.int32(relative | first))
            ref[index * block : (index + 1) * block, :] = whole[
                pl.ds(pl.multiple_of(owner * block, block), block), :
            ]


def share_round_kernel(place, keep_ref, got_ref, *rest):
    keep_out, send_out = rest[-2:]
    half = keep_out.shape[0]
    keep_out[...] = keep_ref[:half] + got_ref[:half]
    send_out[...] = keep_ref[half:] + got_ref[half:]


def out_part_kernel(place, hid_ref, wd_ref, keep_ref, send_ref, whole):
    whole[...] = mm(hid_ref[...], wd_ref[...])
    split_rows(place, whole, keep_ref, send_ref)


def early_grads_kernel(bits, place, gh_ref, y_ref, a_ref, dgr_ref, keep_ref, send_ref, whole):
    width = dgr_ref.shape[1]
    whole[:, :width] = mm(gh_ref[...], y_ref[:, width:], 0, 0).astype(bf16)
    whole[:, width:] = mm(a_ref[...], dgr_ref[...], 0, 0).astype(bf16)
    emit_shares(place, bits, whole, keep_ref, send_ref)


def early_sum_kernel(place, keep_ref, got_ref, turned_ref, plain_ref):
    total = keep_ref[...].astype(f32) + got_ref[...].astype(f32)
    width = plain_ref.shape[1]
    turned_ref[...] = total[:, :width].T
    plain_ref[...] = total[:, width:]


def project_sum_kernel(place, keep_ref, got_ref, *out_refs):
    total = keep_ref[...].astype(f32) + got_ref[...].astype(f32)
    width = out_refs[0].shape[1]
    for index, out_ref in enumerate(out_refs):
        out_ref[...] = total[:, index * width : (index + 1) * width]


def ffn_shares_kernel(place, shares_ref, down_ref, gate_ref, up_ref):
    share = shares_ref.shape[0] // 3
    for index, ref in enumerate((down_ref, gate_ref, up_ref)):
        ref[...] = shares_ref[index * share : (index + 1) * share].astype(f32).T


def residual_back_kernel(
    place, mine, theirs, h_ref, g_ref, fgain_ref, wo_ref, o_ref,
    gate_ref, hgain_ref, steps_ref,
    gh_ref, pull_ref, dh_ref, do_ref, dgr_ref, sums_ref, whole,
):
    rows, head_width = o_ref.shape
    heads = head_width // LANES
    join_rows(place, mine[...].astype(f32), theirs[...].astype(f32), whole)
    h = h_ref[...]
    db = whole[...]
    scale = lax.rsqrt(jnp.mean(h * h, axis=-1, keepdims=True) + 1e-06)
    hat = h * scale
    prod = db * hat
    sums_ref[...] = jnp.zeros(sums_ref.shape, f32)
    sums_ref[0:1, :] = jnp.sum(prod, axis=0, keepdims=True)
    inner = jnp.mean(prod * fgain_ref[...], axis=-1, keepdims=True)
    dh = g_ref[...].astype(f32) + scale * (db * fgain_ref[...] - hat * inner)
    dh_ref[...] = dh
    gh = dh.astype(bf16)
    gh_ref[...] = gh
    dy_all = mm(gh, wo_ref[...], 1, 1)
    hg_sum = jnp.zeros((1, LANES), f32)
    for head in range(heads):
        cols = slice(head * LANES, (head + 1) * LANES)
        out, gate, dy = o_ref[:, cols], gate_ref[:, cols], dy_all[:, cols]
        norm = lax.rsqrt(jnp.mean(out * out, axis=-1, keepdims=True) + 1e-05)
        hat_o = out * norm
        sg = sigmoid(gate)
        act = gate * sg
        hg_sum = hg_sum + jnp.sum(dy * hat_o * act, axis=0, keepdims=True)
        dgain = dy * hgain_ref[...]
        dgr_ref[:, cols] = (dgain * hat_o * (sg * (1.0 + gate * (1.0 - sg)))).astype(bf16)
        e = dgain * act
        do_ref[:, cols] = (norm * (e - hat_o * jnp.mean(e * hat_o, axis=-1, keepdims=True))).astype(bf16)
    sums_ref[1:2, 0:LANES] = hg_sum
    chunks = rows // CHUNK
    kept_rows = steps_ref[rows:, 0:LANES].astype(f32)
    pulls = [None] * heads
    for chunk in range(chunks - 1, -1, -1):
        chunk_rows = slice(chunk * CHUNK, (chunk + 1) * CHUNK)
        for head in range(heads):
            cols = slice(head * LANES, (head + 1) * LANES)
            map_cols = slice(head_width + head * LANES, head_width + (head + 1) * LANES)
            local = mm(steps_ref[chunk_rows, cols], do_ref[chunk_rows, cols], 0, 0)
            if pulls[head] is not None:
                local = (
                    local
                    + kept_rows[chunk : chunk + 1, :] * pulls[head]
                    - mm(steps_ref[chunk_rows, map_cols], pulls[head], 0, 0)
                )
            pulls[head] = local
    for head in range(heads):
        pull_ref[head * HEAD_DIM : (head + 1) * HEAD_DIM, :] = pulls[head].astype(bf16)


def delta_back_kernel(
    last_bit, place, taps_ref, back_ref, facts_ref, steps_ref, keep_ref, do_ref,
    pack_ref, after_ref, other_ref,
    gp_ref, halo_ref, small_ref,
    joined, joined_ids, dq_s, du_s, mask_s,
):
    rows, head_width = do_ref.shape
    width = 3 * head_width
    heads = head_width // LANES
    chunks = rows // CHUNK
    lags = taps_ref.shape[1] - 1
    joined[0:SUB, :] = back_ref[0 : 2 * SUB, :width].astype(f32)[SUB:, :]
    joined[SUB : SUB + rows, :] = back_ref[2 * SUB :, :width].astype(f32)
    joined_ids[...] = facts_ref[:, head_width : head_width + LANES]
    masks = lag_masks(joined_ids, lags)
    row_ids, col_ids = tri_masks()
    flags = [chunk_flags(joined_ids, chunk) for chunk in range(chunks)]
    upper = bit_of(place, 0, last_bit)
    sets = [(head, chunk) for head in range(heads) for chunk in range(chunks)]

    def at_of(head, chunk, part=0):
        col = part * head_width + head * LANES
        return (slice(chunk * CHUNK, (chunk + 1) * CHUNK), slice(col, col + LANES))

    def saved(head, chunk, part):
        col = (3 + part) * head_width + head * LANES
        return back_ref[2 * SUB + chunk * CHUNK : 2 * SUB + (chunk + 1) * CHUNK, col : col + LANES]

    state_grads = {}
    for head in range(heads):
        at = slice(head * HEAD_DIM, (head + 1) * HEAD_DIM)
        after = after_ref[at, :].astype(f32)
        start = pack_ref.shape[0] - after_ref.shape[0] + head * HEAD_DIM
        suffix_m = pack_ref[start : start + HEAD_DIM, :]
        grad = chosen(upper, after, mm(suffix_m, other_ref[at, :]) + after)
        for chunk in range(chunks - 1, -1, -1):
            state_grads[head, chunk] = grad
            if chunk:
                low = grad.astype(bf16)
                grad = (
                    flags[chunk][3] * grad
                    - mm(steps_ref[at_of(head, chunk, 1)], low, 0, 0)
                    + mm(steps_ref[at_of(head, chunk)], do_ref[at_of(head, chunk)], 0, 0)
                )
    lane_ids = lax.broadcasted_iota(jnp.int32, (CHUNK, LANES), 1)
    gb_cols = [jnp.zeros((CHUNK, LANES), f32) for _ in range(chunks)]
    for head, chunk in sets:
        same, opened, closing, kept = flags[chunk]
        at = at_of(head, chunk)
        q, k, v, w_rows, u_rows, inverse, scores = (saved(head, chunk, part) for part in range(7))
        kf, vf = k.astype(f32), v.astype(f32)
        beta = facts_ref[
            SUB + chunk * CHUNK : SUB + (chunk + 1) * CHUNK, head * LANES : (head + 1) * LANES
        ]
        state, do = keep_ref[at], do_ref[at]
        sgrad = state_grads[head, chunk].astype(bf16)
        fresh = (u_rows.astype(f32) - opened * mm(w_rows, state)).astype(bf16)
        dfresh = mm(scores, do, 0, 0) + mm(closing * kf, sgrad)
        dscore = jnp.where(row_ids >= col_ids, mm(do, fresh, 1, 1) * same, 0.0).astype(bf16)
        dw = -(opened * mm(dfresh, state, 1, 1))
        dx = mm(inverse, jnp.concatenate([dfresh, dw], axis=1), 0, 0)
        dxv, dxk = dx[:, :HEAD_DIM], dx[:, HEAD_DIM:]
        dlow = mm(dx, jnp.concatenate([u_rows, w_rows], axis=1), 1, 1)
        dlow = jnp.where(row_ids > col_ids, -dlow * same, 0.0)
        inner = mm(k, k, 1, 1)
        dbeta = jnp.sum(dxv * vf + dxk * kf + dlow * inner, axis=-1, keepdims=True)
        glow = (dlow * beta).astype(bf16)
        dq_s[at_of(head, chunk, 0)] = opened * mm(do, state, 1, 1) + mm(dscore, k)
        dq_s[at_of(head, chunk, 1)] = (
            beta * dxk
            + mm(dscore, q, 0, 0)
            + closing * mm(fresh, sgrad, 1, 1)
            + mm(glow, k)
            + mm(glow, k, 0, 0)
        )
        dq_s[at_of(head, chunk, 2)] = beta * dxv
        raw = jnp.broadcast_to(dbeta, (CHUNK, LANES)) * beta * (1.0 - beta)
        gb_cols[chunk] = jnp.where(lane_ids == head, raw, gb_cols[chunk])
    bias_sum = jnp.zeros((1, LANES), f32)
    for chunk in range(chunks):
        gp_ref[chunk * CHUNK : (chunk + 1) * CHUNK, width:] = gb_cols[chunk]
        bias_sum = bias_sum + jnp.sum(gb_cols[chunk], axis=0, keepdims=True)
    small_ref[...] = jnp.zeros(small_ref.shape, f32)
    tap_count = lags + 1
    small_ref[3 * tap_count : 3 * tap_count + 1, 0:LANES] = bias_sum
    du_s[0:SUB, :] = jnp.zeros((SUB, LANES), f32)
    du_s[SUB + rows :, :] = jnp.zeros((SUB, LANES), f32)
    for lag in range(1, lags + 1):
        mask_s[lag - 1, 0:SUB, :] = jnp.zeros((SUB, LANES), f32)
        mask_s[lag - 1, SUB : SUB + rows, :] = masks[lag]
        mask_s[lag - 1, SUB + rows :, :] = jnp.zeros((SUB, LANES), f32)
    for part in range(3):
        for head in range(heads):
            col = part * head_width + head * LANES
            cols = slice(col, col + LANES)
            tap_cols = slice(head * LANES, (head + 1) * LANES)
            total = conv_sum(joined, taps_ref, masks, part, head, head_width, rows)
            sg = sigmoid(total)
            grad = dq_s[:, cols]
            if part < 2:
                z = total * sg
                norm = lax.rsqrt(jnp.sum(z * z, axis=-1, keepdims=True) + 1e-06)
                hat = z * norm
                grad = norm * (grad - hat * jnp.sum(grad * hat, axis=-1, keepdims=True))
                if part == 0:
                    grad = grad * Q_SCALE
            grad = grad * (sg * (1.0 + total * (1.0 - sg)))
            du_s[SUB : SUB + rows, :] = grad
            dp = taps_ref[part, lags : lags + 1, tap_cols] * grad
            halo = jnp.zeros((SUB, LANES), f32)
            row = part * tap_count + lags
            small_ref[row : row + 1, tap_cols] = jnp.sum(
                grad * joined[SUB : SUB + rows, cols], axis=0, keepdims=True
            )
            for lag in range(1, lags + 1):
                tap = taps_ref[part, lags - lag : lags - lag + 1, tap_cols]
                row = part * tap_count + lags - lag
                small_ref[row : row + 1, tap_cols] = jnp.sum(
                    grad * joined[SUB - lag : SUB - lag + rows, cols] * masks[lag],
                    axis=0,
                    keepdims=True,
                )
                moved = du_s[SUB + lag : SUB + lag + rows, :]
                dp = dp + tap * moved * mask_s[lag - 1, SUB + lag : SUB + lag + rows, :]
                halo = halo + tap * du_s[lag : lag + SUB, :] * mask_s[lag - 1, lag : lag + SUB, :]
            gp_ref[:, cols] = dp
            halo_ref[:, cols] = halo


def input_back_kernel(
    place, gp_ref, next_ref, dgr_ref, wq_ref, wk_ref, wv_ref, wg_ref, wb_ref,
    x_ref, sums_ref, keep_ref, send_ref, whole, gpf_ref,
):
    rows, wide = gp_ref.shape
    width = next_ref.shape[1]
    head_width = width // 3
    gpf_ref[...] = gp_ref[...].astype(bf16)
    last = gp_ref[rows - 2 * SUB :, :width]
    gpf_ref[rows - 2 * SUB :, :width] = jnp.concatenate(
        [last[:SUB], last[SUB:] + next_ref[...]], axis=0
    ).astype(bf16)
    total = mm(dgr_ref[...], wg_ref[...], 1, 1) + mm(gpf_ref[:, width : width + SUB], wb_ref[...])
    for part, w_ref in enumerate((wq_ref, wk_ref, wv_ref)):
        total = total + mm(gpf_ref[:, part * head_width : (part + 1) * head_width], w_ref[...], 1, 1)
    whole[...] = total
    split_rows(place, whole, keep_ref, send_ref)
    x = x_ref[...].astype(f32)
    scale = lax.rsqrt(jnp.mean(x * x, axis=-1, keepdims=True) + 1e-06)
    sums = jnp.concatenate(
        [
            jnp.sum(total * (x * scale), axis=0, keepdims=True),
            sums_ref[1:2, :],
            jnp.zeros((2 * SUB - 2, total.shape[1]), f32),
        ],
        axis=0,
    ).astype(bf16)
    keep_ref[rows // 2 :, :] = sums
    send_ref[rows // 2 :, :] = sums


def small_places(model, taps, heads, width):
    sizes = [model, LANES, model, 3 * taps * heads * LANES, heads * model, LANES]
    starts = [0]
    for size in sizes:
        starts.append(starts[-1] + size // LANES)
    across = width // LANES
    rows = -(-starts[-1] // across)
    return starts[:-1], -(-rows // (2 * SUB)) * 2 * SUB


def piece_at(index, width):
    across = width // LANES
    col = index % across * LANES
    return (slice(index // across, index // across + 1), slice(col, col + LANES))


def project_grads_kernel(
    bits, taps, place, a_ref, before_ref, gp_ref, halo_ref, sums_a, gsmall_ref,
    keep_ref, send_ref, whole, small,
):
    a = a_ref[...]
    model = a.shape[1]
    width = whole.shape[1]
    heads = width // (3 * LANES)
    starts, _ = small_places(model, taps, heads, width)
    small[...] = jnp.zeros(small.shape, f32)
    beta_rows = mm(gp_ref[:, width:], a, 0, 0)
    pieces = model // LANES
    for piece in range(pieces):
        cols = slice(piece * LANES, (piece + 1) * LANES)
        small[piece_at(starts[2] + piece, width)] = sums_a[0:1, cols]
        for head in range(heads):
            small[piece_at(starts[4] + head * pieces + piece, width)] = beta_rows[head : head + 1, cols]
    for row in range(3 * taps):
        for head in range(heads):
            small[piece_at(starts[3] + row * heads + head, width)] = gsmall_ref[
                row : row + 1, head * LANES : (head + 1) * LANES
            ]
    small[piece_at(starts[5], width)] = gsmall_ref[3 * taps : 3 * taps + 1, 0:LANES]
    edge = jnp.concatenate([jnp.zeros((SUB, width), f32), halo_ref[...]], axis=0)
    whole[...] = (mm(a, gp_ref[:, :width], 0, 0) + mm(before_ref[...], edge, 0, 0)).astype(bf16)
    emit_shares(place, bits, whole, keep_ref, send_ref)
    keep_ref[model // 2 :, :] = small[...].astype(bf16)
    send_ref[model // 2 :, :] = small[...].astype(bf16)


def head_rows_kernel(place, da_ref, out_ref):
    out_ref[...] = da_ref[da_ref.shape[0] - 2 * SUB :, :].astype(f32)[0:SUB, :]


def share_small_kernel(taps, place, keep_ref, got_ref, *rest):
    keep_out, send_out_ref, small = rest[-3:]
    width = keep_ref.shape[1]
    heads = width // (3 * LANES)
    tail = small.shape[0]
    half = keep_out.shape[0] - tail
    total = keep_ref[2 * half :, :].astype(f32) + got_ref[2 * half :, :].astype(f32)
    small[...] = total
    if len(rest) > 3:
        head_own, head_got = rest[:2]
        joint = head_own[...] + head_got[...]
        model = joint.shape[1]
        starts, _ = small_places(model, taps, heads, width)
        for piece in range(model // LANES):
            small[piece_at(starts[0] + piece, width)] = joint[0:1, piece * LANES : (piece + 1) * LANES]
        small[piece_at(starts[1], width)] = joint[1:2, 0:LANES]
    keep_out[0:half, :] = keep_ref[0:half, :] + got_ref[0:half, :]
    send_out_ref[0:half, :] = keep_ref[half : 2 * half, :] + got_ref[half : 2 * half, :]
    keep_out[half:, :] = small[...].astype(bf16)
    send_out_ref[half:, :] = small[...].astype(bf16)


def project_sum_kernel(
    taps, place, keep_ref, got_ref, q_ref, k_ref, v_ref,
    norm_ref, hgain_ref, fgain_ref, taps_ref, beta_ref, bias_ref, small, rows_s,
):
    share, head_width = q_ref.shape
    width = 3 * head_width
    heads = head_width // LANES
    total = keep_ref[...].astype(f32) + got_ref[...].astype(f32)
    for index, out_ref in enumerate((q_ref, k_ref, v_ref)):
        out_ref[...] = total[:share, index * head_width : (index + 1) * head_width]
    small[...] = total[share:, :]
    model = norm_ref.shape[1]
    starts, _ = small_places(model, taps, heads, width)
    pieces = model // LANES
    for piece in range(pieces):
        cols = slice(piece * LANES, (piece + 1) * LANES)
        norm_ref[0:1, cols] = small[piece_at(starts[0] + piece, width)]
        fgain_ref[0:1, cols] = small[piece_at(starts[2] + piece, width)]
        for head in range(heads):
            row = small[piece_at(starts[4] + head * pieces + piece, width)]
            rows_s[head * pieces + piece : head * pieces + piece + 1, :] = row
    hgain_ref[...] = small[piece_at(starts[1], width)]
    for part in range(3):
        for tap in range(taps):
            for head in range(heads):
                taps_ref[part, tap : tap + 1, head * LANES : (head + 1) * LANES] = small[
                    piece_at(starts[3] + (part * taps + tap) * heads + head, width)
                ]
    bias_ref[...] = small[piece_at(starts[5], width)][:, : bias_ref.shape[1]]
    if share % LANES:
        for head in range(heads):
            for piece in range(pieces):
                at = head * pieces + piece
                beta_ref[head : head + 1, piece * LANES : (piece + 1) * LANES] = rows_s[at : at + 1, :]
    else:
        for head in range(heads):
            for piece in range(share // LANES):
                at = head * pieces + place[0] * (share // LANES) + piece
                beta_ref[head : head + 1, piece * LANES : (piece + 1) * LANES] = rows_s[pl.ds(at, 1), :]


def input_grad_kernel(place, mine, theirs, x_ref, gain_ref, dh_ref, out_ref, whole):
    join_rows(place, mine[...].astype(f32), theirs[...].astype(f32), whole)
    x = x_ref[...].astype(f32)
    scale = lax.rsqrt(jnp.mean(x * x, axis=-1, keepdims=True) + 1e-06)
    hat = x * scale
    grad = whole[...] * gain_ref[...]
    inner = jnp.mean(grad * hat, axis=-1, keepdims=True)
    out_ref[...] = dh_ref[...] + scale * (grad - hat * inner)


def output_kernel(place, mine, theirs, h_ref, out_ref, whole):
    join_rows(place, mine[...].astype(f32), theirs[...].astype(f32), whole)
    out_ref[...] = (h_ref[...] + whole[...]).astype(bf16)


def add_kernel(place, left_ref, right_ref, out_ref):
    out_ref[...] = (left_ref[...].astype(f32) + right_ref[...].astype(f32)).astype(out_ref.dtype)


def added(place, left, right, deps=()):
    shape = left.value.shape if isinstance(left, Free) else left.shape
    (out,) = kernel_call(
        add_kernel, (shaped(shape, right.dtype),), place, left, right, name="added", deps=deps
    )
    return out


def head_sum(place, keep, send, first=(), second=()):
    count = lax.axis_size("head")
    mine = added(place, keep, swap(send, "head", 1), first)
    bit = 2
    while bit < count:
        mine = added(place, mine, swap(mine, "head", bit), second)
        bit *= 2
    return mine, swap(mine, "head", 1)


def gathered(value):
    count = lax.axis_size("head")
    blocks = [value]
    bit = 2
    while bit < count:
        blocks = blocks + [swap(block, "head", bit) for block in blocks]
        bit *= 2
    return blocks + [swap(block, "head", 1) for block in blocks]


def share_rounds(place, keep, send, bits, waits=None):
    arrived = []
    for index, bit in enumerate(bits):
        got = swap(send, "seq", 1 << bit)
        arrived.append(got)
        if index == len(bits) - 1:
            return (keep, got), arrived
        shape = keep.value.shape if isinstance(keep, Free) else keep.shape
        half = (shape[0] // 2,) + shape[1:]
        keep, send = kernel_call(
            share_round_kernel, (shaped(half, bf16), shaped(half, bf16)),
            place, keep, got, name="share_round",
            deps=waits[index] if waits and index < len(waits) else (),
        )


def body(
    block_input, cotangent, segment_ids, norm_gain, w_query, w_key, w_value, w_gate, w_beta,
    beta_bias, conv_weight, head_gain, w_out, ffn_gain, w_ffn_gate, w_ffn_up, w_ffn_down,
):
    rows, model = block_input.shape
    heads = w_beta.shape[1]
    head_width = w_query.shape[1]
    ffn_width = w_ffn_gate.shape[1]
    taps = conv_weight.shape[1]
    seq_count = lax.axis_size("seq")
    rounds = seq_count.bit_length() - 1
    share = model // seq_count
    width = 3 * head_width
    chunks = rows // CHUNK
    y_first = list(range(rounds))

    place = Place()
    bias_in = beta_bias[None] if heads > 1 else jnp.broadcast_to(beta_bias[None], (1, 2))
    gain_row, fgain_row, hgain_row = Free(norm_gain[None]), Free(ffn_gain[None]), Free(head_gain[None])
    taps_in = Free(conv_weight)

    square = (rows, head_width)
    p, beta, seg_cols, tail, a, gate_raw, w_beta8, w_out_copy = kernel_call(
        project_kernel,
        (
            shaped((rows, width), bf16),
            shaped(square, f32),
            shaped((rows, LANES), f32),
            shaped((SUB, width + LANES + model), f32),
            Direct((rows, model), bf16),
            Direct(square, f32),
            Direct((SUB, model), f32),
            Direct(w_out.shape, bf16),
        ),
        place, Far(block_input), Far(w_query), Far(w_key), Far(w_value), Far(w_gate),
        Far(norm_gain[None]), Far(w_beta.T), Far(bias_in),
        Far(segment_ids.reshape(chunks, LANES)), Far(w_out),
        scratch=(
            pltpu.VMEM((rows, model), bf16),
            pltpu.VMEM((4, model, head_width), bf16),
            pltpu.VMEM((1, model), f32),
            pltpu.VMEM((heads, model), bf16),
            pltpu.VMEM(bias_in.shape, f32),
            pltpu.VMEM((chunks, LANES), jnp.int32),
            pltpu.VMEM((rows, model), bf16),
            pltpu.VMEM(square, f32),
            pltpu.VMEM((SUB, model), f32),
            pltpu.VMEM(w_out.shape, bf16),
            pltpu.SemaphoreType.DMA((10,)),
            pltpu.SemaphoreType.DMA((4,)),
        ),
        name="project",
        flops=2 * rows * model * (4 * head_width + LANES),
    )
    halo = shift(tail, "seq", 1)
    joined = pltpu.VMEM((rows + SUB, width), f32)
    joined_ids = pltpu.VMEM((rows + SUB, LANES), f32)
    maps, mix, back, facts, a_before = kernel_call(
        delta_kernel,
        (
            shaped((2 * heads * HEAD_DIM, HEAD_DIM), bf16),
            shaped((rows + 2 * SUB, 4 * head_width), bf16),
            shaped((rows + 2 * SUB, 2 * width + 4 * head_width), bf16),
            shaped((rows + SUB, head_width + LANES), f32),
            shaped((2 * SUB, model), bf16),
        ),
        place, p, halo, Held(conv_weight), seg_cols, beta,
        scratch=(joined, joined_ids),
        name="delta",
        flops=2 * heads * chunks * 128**3 * 30,
    )
    half_maps = heads * HEAD_DIM
    back, facts, steps, a_before = park(
        place, (back, None), (facts, None), (mix, 2 * head_width), (a_before, None), name="park_delta"
    )
    w_out_all = gathered(w_out_copy)
    prefix = pack = maps
    for bit in range(rounds - 1):
        other = swap(maps, "seq", 1 << bit)
        maps, prefix, pack = kernel_call(
            functools.partial(scan_round_kernel, bit),
            (
                shaped((half_maps if bit == rounds - 2 else 2 * half_maps, HEAD_DIM), bf16),
                shaped((2 * half_maps, HEAD_DIM), bf16),
                shaped((2 * half_maps * (bit + 1), HEAD_DIM), bf16),
            ),
            place, maps, other, prefix, pack,
            name="scan_round",
            flops=2 * heads * 128**3 * 5,
            deps=(Held(steps),) if bit == 0 else (),
        )
    other_a = swap(maps, "seq", 1 << (rounds - 1))
    y, mixed, keep_y = kernel_call(
        functools.partial(mixer_kernel, rounds - 1),
        (shaped(square, bf16), shaped(square, f32), shaped((rows, 2 * head_width), bf16)),
        place, prefix, other_a, mix, Free(gate_raw), hgain_row,
        name="mixer",
        flops=2 * heads * chunks * 128**3 * 2,
    )
    mixed, keep_y, pack = park(
        place, (mixed, None), (keep_y, None), (pack, None), name="park_mixer"
    )
    y_all = gathered(y)
    half = (rows // 2, model)
    wide = pltpu.VMEM((rows, model), f32)
    db_send, h, grad_ffn, hidden, db_keep = kernel_call(
        functools.partial(ffn_kernel, share),
        (
            shaped(half, bf16),
            Direct((rows, model), f32),
            Direct((3 * model, ffn_width), bf16),
            Direct((rows, ffn_width), bf16),
            Direct(half, bf16),
        ),
        place, Free(block_input), Free(cotangent), fgain_row,
        Free(w_ffn_gate.T), Free(w_ffn_up.T), Free(w_ffn_down),
        *y_all, Free(w_out_all[0]), *w_out_all[1:],
        scratch=(
            wide,
            pltpu.VMEM((3 * model, ffn_width), bf16),
            pltpu.VMEM((rows, ffn_width), bf16),
            pltpu.VMEM(half, bf16),
            wide,
            pltpu.SemaphoreType.DMA((4,)),
        ),
        deps=(Held(keep_y),),
        name="ffn",
        flops=2 * rows * model * (model + 8 * ffn_width),
    )
    ffn_shares = lax.psum_scatter(grad_ffn, "seq", scatter_dimension=0, tiled=True)
    out_keep, out_send = kernel_call(
        out_part_kernel,
        (shaped(half, bf16), shaped(half, bf16)),
        place, Held(hidden), Held(w_ffn_down),
        scratch=(wide,),
        name="out_part",
        flops=2 * rows * model * ffn_width,
    )
    db_parts = head_sum(place, Held(db_keep), db_send, second=(out_keep,))
    gh, pull, dh, d_out, d_gate_raw, sums_a = kernel_call(
        residual_back_kernel,
        (
            shaped((rows, model), bf16),
            shaped((half_maps, HEAD_DIM), bf16),
            shaped((rows, model), f32),
            shaped(square, bf16),
            shaped(square, bf16),
            shaped((SUB, model), f32),
        ),
        place, *db_parts, Free(h), Free(cotangent), fgain_row, Free(w_out), Free(mixed),
        Free(gate_raw), hgain_row, Free(steps),
        scratch=(wide,),
        name="residual_back",
        flops=2 * rows * model * head_width,
    )
    dh, d_out, d_gate_raw, sums_a = park(
        place, (dh, None), (d_out, None), (d_gate_raw, None), (sums_a, None), name="park_residual"
    )
    other_pulls = [swap(pull, "seq", 1)]
    early_keep, early_send = kernel_call(
        functools.partial(early_grads_kernel, y_first),
        (shaped((model // 2, 2 * head_width), bf16), shaped((model // 2, 2 * head_width), bf16)),
        place, gh, Free(keep_y), Free(a), Free(d_gate_raw),
        scratch=(pltpu.VMEM((model, 2 * head_width), bf16),),
        deps=(other_pulls[0],),
        name="early_grads",
        flops=2 * rows * model * 2 * head_width,
    )
    early_pair, early_got = share_rounds(place, early_keep, early_send, y_first)
    out_parts = head_sum(place, out_keep, out_send, first=(pull,))
    after = pull
    for bit in range(rounds - 1):
        pull, after = kernel_call(
            functools.partial(back_round_kernel, bit),
            (shaped(pull.shape, bf16), shaped(pull.shape, bf16)),
            place, Free(pack), pull, other_pulls[bit], after,
            name="back_round",
            flops=2 * heads * 128**3 * 2,
            deps=((Held(dh),), (early_keep,))[min(bit, 1)],
        )
        other_pulls.append(swap(pull, "seq", 2 << bit))
    gp, gp_halo, grad_small = kernel_call(
        functools.partial(delta_back_kernel, rounds - 1),
        (
            shaped((rows, width + LANES), f32),
            shaped((SUB, width), f32),
            stored((-(-(3 * taps + 1) // SUB) * SUB, head_width), f32),
        ),
        place, taps_in, Free(back), Free(facts), Free(steps), Free(keep_y), Free(d_out),
        Free(pack), after, other_pulls[-1],
        deps=(out_parts[0],),
        scratch=(
            joined,
            joined_ids,
            pltpu.VMEM((rows, width), f32),
            pltpu.VMEM((rows + 2 * SUB, LANES), f32),
            pltpu.VMEM((taps - 1, rows + 2 * SUB, LANES), f32),
        ),
        name="delta_back",
        flops=2 * heads * chunks * 128**3 * 20,
    )
    from_next = shift(gp_halo, "seq", -1)
    _, small_extra = small_places(model, taps, heads, width)
    keep, send = kernel_call(
        functools.partial(project_grads_kernel, y_first, taps),
        (
            shaped((model // 2 + small_extra, width), bf16),
            shaped((model // 2 + small_extra, width), bf16),
        ),
        place, Free(a), Free(a_before), gp, gp_halo, Free(sums_a), Free(grad_small),
        scratch=(pltpu.VMEM((model, width), bf16), pltpu.VMEM((small_extra, width), f32)),
        name="project_grads",
    )
    (block_output,) = kernel_call(
        output_kernel,
        (final((rows, model), bf16),),
        place, *out_parts, Free(h),
        scratch=(wide,),
        name="output",
    )
    da_keep, da_send = kernel_call(
        input_back_kernel,
        (
            shaped((rows // 2 + 2 * SUB, model), bf16),
            shaped((rows // 2 + 2 * SUB, model), bf16),
        ),
        place, gp, from_next, Free(d_gate_raw),
        Free(w_query), Free(w_key), Free(w_value), Free(w_gate), Free(w_beta8), Free(block_input),
        Free(sums_a),
        deps=(early_got[0], keep),
        scratch=(wide, pltpu.VMEM((rows, width + LANES), bf16)),
        name="input_back",
    )
    da_parts = head_sum(place, da_keep, da_send, second=(Held(block_output), early_got[1]))
    (head_small,) = kernel_call(
        head_rows_kernel, (shaped((SUB, model), f32),), place, da_parts[0], name="head_rows"
    )
    head_got = swap(head_small, "seq", 1)
    (input_grad,) = kernel_call(
        input_grad_kernel,
        (final((rows, model), f32),),
        place, *da_parts, Free(block_input), gain_row, Free(dh),
        scratch=(wide,),
        name="input_grad",
    )
    for bit in range(rounds):
        got = swap(send, "seq", 1 << bit)
        if bit < rounds - 1:
            shape = ((keep.shape[0] - small_extra) // 2 + small_extra, width)
            keep, send = kernel_call(
                functools.partial(share_small_kernel, taps),
                (shaped(shape, bf16), shaped(shape, bf16)),
                place, keep, got, *((head_small, head_got) if bit == 0 else ()),
                scratch=(pltpu.VMEM((small_extra, width), f32),),
                name="share_small",
            )
    out_share, w_gate_share = kernel_call(
        early_sum_kernel,
        (final((head_width, share), f32), final((share, head_width), f32)),
        place, *early_pair, name="early_sum",
    )
    beta_shape = (heads, model if share % LANES else share)
    (
        q_share, k_share, v_share, norm_total, head_gain_total, ffn_gain_total, conv_total, beta_rows,
        bias_total,
    ) = kernel_call(
        functools.partial(project_sum_kernel, taps),
        tuple(final((share, head_width), f32) for _ in range(3))
        + (
            final((1, model), f32),
            final((1, LANES), f32),
            final((1, model), f32),
            final(conv_weight.shape, f32),
            final(beta_shape, f32),
            final((1, heads), f32),
        ),
        place, keep, got,
        deps=(Held(input_grad), Held(out_share)),
        scratch=(
            pltpu.VMEM((small_extra, width), f32),
            pltpu.VMEM((-(-heads * model // LANES // SUB) * SUB, LANES), f32),
        ),
        name="project_sum",
    )
    if share % LANES:
        beta_rows = lax.dynamic_slice(beta_rows, (0, lax.axis_index("seq") * share), (heads, share))
    beta_share = beta_rows.T
    down_share, ffn_gate_share, ffn_up_share = kernel_call(
        ffn_shares_kernel,
        tuple(final((ffn_width, share), f32) for _ in range(3)),
        place, Free(ffn_shares), name="ffn_shares",
    )
    return (
        block_output,
        input_grad,
        norm_total[0],
        q_share,
        k_share,
        v_share,
        w_gate_share,
        beta_share,
        bias_total[0],
        conv_total,
        head_gain_total[0],
        out_share,
        ffn_gain_total[0],
        ffn_gate_share.T,
        ffn_up_share.T,
        down_share,
    )


def solution(mesh):
    return jax.shard_map(
        body,
        mesh=mesh,
        in_specs=(
            P("seq", None), P("seq", None), P("seq"), P(),
            P(None, "head"), P(None, "head"), P(None, "head"), P(None, "head"), P(None, "head"),
            P("head"), P(None, None, "head"), P(), P("head", None), P(),
            P(None, "head"), P(None, "head"), P("head", None),
        ),
        out_specs=(
            P("seq", None), P("seq", None), P(),
            P("seq", "head"), P("seq", "head"), P("seq", "head"), P("seq", "head"), P("seq", "head"),
            P("head"), P(None, None, "head"), P(), P("head", "seq"), P(),
            P("seq", "head"), P("seq", "head"), P("head", "seq"),
        ),
        check_vma=False,
    )
```

```python
import functools
import math

import jax
import jax.numpy as jnp
from jax import lax
from jax.experimental import pallas as pl
from jax.experimental.pallas import tpu as pltpu
from jax.sharding import PartitionSpec as P

HEAD_DIM = 128
CHUNK = 128
LANES = 128
SUB = 8
Q_SCALE = HEAD_DIM ** (-0.5)
VMEM_SLACK = 14 * 1024 * 1024

ORDER = (
    "db_core",
    "out_part",
    "db_far",
    "residual_back",
    "park_back",
    "down_one",
    "gate_one",
    "scan_back",
    "up_blocks",
    "out_core",
    "scan_rest",
    "delta_query",
    "early_grads",
    "down_two",
    "gate_two",
    "out_far",
    "delta_back",
    "input_back",
    "up_one",
    "rows_core",
    "input_split",
    "rows_far",
    "project_grads",
    "up_two",
    "early_one",
    "da_core",
    "output",
    "down_out",
    "share_one",
    "early_two",
    "up_out",
    "da_far",
    "input_grad",
    "share_two",
    "early_out",
    "gate_out",
)
PLANS = {"down": "first", "gate": "last", "up": "first", "early": "first", "project": "first"}

bf16 = jnp.bfloat16
f32 = jnp.float32


def mm(left, right, left_dim=1, right_dim=0):
    return lax.dot_general(
        left.astype(bf16),
        right.astype(bf16),
        (((left_dim,), (right_dim,)), ((), ())),
        preferred_element_type=f32,
    )


def sigmoid(value):
    return 1.0 / (1.0 + jnp.exp(-value))


class Free:
    def __init__(self, value):
        self.value = value


class Held(Free):
    pass


class Far(Free):
    pass


class Place:
    def __getitem__(self, which):
        return lax.axis_index(("seq", "head")[which])


class Direct:
    def __init__(self, shape, dtype):
        self.shape, self.dtype = tuple(shape), dtype


class Chain:
    def __init__(self):
        self.token = None


def kernel_call(body, out_shapes, chain, *args, scratch=(), name, deps=()):
    vmem = pl.BlockSpec(memory_space=pltpu.VMEM)
    anywhere = pl.BlockSpec(memory_space=pl.ANY)
    size_of = lambda a: math.prod(a.shape) * jnp.dtype(a.dtype).itemsize
    held = sum(size_of(s) for s in scratch if hasattr(s, "dtype") and not is_semaphore(s))
    operands, specs = [], []
    for arg in args:
        if isinstance(arg, Free):
            value = arg.value
            if not type(arg) is Free:
                value = pltpu.with_memory_space_constraint(value, pltpu.HBM)
            operands.append(value)
            specs.append(anywhere if isinstance(arg, Far) else vmem)
            if not isinstance(arg, Far):
                held += size_of(value)
        else:
            operands.append(pltpu.with_memory_space_constraint(arg, pltpu.VMEM))
            specs.append(vmem)
    ins, outs = len(args), len(out_shapes)
    waits = (0 if chain.token is None else 1) + len(deps)
    operands += list(deps)
    specs += [anywhere] * len(deps)
    if chain.token is not None:
        operands.append(pltpu.with_memory_space_constraint(chain.token, pltpu.VMEM))
        specs.append(vmem)
    results, result_specs = [], []
    for out in out_shapes:
        if isinstance(out, Direct):
            results.append(pltpu.HBM(out.shape, out.dtype))
            result_specs.append(anywhere)
        else:
            results.append(out)
            result_specs.append(vmem)
            if isinstance(out, jax.ShapeDtypeStruct) or out.memory_space == pltpu.HBM:
                held += size_of(out)
    results.append(shaped((SUB, LANES), f32))
    result_specs.append(vmem)
    here = Place()

    def run(*refs):
        refs[ins + waits + outs][...] = jnp.zeros((SUB, LANES), f32)
        body(here, *refs[:ins], *refs[ins + waits : ins + waits + outs], *refs[ins + waits + outs + 1 :])

    *values, chain.token = pl.pallas_call(
        run,
        out_shape=tuple(results),
        in_specs=specs,
        out_specs=tuple(result_specs),
        scratch_shapes=list(scratch),
        compiler_params=pltpu.CompilerParams(vmem_limit_bytes=int(held) + VMEM_SLACK),
        cost_estimate=pl.CostEstimate(flops=0, bytes_accessed=0, transcendentals=0),
        name=name,
    )(*operands)
    return values


def stored(shape, dtype):
    return pltpu.HBM(tuple(shape), dtype)


def send_out(source, target, sems, index):
    copy = pltpu.make_async_copy(source, target, sems.at[index])
    copy.start()
    return copy


def is_semaphore(scratch):
    return not (
        jnp.issubdtype(scratch.dtype, jnp.floating) or jnp.issubdtype(scratch.dtype, jnp.integer)
    )


def final(shape, dtype):
    return jax.ShapeDtypeStruct(tuple(shape), dtype)


def shaped(shape, dtype):
    return pltpu.VMEM(tuple(shape), dtype)


def swap(value, axis, bit):
    count = lax.axis_size(axis)
    return lax.ppermute(value, axis, [(s, s ^ bit) for s in range(count)])


def shift(value, axis, step):
    count = lax.axis_size(axis)
    return lax.ppermute(
        value, axis, [(s, s + step) for s in range(count) if 0 <= s + step < count]
    )


def bit_of(place_ref, which, bit):
    return lax.rem(lax.shift_right_logical(place_ref[which], bit), 2)


def chosen(flag, when_one, when_zero):
    return jnp.where(flag == 1, when_one, when_zero)


def tri_masks():
    rows = lax.broadcasted_iota(jnp.int32, (CHUNK, CHUNK), 0)
    cols = lax.broadcasted_iota(jnp.int32, (CHUNK, CHUNK), 1)
    return rows, cols


def unit_inverses(lowers):
    rows, cols = tri_masks()
    eye = jnp.where(rows == cols, 1.0, 0.0).astype(f32)
    width = 1
    inverses = None
    while width < CHUNK:
        shift_bits = width.bit_length() - 1
        row_block = lax.shift_right_logical(rows, shift_bits)
        col_block = lax.shift_right_logical(cols, shift_bits)
        within = (
            lax.shift_right_logical(row_block, 1) == lax.shift_right_logical(col_block, 1)
        ) & (row_block != col_block)
        couplings = [jnp.where(within, low, 0.0) for low in lowers]
        if inverses is None:
            inverses = [eye - coupling for coupling in couplings]
        else:
            halves = [mm(inv, coupling) for inv, coupling in zip(inverses, couplings)]
            inverses = [inv - mm(half, inv) for inv, half in zip(inverses, halves)]
        width *= 2
    return inverses


def project_kernel(
    place, x_hbm, wq_hbm, wk_hbm, wv_hbm, wg_hbm, gain_hbm, wb_hbm, bias_hbm, seg_hbm, wo_hbm,
    p_ref, beta_ref, segc_ref, tail_ref, a_hbm, gate_hbm, wb8_hbm, wo_out,
    x_s, weights, gain_s, wb_s, bias_s, seg_s, a_s, gate_s, wb8_s, wo_s, arrived, left,
):
    rows = x_s.shape[0]
    head_width = wq_hbm.shape[1]
    heads = head_width // LANES
    pairs = ((x_hbm, x_s), (gain_hbm, gain_s), (seg_hbm, seg_s), (wb_hbm, wb_s), (bias_hbm, bias_s))
    pairs += ((wo_hbm, wo_s),)
    pairs += tuple(
        (source, weights.at[index]) for index, source in enumerate((wg_hbm, wq_hbm, wk_hbm, wv_hbm))
    )
    copies = [send_out(source, target, arrived, index) for index, (source, target) in enumerate(pairs)]
    for copy in copies[:5]:
        copy.wait()
    wo_copy, *copies = copies[5:]
    segr = seg_s[...].astype(f32)
    wb8_s[...] = jnp.zeros(wb8_s.shape, f32)
    wb8_s[0:heads, :] = wb_s[...].astype(f32)
    leaving = [send_out(wb8_s, wb8_hbm, left, 2)]
    x = x_s[...].astype(f32)
    scale = lax.rsqrt(jnp.mean(x * x, axis=-1, keepdims=True) + 1e-06)
    a = (x * scale * gain_s[...]).astype(bf16)
    a_s[...] = a
    tail_ref[:, 3 * head_width + LANES :] = a.astype(f32)[rows - SUB :, :]
    leaving.append(send_out(a_s, a_hbm, left, 0))
    logits = mm(a, wb8_s[...], 1, 1)
    for head in range(heads):
        column = logits[:, head : head + 1] + bias_s[:, head : head + 1]
        beta_ref[:, head * LANES : (head + 1) * LANES] = sigmoid(
            jnp.broadcast_to(column, (rows, LANES))
        )
    for chunk in range(rows // CHUNK):
        ids = jnp.broadcast_to(segr[chunk : chunk + 1, :], (CHUNK, LANES))
        turned = ids.T
        segc_ref[chunk * CHUNK : (chunk + 1) * CHUNK, :] = turned
        if chunk == rows // CHUNK - 1:
            tail_ref[:, 3 * head_width : 3 * head_width + LANES] = turned[CHUNK - SUB :, :]
    wo_copy.wait()
    leaving.append(send_out(wo_s, wo_out, left, 3))
    copies[0].wait()
    gate_s[...] = mm(a, weights[0])
    leaving.append(send_out(gate_s, gate_hbm, left, 1))
    for part in range(3):
        copies[part + 1].wait()
        value = mm(a, weights[part + 1])
        cols = slice(part * head_width, (part + 1) * head_width)
        low = value.astype(bf16)
        p_ref[:, cols] = low
        tail_ref[:, cols] = low.astype(f32)[rows - SUB :, :]
    for copy in leaving:
        copy.wait()


def lag_masks(joined_ids, lags):
    rows = joined_ids.shape[0] - SUB
    ids = joined_ids[SUB : SUB + rows, :]
    return [None] + [
        jnp.where(joined_ids[SUB - lag : SUB - lag + rows, :] == ids, 1.0, 0.0)
        for lag in range(1, lags + 1)
    ]


def conv_sum(joined, taps_ref, masks, part, head, head_width, rows):
    lags = taps_ref.shape[1] - 1
    col = part * head_width + head * LANES
    tap_cols = slice(head * LANES, (head + 1) * LANES)
    total = taps_ref[part, lags : lags + 1, tap_cols] * joined[SUB : SUB + rows, col : col + LANES]
    for lag in range(1, lags + 1):
        tap = taps_ref[part, lags - lag : lags - lag + 1, tap_cols]
        total = total + tap * joined[SUB - lag : SUB - lag + rows, col : col + LANES] * masks[lag]
    return total


def chunk_flags(joined_ids, chunk):
    start = chunk * CHUNK
    ids = joined_ids[SUB + start : SUB + start + CHUNK, :]
    same = jnp.where(ids == ids.T, 1.0, 0.0)
    before = joined_ids[SUB + start - 1 : SUB + start, :]
    final_id = joined_ids[SUB + start + CHUNK - 1 : SUB + start + CHUNK, :]
    opened = jnp.where(ids == before, 1.0, 0.0)
    closing = jnp.where(ids == final_id, 1.0, 0.0)
    kept = jnp.where(final_id == before, 1.0, 0.0)
    return same, opened, closing, kept


def delta_kernel(
    place, p_ref, tail_ref, taps_ref, segc_ref, beta_ref,
    maps_ref, mix_ref, back_ref, facts_ref, before_ref,
    joined, joined_ids,
):
    rows, width = p_ref.shape
    head_width = width // 3
    heads = head_width // LANES
    chunks = rows // CHUNK
    first = 2 * SUB
    joined[0:SUB, :] = tail_ref[:, :width]
    joined[SUB : SUB + rows, :] = p_ref[...].astype(f32)
    joined_ids[0:SUB, :] = tail_ref[:, width : width + LANES]
    joined_ids[SUB : SUB + rows, :] = segc_ref[...]
    facts_ref[SUB:, 0:head_width] = beta_ref[...]
    facts_ref[0:SUB, 0:head_width] = jnp.zeros((SUB, head_width), f32)
    facts_ref[:, head_width:] = joined_ids[...]
    before_ref[...] = jnp.concatenate(
        [jnp.zeros((SUB, before_ref.shape[1]), f32), tail_ref[:, width + LANES :]], axis=0
    ).astype(bf16)
    back_ref[first:, 0:width] = p_ref[...]
    back_ref[0:first, 0:width] = jnp.concatenate(
        [jnp.zeros((SUB, width), f32), tail_ref[:, :width]], axis=0
    ).astype(bf16)
    back_ref[0:first, width:] = jnp.zeros((first, back_ref.shape[1] - width), bf16)
    masks = lag_masks(joined_ids, taps_ref.shape[1] - 1)
    for part in range(3):
        for head in range(heads):
            total = conv_sum(joined, taps_ref, masks, part, head, head_width, rows)
            z = total * sigmoid(total)
            if part < 2:
                z = z * lax.rsqrt(jnp.sum(z * z, axis=-1, keepdims=True) + 1e-06)
                if part == 0:
                    z = z * Q_SCALE
            col = width + part * head_width + head * LANES
            back_ref[first:, col : col + LANES] = z.astype(bf16)
    row_ids, col_ids = tri_masks()
    flags = [chunk_flags(joined_ids, chunk) for chunk in range(chunks)]
    mix_ref[rows:, :] = jnp.concatenate(
        [jnp.concatenate([flags[min(row, chunks - 1)][3]] * (4 * heads), axis=1) for row in range(2 * SUB)],
        axis=0,
    ).astype(bf16)
    sets = [(head, chunk) for head in range(heads) for chunk in range(chunks)]

    def at_of(head, chunk, part=0):
        col = part * head_width + head * LANES
        return (slice(chunk * CHUNK, (chunk + 1) * CHUNK), slice(col, col + LANES))

    def kept_at(head, chunk, part):
        col = (3 + part) * head_width + head * LANES
        return (slice(first + chunk * CHUNK, first + (chunk + 1) * CHUNK), slice(col, col + LANES))

    lowers = []
    for head, chunk in sets:
        same = flags[chunk][0]
        q, k = back_ref[kept_at(head, chunk, 0)], back_ref[kept_at(head, chunk, 1)]
        inner = mm(jnp.concatenate([q, k], axis=0), k, 1, 1)
        scores = jnp.where(row_ids >= col_ids, inner[:CHUNK] * same, 0.0)
        back_ref[kept_at(head, chunk, 6)] = scores.astype(bf16)
        lowers.append(
            jnp.where(row_ids > col_ids, inner[CHUNK:] * same * beta_ref[at_of(head, chunk)], 0.0)
        )
    inverses = unit_inverses(lowers)
    eye = jnp.where(row_ids == col_ids, 1.0, 0.0).astype(f32)
    maps = [
        jnp.concatenate([eye, jnp.zeros((HEAD_DIM, HEAD_DIM), f32)], axis=1) for _ in range(heads)
    ]
    products = []
    for (head, chunk), inverse in zip(sets, inverses):
        beta = beta_ref[at_of(head, chunk)]
        k = back_ref[kept_at(head, chunk, 1)].astype(f32)
        v = back_ref[kept_at(head, chunk, 2)].astype(f32)
        both = jnp.concatenate([beta * k, beta * v], axis=1)
        products.append(mm(inverse, both))
    steps = {}
    for (head, chunk), inverse, product in zip(sets, inverses, products):
        same, opened, closing, kept = flags[chunk]
        w_rows, u_rows = product[:, :HEAD_DIM], product[:, HEAD_DIM:]
        back_ref[kept_at(head, chunk, 3)] = w_rows.astype(bf16)
        back_ref[kept_at(head, chunk, 4)] = u_rows.astype(bf16)
        back_ref[kept_at(head, chunk, 5)] = inverse.astype(bf16)
        both = jnp.concatenate([opened * w_rows, u_rows], axis=1)
        k = back_ref[kept_at(head, chunk, 1)].astype(f32)
        q = back_ref[kept_at(head, chunk, 0)].astype(f32)
        step = mm(closing * k, both, 0, 0)
        through = mm(back_ref[kept_at(head, chunk, 6)], both)
        mix_ref[at_of(head, chunk, 0)] = (opened * q - through[:, :HEAD_DIM]).astype(bf16)
        mix_ref[at_of(head, chunk, 1)] = step[:, :HEAD_DIM].astype(bf16)
        mix_ref[at_of(head, chunk, 2)] = through[:, HEAD_DIM:].astype(bf16)
        mix_ref[at_of(head, chunk, 3)] = step[:, HEAD_DIM:].astype(bf16)
        steps[head, chunk] = step
    for chunk in range(chunks):
        kept = flags[chunk][3]
        kept_wide = jnp.concatenate([kept, kept], axis=1)
        for head in range(heads):
            step = steps[head, chunk]
            pushed = kept_wide * maps[head] - mm(step[:, :HEAD_DIM], maps[head])
            maps[head] = jnp.concatenate(
                [pushed[:, :HEAD_DIM], pushed[:, HEAD_DIM:] + step[:, HEAD_DIM:]], axis=1
            )
    for head in range(heads):
        maps_ref[head * HEAD_DIM : (head + 1) * HEAD_DIM, :] = maps[head][:, :HEAD_DIM].astype(bf16)
        base = (heads + head) * HEAD_DIM
        maps_ref[base : base + HEAD_DIM, :] = maps[head][:, HEAD_DIM:].astype(bf16)


def park_kernel(count, place, *refs):
    sources, targets, left = refs[:count], refs[count : 2 * count], refs[-1]
    copies = []
    for index, (source, target) in enumerate(zip(sources, targets)):
        if source.shape != target.shape:
            source = source.at[:, 0 : target.shape[1]]
        copies.append(send_out(source, target, left, index))
    for copy in copies:
        copy.wait()


def park(chain, *pairs, name):
    arrays = [value.value if isinstance(value, Free) else value for value, _ in pairs]
    return kernel_call(
        functools.partial(park_kernel, len(pairs)),
        [
            Direct((array.shape[0], array.shape[1] if cols is None else cols), array.dtype)
            for array, (_, cols) in zip(arrays, pairs)
        ],
        chain,
        *[value for value, _ in pairs],
        scratch=(pltpu.SemaphoreType.DMA((len(pairs),)),),
        name=name,
    )


def scan_round_kernel(bit, place, own_ref, other_ref, prefix_ref, pack_ref, total_ref, prefix_out, pack_out):
    upper = bit_of(place, 0, bit)
    half = own_ref.shape[0] // 2
    heads = half // HEAD_DIM
    base = 2 * half * bit
    if bit:
        pack_out[0:base, :] = pack_ref[...]
    for head in range(heads):
        m_at = slice(head * HEAD_DIM, (head + 1) * HEAD_DIM)
        a_at = slice((heads + head) * HEAD_DIM, (heads + head + 1) * HEAD_DIM)
        low_at = slice(base + head * HEAD_DIM, base + (head + 1) * HEAD_DIM)
        suffix_at = slice(base + half + head * HEAD_DIM, base + half + (head + 1) * HEAD_DIM)
        own_m, own_a = own_ref[m_at, :].astype(f32), own_ref[a_at, :].astype(f32)
        other_m, other_a = other_ref[m_at, :].astype(f32), other_ref[a_at, :].astype(f32)
        high_m, high_a = chosen(upper, own_m, other_m), chosen(upper, own_a, other_a)
        low_m, low_a = chosen(upper, other_m, own_m), chosen(upper, other_a, own_a)
        pack_out[low_at, :] = low_m.astype(bf16)
        total = mm(high_m, jnp.concatenate([low_m, low_a], axis=1))
        added_part = (total[:, HEAD_DIM:] + high_a).astype(bf16)
        if total_ref.shape[0] == own_ref.shape[0]:
            total_ref[m_at, :] = total[:, :HEAD_DIM].astype(bf16)
            total_ref[a_at, :] = added_part
        else:
            total_ref[m_at, :] = added_part
        if bit == 0:
            rows, cols = tri_masks()
            eye = jnp.where(rows == cols, 1.0, 0.0).astype(f32)
            prefix_out[m_at, :] = chosen(upper, other_m, eye).astype(bf16)
            prefix_out[a_at, :] = chosen(upper, other_a, jnp.zeros_like(other_a)).astype(bf16)
            pack_out[suffix_at, :] = chosen(upper, eye, other_m.T).astype(bf16)
        else:
            before_m, before_a = prefix_ref[m_at, :].astype(f32), prefix_ref[a_at, :].astype(f32)
            at = base - half + head * HEAD_DIM
            after_m = pack_ref[at : at + HEAD_DIM, :].astype(f32)
            joint = mm(before_m, jnp.concatenate([other_m, other_a], axis=1))
            prefix_out[m_at, :] = chosen(upper, joint[:, :HEAD_DIM], before_m).astype(bf16)
            prefix_out[a_at, :] = chosen(
                upper, joint[:, HEAD_DIM:] + before_a, before_a
            ).astype(bf16)
            pack_out[suffix_at, :] = chosen(upper, after_m, mm(after_m, other_m, 1, 1)).astype(bf16)


def back_round_kernel(bit, place, pack_ref, own_ref, other_ref, after_ref, total_ref, after_out):
    upper = bit_of(place, 0, bit)
    half = own_ref.shape[0]
    base = 2 * half * bit
    for head in range(half // HEAD_DIM):
        at = slice(head * HEAD_DIM, (head + 1) * HEAD_DIM)
        own, other = own_ref[at, :].astype(f32), other_ref[at, :].astype(f32)
        high, low = chosen(upper, own, other), chosen(upper, other, own)
        low_m = pack_ref[base + head * HEAD_DIM : base + (head + 1) * HEAD_DIM, :]
        total_ref[at, :] = (mm(low_m, high, 0, 0) + low).astype(bf16)
        if bit == 0:
            after_out[at, :] = chosen(upper, jnp.zeros_like(other), other).astype(bf16)
        else:
            start = base - half + head * HEAD_DIM
            suffix_m = pack_ref[start : start + HEAD_DIM, :]
            after = after_ref[at, :].astype(f32)
            after_out[at, :] = chosen(upper, after, mm(suffix_m, other) + after).astype(bf16)


def mixer_kernel(
    last_bit, place, prefix_ref, other_a_ref, mix_ref, gate_ref, hgain_ref,
    y_ref, o_ref, keep_ref,
):
    rows, head_width = gate_ref.shape
    heads = head_width // LANES
    upper = bit_of(place, 0, last_bit)
    kept_rows = mix_ref[rows:, 0:LANES].astype(f32)
    for head in range(heads):
        m_at = slice(head * HEAD_DIM, (head + 1) * HEAD_DIM)
        a_at = slice((heads + head) * HEAD_DIM, (heads + head + 1) * HEAD_DIM)
        before_m, before_a = prefix_ref[m_at, :], prefix_ref[a_at, :].astype(f32)
        state = chosen(upper, mm(before_m, other_a_ref[m_at, :]) + before_a, before_a)
        for chunk in range(rows // CHUNK):
            chunk_rows = slice(chunk * CHUNK, (chunk + 1) * CHUNK)
            cols = [
                slice(part * head_width + head * LANES, part * head_width + (head + 1) * LANES)
                for part in range(4)
            ]
            at = (chunk_rows, cols[0])
            low = state.astype(bf16)
            keep_ref[at] = low
            out = mm(mix_ref[at], low) + mix_ref[chunk_rows, cols[2]].astype(f32)
            o_ref[at] = out
            state = (
                kept_rows[chunk : chunk + 1, :] * state
                - mm(mix_ref[chunk_rows, cols[1]], low)
                + mix_ref[chunk_rows, cols[3]].astype(f32)
            )
            gate = gate_ref[at]
            scale = lax.rsqrt(jnp.mean(out * out, axis=-1, keepdims=True) + 1e-05)
            y = (out * scale * hgain_ref[...] * (gate * sigmoid(gate))).astype(bf16)
            y_ref[at] = y
            keep_ref[chunk_rows, cols[1]] = y


def ffn_kernel(
    axis, down_bits, gate_bits, place, x_ref, g_ref, fgain_ref, wg_ref, wu_ref, wd_ref, *rest,
):
    (
        *parts, send_ref, down_send, gate_send, h_hbm, hid_hbm, keep_hbm, down_hbm, gate_hbm, up_hbm,
        h_s, hid_s, keep_s, down_keep, gate_keep, grad_s, up_s, whole, left,
    ) = rest
    y_refs, wo_refs = parts[: len(parts) // 2], parts[len(parts) // 2 :]
    att = None
    for y_ref, wo_ref in zip(y_refs, wo_refs):
        part = mm(y_ref[...], wo_ref[...])
        att = part if att is None else att + part
    h = x_ref[...].astype(f32) + att
    h_s[...] = h
    leaving = [send_out(h_s, h_hbm, left, 0)]
    scale = lax.rsqrt(jnp.mean(h * h, axis=-1, keepdims=True) + 1e-06)
    b = (h * scale * fgain_ref[...]).astype(bf16)
    gate = mm(b, wg_ref[...], 1, 1)
    up = mm(b, wu_ref[...], 1, 1)
    sg = sigmoid(gate)
    act = gate * sg
    hid = (act * up).astype(bf16)
    hid_s[...] = hid
    leaving.append(send_out(hid_s, hid_hbm, left, 2))
    dhid = mm(g_ref[...], wd_ref[...], 1, 1)
    dgate = (dhid * up * (sg * (1.0 + gate * (1.0 - sg)))).astype(bf16)
    dup = (dhid * act).astype(bf16)

    def grad_of(by_units, by_model, out):
        if axis:
            out[...] = mm(by_units, by_model, 0, 0).astype(bf16)
            return
        units = by_units.shape[1]
        if out.shape[1] > units:
            out[:, units:] = jnp.zeros((out.shape[0], out.shape[1] - units), bf16)
        out[:, :units] = mm(by_model, by_units, 0, 0).astype(bf16)

    grad_of(hid, g_ref[...], grad_s)
    emit_shares(place, down_bits, grad_s, down_keep, down_send, axis)
    leaving.append(send_out(down_keep, down_hbm, left, 1))
    grad_of(dgate, b, grad_s)
    emit_shares(place, gate_bits, grad_s, gate_keep, gate_send, axis)
    leaving.append(send_out(gate_keep, gate_hbm, left, 4))
    grad_of(dup, b, up_s)
    leaving.append(send_out(up_s, up_hbm, left, 5))
    whole[...] = mm(dgate, wg_ref[...]) + mm(dup, wu_ref[...])
    split_rows(place, whole, keep_s, send_ref)
    leaving.append(send_out(keep_s, keep_hbm, left, 3))
    for copy in leaving:
        copy.wait()


def split_rows(place, whole, keep_ref, send_ref):
    half = whole.shape[0] // 2
    core = bit_of(place, 1, 0)
    keep_ref[0:half, :] = whole[pl.ds(pl.multiple_of(core * half, half), half), :].astype(bf16)
    send_ref[0:half, :] = whole[pl.ds(pl.multiple_of((1 - core) * half, half), half), :].astype(bf16)


def join_rows(place, mine, theirs, whole):
    half = whole.shape[0] // 2
    core = bit_of(place, 1, 0)
    mine, theirs = mine[:half], theirs[:half]
    whole[pl.ds(pl.multiple_of(core * half, half), half), :] = mine
    whole[pl.ds(pl.multiple_of((1 - core) * half, half), half), :] = theirs


def emit_shares(place, bits, whole, keep_ref, send_ref, axis=0):
    order = [0]
    for bit in reversed(bits[1:]):
        order = order + [relative | (1 << bit) for relative in order]
    block = whole.shape[axis] // (2 * len(order))
    for index, relative in enumerate(order):
        for ref, first in ((keep_ref, 0), (send_ref, 1 << bits[0])):
            owner = lax.bitwise_xor(place[0], jnp.int32(relative | first))
            source = pl.ds(pl.multiple_of(owner * block, block), block)
            target = slice(index * block, (index + 1) * block)
            if axis:
                ref[:, target] = whole[:, source]
            else:
                ref[target, :] = whole[source, :]


def share_round_kernel(axis, place, keep_ref, got_ref, keep_out, send_out):
    half = keep_out.shape[axis]
    for at, ref in ((slice(0, half), keep_out), (slice(half, 2 * half), send_out)):
        if axis:
            ref[...] = keep_ref[:, at] + got_ref[:, at]
        else:
            ref[...] = keep_ref[at] + got_ref[at]


def out_part_kernel(place, hid_ref, wd_ref, keep_ref, send_ref, whole):
    whole[...] = mm(hid_ref[...], wd_ref[...])
    split_rows(place, whole, keep_ref, send_ref)


def emit_kernel(axis, bits, place, whole, keep_ref, send_ref):
    emit_shares(place, bits, whole, keep_ref, send_ref, axis)


def early_grads_kernel(
    bits, place, gh_ref, y_ref, a_ref, dgr_ref, gq_ref, halo_ref, before_ref,
    keep_ref, send_ref, whole,
):
    width = dgr_ref.shape[1]
    whole[:, :width] = mm(gh_ref[...], y_ref[:, width:], 0, 0).astype(bf16)
    whole[:, width : 2 * width] = mm(a_ref[...], dgr_ref[...], 0, 0).astype(bf16)
    edge = jnp.concatenate([jnp.zeros((SUB, width), f32), halo_ref[...]], axis=0)
    whole[:, 2 * width :] = (
        mm(a_ref[...], gq_ref[...], 0, 0) + mm(before_ref[...], edge, 0, 0)
    ).astype(bf16)
    emit_shares(place, bits, whole, keep_ref, send_ref)


def early_sum_kernel(place, keep_ref, got_ref, turned_ref, gate_ref, query_ref):
    total = keep_ref[...].astype(f32) + got_ref[...].astype(f32)
    width = gate_ref.shape[1]
    turned_ref[...] = total[:, :width].T
    gate_ref[...] = total[:, width : 2 * width]
    query_ref[...] = total[:, 2 * width :]


def ffn_share_kernel(axis, place, keep_ref, got_ref, out_ref):
    total = keep_ref[...].astype(f32) + got_ref[...].astype(f32)
    out_ref[...] = total if axis else total.T[: out_ref.shape[0], :]


def residual_back_kernel(
    place, mine, theirs, h_ref, g_ref, fgain_ref, wo_ref, o_ref,
    gate_ref, hgain_ref, steps_ref,
    gh_ref, pull_ref, dh_ref, do_ref, dgr_ref, sums_ref, whole,
):
    rows, head_width = o_ref.shape
    heads = head_width // LANES
    join_rows(place, mine[...].astype(f32), theirs[...].astype(f32), whole)
    h = h_ref[...]
    db = whole[...]
    scale = lax.rsqrt(jnp.mean(h * h, axis=-1, keepdims=True) + 1e-06)
    hat = h * scale
    prod = db * hat
    sums_ref[...] = jnp.zeros(sums_ref.shape, f32)
    sums_ref[0:1, :] = jnp.sum(prod, axis=0, keepdims=True)
    inner = jnp.mean(prod * fgain_ref[...], axis=-1, keepdims=True)
    dh = g_ref[...].astype(f32) + scale * (db * fgain_ref[...] - hat * inner)
    dh_ref[...] = dh
    gh = dh.astype(bf16)
    gh_ref[...] = gh
    dy_all = mm(gh, wo_ref[...], 1, 1)
    hg_sum = jnp.zeros((1, LANES), f32)
    for head in range(heads):
        cols = slice(head * LANES, (head + 1) * LANES)
        out, gate, dy = o_ref[:, cols], gate_ref[:, cols], dy_all[:, cols]
        norm = lax.rsqrt(jnp.mean(out * out, axis=-1, keepdims=True) + 1e-05)
        hat_o = out * norm
        sg = sigmoid(gate)
        act = gate * sg
        hg_sum = hg_sum + jnp.sum(dy * hat_o * act, axis=0, keepdims=True)
        dgain = dy * hgain_ref[...]
        dgr_ref[:, cols] = (dgain * hat_o * (sg * (1.0 + gate * (1.0 - sg)))).astype(bf16)
        e = dgain * act
        do_ref[:, cols] = (norm * (e - hat_o * jnp.mean(e * hat_o, axis=-1, keepdims=True))).astype(bf16)
    sums_ref[1:2, 0:LANES] = hg_sum
    chunks = rows // CHUNK
    kept_rows = steps_ref[rows:, 0:LANES].astype(f32)
    pulls = [None] * heads
    for chunk in range(chunks - 1, -1, -1):
        chunk_rows = slice(chunk * CHUNK, (chunk + 1) * CHUNK)
        for head in range(heads):
            cols = slice(head * LANES, (head + 1) * LANES)
            map_cols = slice(head_width + head * LANES, head_width + (head + 1) * LANES)
            local = mm(steps_ref[chunk_rows, cols], do_ref[chunk_rows, cols], 0, 0)
            if pulls[head] is not None:
                local = (
                    local
                    + kept_rows[chunk : chunk + 1, :] * pulls[head]
                    - mm(steps_ref[chunk_rows, map_cols], pulls[head], 0, 0)
                )
            pulls[head] = local
    for head in range(heads):
        pull_ref[head * HEAD_DIM : (head + 1) * HEAD_DIM, :] = pulls[head].astype(bf16)


def back_places(head_width):
    def at_of(head, chunk, part=0):
        col = part * head_width + head * LANES
        return (slice(chunk * CHUNK, (chunk + 1) * CHUNK), slice(col, col + LANES))

    def kept_at(head, chunk, part):
        col = (3 + part) * head_width + head * LANES
        start = 2 * SUB + chunk * CHUNK
        return (slice(start, start + CHUNK), slice(col, col + LANES))

    return at_of, kept_at


def fill_joined(back_ref, facts_ref, joined, joined_ids, head_width):
    width = 3 * head_width
    joined[0:SUB, :] = back_ref[0 : 2 * SUB, :width].astype(f32)[SUB:, :]
    joined[SUB:, :] = back_ref[2 * SUB :, :width].astype(f32)
    joined_ids[...] = facts_ref[:, head_width : head_width + LANES]


def fill_lag_masks(masks, mask_s, du_s):
    rows = mask_s.shape[1] - 2 * SUB
    du_s[0:SUB, :] = jnp.zeros((SUB, LANES), f32)
    du_s[SUB + rows :, :] = jnp.zeros((SUB, LANES), f32)
    for lag in range(1, len(masks)):
        mask_s[lag - 1, 0:SUB, :] = jnp.zeros((SUB, LANES), f32)
        mask_s[lag - 1, SUB : SUB + rows, :] = masks[lag]
        mask_s[lag - 1, SUB + rows :, :] = jnp.zeros((SUB, LANES), f32)


def conv_back(taps_ref, joined, masks, mask_s, du_s, part, head, head_width, rows, grad):
    lags = len(masks) - 1
    col = part * head_width + head * LANES
    cols = slice(col, col + LANES)
    tap_cols = slice(head * LANES, (head + 1) * LANES)
    total = conv_sum(joined, taps_ref, masks, part, head, head_width, rows)
    sg = sigmoid(total)
    if part < 2:
        z = total * sg
        norm = lax.rsqrt(jnp.sum(z * z, axis=-1, keepdims=True) + 1e-06)
        hat = z * norm
        grad = norm * (grad - hat * jnp.sum(grad * hat, axis=-1, keepdims=True))
        if part == 0:
            grad = grad * Q_SCALE
    grad = grad * (sg * (1.0 + total * (1.0 - sg)))
    du_s[SUB : SUB + rows, :] = grad
    before = taps_ref[part, lags : lags + 1, tap_cols] * grad
    halo = jnp.zeros((SUB, LANES), f32)
    tap_grads = [None] * (lags + 1)
    tap_grads[lags] = jnp.sum(grad * joined[SUB : SUB + rows, cols], axis=0, keepdims=True)
    for lag in range(1, lags + 1):
        tap = taps_ref[part, lags - lag : lags - lag + 1, tap_cols]
        tap_grads[lags - lag] = jnp.sum(
            grad * joined[SUB - lag : SUB - lag + rows, cols] * masks[lag], axis=0, keepdims=True
        )
        moved = du_s[SUB + lag : SUB + lag + rows, :]
        before = before + tap * moved * mask_s[lag - 1, SUB + lag : SUB + lag + rows, :]
        halo = halo + tap * du_s[lag : lag + SUB, :] * mask_s[lag - 1, lag : lag + SUB, :]
    return before, halo, tap_grads


def delta_query_kernel(
    place, taps_ref, back_ref, facts_ref, keep_ref, do_ref,
    pre_ref, dk_ref, gq_ref, halo_ref, small_ref,
    joined, joined_ids, dq_s, du_s, mask_s,
):
    rows, head_width = do_ref.shape
    heads = head_width // LANES
    chunks = rows // CHUNK
    fill_joined(back_ref, facts_ref, joined, joined_ids, head_width)
    masks = lag_masks(joined_ids, taps_ref.shape[1] - 1)
    row_ids, col_ids = tri_masks()
    flags = [chunk_flags(joined_ids, chunk) for chunk in range(chunks)]
    at_of, kept_at = back_places(head_width)
    for head in range(heads):
        for chunk in range(chunks):
            same, opened, closing, kept = flags[chunk]
            at = at_of(head, chunk)
            q, k, w_rows, u_rows, scores = (
                back_ref[kept_at(head, chunk, part)] for part in (0, 1, 3, 4, 6)
            )
            state, do = keep_ref[at], do_ref[at]
            fresh = (u_rows.astype(f32) - opened * mm(w_rows, state)).astype(bf16)
            pre_ref[at] = fresh
            pre_ref[at_of(head, chunk, 1)] = mm(scores, do, 0, 0).astype(bf16)
            dscore = jnp.where(row_ids >= col_ids, mm(do, fresh, 1, 1) * same, 0.0).astype(bf16)
            dq_s[at] = opened * mm(do, state, 1, 1) + mm(dscore, k)
            dk_ref[at] = mm(dscore, q, 0, 0)
    fill_lag_masks(masks, mask_s, du_s)
    small_ref[...] = jnp.zeros(small_ref.shape, f32)
    for head in range(heads):
        cols = slice(head * LANES, (head + 1) * LANES)
        gq_ref[:, cols], halo_ref[:, cols], tap_grads = conv_back(
            taps_ref, joined, masks, mask_s, du_s, 0, head, head_width, rows, dq_s[:, cols]
        )
        for row, tap_grad in enumerate(tap_grads):
            small_ref[row : row + 1, cols] = tap_grad


def delta_back_kernel(
    last_bit, place, taps_ref, back_ref, facts_ref, steps_ref, keep_ref, do_ref, pre_ref, dk_ref,
    pack_ref, after_ref, other_ref,
    gp_ref, halo_ref, small_ref,
    joined, joined_ids, dk_s, du_s, mask_s,
):
    rows, head_width = do_ref.shape
    width = 2 * head_width
    heads = head_width // LANES
    chunks = rows // CHUNK
    fill_joined(back_ref, facts_ref, joined, joined_ids, head_width)
    masks = lag_masks(joined_ids, taps_ref.shape[1] - 1)
    row_ids, col_ids = tri_masks()
    flags = [chunk_flags(joined_ids, chunk) for chunk in range(chunks)]
    upper = bit_of(place, 0, last_bit)
    sets = [(head, chunk) for head in range(heads) for chunk in range(chunks)]
    at_of, kept_at = back_places(head_width)
    state_grads = {}
    for head in range(heads):
        at = slice(head * HEAD_DIM, (head + 1) * HEAD_DIM)
        after = after_ref[at, :].astype(f32)
        start = pack_ref.shape[0] - after_ref.shape[0] + head * HEAD_DIM
        suffix_m = pack_ref[start : start + HEAD_DIM, :]
        grad = chosen(upper, after, mm(suffix_m, other_ref[at, :]) + after)
        for chunk in range(chunks - 1, -1, -1):
            state_grads[head, chunk] = grad
            if chunk:
                low = grad.astype(bf16)
                grad = (
                    flags[chunk][3] * grad
                    - mm(steps_ref[at_of(head, chunk, 1)], low, 0, 0)
                    + mm(steps_ref[at_of(head, chunk)], do_ref[at_of(head, chunk)], 0, 0)
                )
    lane_ids = lax.broadcasted_iota(jnp.int32, (CHUNK, LANES), 1)
    gb_cols = [jnp.zeros((CHUNK, LANES), f32) for _ in range(chunks)]
    for head, chunk in sets:
        same, opened, closing, kept = flags[chunk]
        at = at_of(head, chunk)
        k, v, w_rows, u_rows, inverse = (
            back_ref[kept_at(head, chunk, part)] for part in (1, 2, 3, 4, 5)
        )
        kf, vf = k.astype(f32), v.astype(f32)
        beta = facts_ref[
            SUB + chunk * CHUNK : SUB + (chunk + 1) * CHUNK, head * LANES : (head + 1) * LANES
        ]
        state = keep_ref[at]
        sgrad = state_grads[head, chunk].astype(bf16)
        fresh = pre_ref[at]
        dfresh = pre_ref[at_of(head, chunk, 1)].astype(f32) + mm(closing * kf, sgrad)
        dw = -(opened * mm(dfresh, state, 1, 1))
        dx = mm(inverse, jnp.concatenate([dfresh, dw], axis=1), 0, 0)
        dxv, dxk = dx[:, :HEAD_DIM], dx[:, HEAD_DIM:]
        dlow = mm(dx, jnp.concatenate([u_rows, w_rows], axis=1), 1, 1)
        dlow = jnp.where(row_ids > col_ids, -dlow * same, 0.0)
        inner = mm(k, k, 1, 1)
        dbeta = jnp.sum(dxv * vf + dxk * kf + dlow * inner, axis=-1, keepdims=True)
        glow = (dlow * beta).astype(bf16)
        dk_s[at_of(head, chunk, 0)] = (
            beta * dxk
            + dk_ref[at]
            + closing * mm(fresh, sgrad, 1, 1)
            + mm(glow, k)
            + mm(glow, k, 0, 0)
        )
        dk_s[at_of(head, chunk, 1)] = beta * dxv
        raw = jnp.broadcast_to(dbeta, (CHUNK, LANES)) * beta * (1.0 - beta)
        gb_cols[chunk] = jnp.where(lane_ids == head, raw, gb_cols[chunk])
    bias_sum = jnp.zeros((1, LANES), f32)
    for chunk in range(chunks):
        gp_ref[chunk * CHUNK : (chunk + 1) * CHUNK, width:] = gb_cols[chunk]
        bias_sum = bias_sum + jnp.sum(gb_cols[chunk], axis=0, keepdims=True)
    small_ref[...] = jnp.zeros(small_ref.shape, f32)
    tap_count = len(masks)
    small_ref[2 * tap_count : 2 * tap_count + 1, 0:LANES] = bias_sum
    fill_lag_masks(masks, mask_s, du_s)
    for part in (1, 2):
        for head in range(heads):
            col = (part - 1) * head_width + head * LANES
            cols = slice(col, col + LANES)
            gp_ref[:, cols], halo_ref[:, cols], tap_grads = conv_back(
                taps_ref, joined, masks, mask_s, du_s, part, head, head_width, rows, dk_s[:, cols]
            )
            for tap, tap_grad in enumerate(tap_grads):
                row = (part - 1) * tap_count + tap
                small_ref[row : row + 1, head * LANES : (head + 1) * LANES] = tap_grad


def input_back_kernel(
    place, gp_ref, halo_ref, gq_ref, qhalo_ref, dgr_ref, wq_ref, wk_ref, wv_ref, wg_ref, wb_ref,
    x_ref, gain_ref, before_ref, sums_ref, whole, edge_ref, rows_ref,
):
    width = halo_ref.shape[1]
    head_width = width // 2
    zeros = jnp.zeros((SUB, head_width), f32)
    total = mm(dgr_ref[...], wg_ref[...], 1, 1) + mm(gp_ref[:, width : width + SUB], wb_ref[...])
    edge = None
    first, second = slice(0, head_width), slice(head_width, width)
    for grads, halo, w_ref in (
        (gq_ref[...], qhalo_ref[...], wq_ref),
        (gp_ref[:, first], halo_ref[:, first], wk_ref),
        (gp_ref[:, second], halo_ref[:, second], wv_ref),
    ):
        total = total + mm(grads, w_ref[...], 1, 1)
        piece = mm(jnp.concatenate([zeros, halo], axis=0), w_ref[...], 1, 1)
        edge = piece if edge is None else edge + piece
    whole[...] = total
    edge_ref[...] = edge[SUB:, :]
    x = x_ref[...].astype(f32)
    scale = lax.rsqrt(jnp.mean(x * x, axis=-1, keepdims=True) + 1e-06)
    hat_before = before_ref[...].astype(f32) / gain_ref[...]
    rows_ref[...] = jnp.zeros(rows_ref.shape, f32)
    rows_ref[0:1, :] = jnp.sum(total * (x * scale), axis=0, keepdims=True) + jnp.sum(
        edge * hat_before, axis=0, keepdims=True
    )
    rows_ref[1:2, :] = sums_ref[1:2, :]


def input_split_kernel(place, whole_ref, next_ref, keep_ref, send_ref, whole):
    rows = whole.shape[0]
    whole[...] = whole_ref[...]
    whole[rows - SUB :, :] = whole[rows - SUB :, :] + next_ref[...]
    split_rows(place, whole, keep_ref, send_ref)


def small_places(model, taps, heads, width):
    sizes = [model, LANES, model, 3 * taps * heads * LANES, heads * model, LANES]
    starts = [0]
    for size in sizes:
        starts.append(starts[-1] + size // LANES)
    across = width // LANES
    rows = -(-starts[-1] // across)
    return starts[:-1], -(-rows // (2 * SUB)) * 2 * SUB


def piece_at(index, width):
    across = width // LANES
    col = index % across * LANES
    return (slice(index // across, index // across + 1), slice(col, col + LANES))


def project_grads_kernel(
    bits, taps, place, a_ref, before_ref, gp_ref, halo_ref, sums_a, qsmall_ref, gsmall_ref, head_rows,
    keep_ref, send_ref, whole, small,
):
    a = a_ref[...]
    model = a.shape[1]
    width = whole.shape[1]
    heads = width // (2 * LANES)
    starts, _ = small_places(model, taps, heads, width)
    small[...] = jnp.zeros(small.shape, f32)
    beta_rows = mm(gp_ref[:, width:], a, 0, 0)
    pieces = model // LANES
    for piece in range(pieces):
        cols = slice(piece * LANES, (piece + 1) * LANES)
        small[piece_at(starts[0] + piece, width)] = head_rows[0:1, cols]
        small[piece_at(starts[2] + piece, width)] = sums_a[0:1, cols]
        for head in range(heads):
            small[piece_at(starts[4] + head * pieces + piece, width)] = beta_rows[head : head + 1, cols]
    for row in range(3 * taps):
        ref, at = (qsmall_ref, row) if row < taps else (gsmall_ref, row - taps)
        for head in range(heads):
            small[piece_at(starts[3] + row * heads + head, width)] = ref[
                at : at + 1, head * LANES : (head + 1) * LANES
            ]
    small[piece_at(starts[1], width)] = head_rows[1:2, 0:LANES]
    small[piece_at(starts[5], width)] = gsmall_ref[2 * taps : 2 * taps + 1, 0:LANES]
    edge = jnp.concatenate([jnp.zeros((SUB, width), f32), halo_ref[...]], axis=0)
    whole[...] = (mm(a, gp_ref[:, :width], 0, 0) + mm(before_ref[...], edge, 0, 0)).astype(bf16)
    emit_shares(place, bits, whole, keep_ref, send_ref)
    keep_ref[model // 2 :, :] = small[...].astype(bf16)
    send_ref[model // 2 :, :] = small[...].astype(bf16)


def share_small_kernel(place, keep_ref, got_ref, keep_out, send_out_ref):
    extra = 2 * keep_out.shape[0] - keep_ref.shape[0]
    half = keep_out.shape[0] - extra
    small = keep_ref[2 * half :, :] + got_ref[2 * half :, :]
    keep_out[0:half, :] = keep_ref[0:half, :] + got_ref[0:half, :]
    send_out_ref[0:half, :] = keep_ref[half : 2 * half, :] + got_ref[half : 2 * half, :]
    keep_out[half:, :] = small
    send_out_ref[half:, :] = small


def project_sum_kernel(
    taps, place, keep_ref, got_ref, k_ref, v_ref,
    norm_ref, hgain_ref, fgain_ref, taps_ref, beta_ref, bias_ref, small, rows_s,
):
    share, head_width = k_ref.shape
    width = 2 * head_width
    heads = head_width // LANES
    total = keep_ref[...].astype(f32) + got_ref[...].astype(f32)
    for index, out_ref in enumerate((k_ref, v_ref)):
        out_ref[...] = total[:share, index * head_width : (index + 1) * head_width]
    small[...] = total[share:, :]
    model = norm_ref.shape[1]
    starts, _ = small_places(model, taps, heads, width)
    pieces = model // LANES
    for piece in range(pieces):
        cols = slice(piece * LANES, (piece + 1) * LANES)
        norm_ref[0:1, cols] = small[piece_at(starts[0] + piece, width)]
        fgain_ref[0:1, cols] = small[piece_at(starts[2] + piece, width)]
        for head in range(heads):
            row = small[piece_at(starts[4] + head * pieces + piece, width)]
            rows_s[head * pieces + piece : head * pieces + piece + 1, :] = row
    hgain_ref[...] = small[piece_at(starts[1], width)]
    for part in range(3):
        for tap in range(taps):
            for head in range(heads):
                taps_ref[part, tap : tap + 1, head * LANES : (head + 1) * LANES] = small[
                    piece_at(starts[3] + (part * taps + tap) * heads + head, width)
                ]
    bias_ref[...] = small[piece_at(starts[5], width)][:, : bias_ref.shape[1]]
    if share % LANES:
        for head in range(heads):
            for piece in range(pieces):
                at = head * pieces + piece
                beta_ref[head : head + 1, piece * LANES : (piece + 1) * LANES] = rows_s[at : at + 1, :]
    else:
        for head in range(heads):
            for piece in range(share // LANES):
                at = head * pieces + place[0] * (share // LANES) + piece
                beta_ref[head : head + 1, piece * LANES : (piece + 1) * LANES] = rows_s[pl.ds(at, 1), :]


def input_grad_kernel(place, mine, theirs, x_ref, gain_ref, dh_ref, out_ref, whole):
    join_rows(place, mine[...].astype(f32), theirs[...].astype(f32), whole)
    x = x_ref[...].astype(f32)
    scale = lax.rsqrt(jnp.mean(x * x, axis=-1, keepdims=True) + 1e-06)
    hat = x * scale
    grad = whole[...] * gain_ref[...]
    inner = jnp.mean(grad * hat, axis=-1, keepdims=True)
    out_ref[...] = dh_ref[...] + scale * (grad - hat * inner)


def output_kernel(place, mine, theirs, h_ref, out_ref, whole):
    join_rows(place, mine[...].astype(f32), theirs[...].astype(f32), whole)
    out_ref[...] = (h_ref[...] + whole[...]).astype(bf16)


def add_kernel(place, left_ref, right_ref, out_ref):
    out_ref[...] = (left_ref[...].astype(f32) + right_ref[...].astype(f32)).astype(out_ref.dtype)


def added(chain, left, right):
    shape = left.value.shape if isinstance(left, Free) else left.shape
    (out,) = kernel_call(
        add_kernel, (shaped(shape, right.dtype),), chain, left, right, name="added"
    )
    return out


def gathered(value):
    count = lax.axis_size("head")
    blocks = [value]
    bit = 2
    while bit < count:
        blocks = blocks + [swap(block, "head", bit) for block in blocks]
        bit *= 2
    return blocks + [swap(block, "head", 1) for block in blocks]


class Shares:
    def __init__(self, keep, send, bits, axis=0):
        self.keep, self.bits, self.axis = keep, list(bits), axis
        self.got = swap(send, "seq", 1 << self.bits.pop(0))

    def step(self, chain):
        half = list(self.got.shape)
        half[self.axis] //= 2
        self.keep, send = kernel_call(
            functools.partial(share_round_kernel, self.axis),
            (shaped(half, bf16), shaped(half, bf16)),
            chain, self.keep, self.got, name="share_round",
        )
        self.got = swap(send, "seq", 1 << self.bits.pop(0))

    def until(self, chain, left):
        while len(self.bits) > left:
            self.step(chain)

    def pair(self, chain):
        self.until(chain, 0)
        return self.keep, self.got


def head_rounds(chain, value):
    count = lax.axis_size("head")
    bit = 1
    while bit < count:
        value = added(chain, value, swap(value, "head", bit))
        bit *= 2
    return value


def body(
    block_input, cotangent, segment_ids, norm_gain, w_query, w_key, w_value, w_gate, w_beta,
    beta_bias, conv_weight, head_gain, w_out, ffn_gain, w_ffn_gate, w_ffn_up, w_ffn_down,
):
    rows, model = block_input.shape
    heads = w_beta.shape[1]
    head_width = w_query.shape[1]
    ffn_width = w_ffn_gate.shape[1]
    taps = conv_weight.shape[1]
    seq_count = lax.axis_size("seq")
    rounds = seq_count.bit_length() - 1
    share = model // seq_count
    width = 3 * head_width
    chunks = rows // CHUNK
    y_first = list(range(rounds))
    y_last = y_first[1:] + y_first[:1]
    y_next = y_first[1:2] + y_first[:1] + y_first[2:]
    by_plan = {"first": y_first, "last": y_last, "next": y_next}
    down_bits, gate_bits, up_bits, early_bits, project_bits = (
        by_plan[PLANS[key]] for key in ("down", "gate", "up", "early", "project")
    )

    chain = Chain()

    def ffn_share(chain, pair):
        return kernel_call(
            functools.partial(ffn_share_kernel, ffn_axis),
            (final((ffn_width, share), f32),), chain, *pair, name="ffn_share",
        )

    bias_in = beta_bias[None] if heads > 1 else jnp.broadcast_to(beta_bias[None], (1, 2))
    gain_row, fgain_row, hgain_row = Free(norm_gain[None]), Free(ffn_gain[None]), Free(head_gain[None])
    taps_in = Free(conv_weight)

    square = (rows, head_width)
    p, beta, seg_cols, tail, a, gate_raw, w_beta8, w_out_copy = kernel_call(
        project_kernel,
        (
            shaped((rows, width), bf16),
            shaped(square, f32),
            shaped((rows, LANES), f32),
            shaped((SUB, width + LANES + model), f32),
            Direct((rows, model), bf16),
            Direct(square, f32),
            Direct((SUB, model), f32),
            Direct(w_out.shape, bf16),
        ),
        chain, Far(block_input), Far(w_query), Far(w_key), Far(w_value), Far(w_gate),
        Far(norm_gain[None]), Far(w_beta.T), Far(bias_in),
        Far(segment_ids.reshape(chunks, LANES)), Far(w_out),
        scratch=(
            pltpu.VMEM((rows, model), bf16),
            pltpu.VMEM((4, model, head_width), bf16),
            pltpu.VMEM((1, model), f32),
            pltpu.VMEM((heads, model), bf16),
            pltpu.VMEM(bias_in.shape, f32),
            pltpu.VMEM((chunks, LANES), jnp.int32),
            pltpu.VMEM((rows, model), bf16),
            pltpu.VMEM(square, f32),
            pltpu.VMEM((SUB, model), f32),
            pltpu.VMEM(w_out.shape, bf16),
            pltpu.SemaphoreType.DMA((10,)),
            pltpu.SemaphoreType.DMA((4,)),
        ),
        name="project",
    )
    halo = shift(tail, "seq", 1)
    joined = pltpu.VMEM((rows + SUB, width), f32)
    joined_ids = pltpu.VMEM((rows + SUB, LANES), f32)
    maps, mix, back, facts, a_before = kernel_call(
        delta_kernel,
        (
            shaped((2 * heads * HEAD_DIM, HEAD_DIM), bf16),
            shaped((rows + 2 * SUB, 4 * head_width), bf16),
            shaped((rows + 2 * SUB, 2 * width + 4 * head_width), bf16),
            shaped((rows + SUB, head_width + LANES), f32),
            shaped((2 * SUB, model), bf16),
        ),
        chain, p, halo, Held(conv_weight), seg_cols, beta,
        scratch=(joined, joined_ids),
        name="delta",
    )
    half_maps = heads * HEAD_DIM
    w_out_all = gathered(w_out_copy)
    prefix = pack = maps
    for bit in range(rounds - 1):
        other = swap(maps, "seq", 1 << bit)
        if bit == 0:
            back, facts, steps, a_before = park(
                chain, (back, None), (facts, None), (mix, 2 * head_width), (a_before, None), name="park_delta"
            )
        maps, prefix, pack = kernel_call(
            functools.partial(scan_round_kernel, bit),
            (
                shaped((half_maps if bit == rounds - 2 else 2 * half_maps, HEAD_DIM), bf16),
                shaped((2 * half_maps, HEAD_DIM), bf16),
                shaped((2 * half_maps * (bit + 1), HEAD_DIM), bf16),
            ),
            chain, maps, other, prefix, pack,
            name="scan_round",
            )
    other_a = swap(maps, "seq", 1 << (rounds - 1))
    y, mixed, keep_y = kernel_call(
        functools.partial(mixer_kernel, rounds - 1),
        (shaped(square, bf16), shaped(square, f32), shaped((rows, 2 * head_width), bf16)),
        chain, prefix, other_a, mix, Free(gate_raw), hgain_row,
        name="mixer",
    )
    mixed, keep_y, pack = park(
        chain, (mixed, None), (keep_y, None), (pack, None), name="park_mixer"
    )
    y_all = gathered(y)
    half = (rows // 2, model)
    wide = pltpu.VMEM((rows, model), f32)
    ffn_wide = -(-ffn_width // LANES) * LANES
    ffn_axis = 0 if share % LANES else 1
    ffn_whole = (ffn_width, model) if ffn_axis else (model, ffn_wide)
    ffn_half = (ffn_width, model // 2) if ffn_axis else (model // 2, ffn_wide)
    (
        db_send, down_send, gate_send, h, hidden, db_keep, down_keep, gate_keep, grad_up,
    ) = kernel_call(
        functools.partial(ffn_kernel, ffn_axis, down_bits, gate_bits),
        (
            shaped(half, bf16),
            shaped(ffn_half, bf16),
            shaped(ffn_half, bf16),
            Direct((rows, model), f32),
            Direct((rows, ffn_width), bf16),
            Direct(half, bf16),
            Direct(ffn_half, bf16),
            Direct(ffn_half, bf16),
            Direct(ffn_whole, bf16),
        ),
        chain, Free(block_input), Free(cotangent), fgain_row,
        Free(w_ffn_gate.T), Free(w_ffn_up.T), Free(w_ffn_down),
        *y_all, Free(w_out_all[0]), *w_out_all[1:],
        scratch=(
            wide,
            pltpu.VMEM((rows, ffn_width), bf16),
            pltpu.VMEM(half, bf16),
            pltpu.VMEM(ffn_half, bf16),
            pltpu.VMEM(ffn_half, bf16),
            pltpu.VMEM(ffn_whole, bf16),
            pltpu.VMEM(ffn_whole, bf16),
            wide,
            pltpu.SemaphoreType.DMA((6,)),
        ),
        name="ffn",
    )
    down = Shares(Held(down_keep), down_send, down_bits, ffn_axis)
    gate = Shares(Held(gate_keep), gate_send, gate_bits, ffn_axis)
    head_bits = [1 << bit for bit in range(1, lax.axis_size("head").bit_length() - 1)]
    pre = dk_part = gq = q_halo = q_small = q_share = None
    conv_scratch = (
        pltpu.VMEM((rows + 2 * SUB, LANES), f32),
        pltpu.VMEM((taps - 1, rows + 2 * SUB, LANES), f32),
    )
    step_bits = list(range(rounds - 1))
    rest_bits = list(project_bits[1:])
    _, small_extra = small_places(model, taps, heads, 2 * head_width)
    mine = out_keep = out_send = gh = pull = dh = d_out = d_gate_raw = sums_a = other = after = up = up_keep = up_send = out_mine = early = early_keep = early_send = gp = gp_halo = grad_small = da = da_edge = head_rows = from_next = keep = send = got = da_keep = da_send = block_output = input_grad = out_share = w_gate_share = down_share = ffn_gate_share = ffn_up_share = None

    def db_core():
        nonlocal mine
        mine = added(chain, Held(db_keep), swap(db_send, "head", 1))

    def out_part():
        nonlocal out_keep, out_send
        out_keep, out_send = kernel_call(
            out_part_kernel,
            (shaped(half, bf16), shaped(half, bf16)),
            chain, Held(hidden), Held(w_ffn_down),
            scratch=(wide,),
            name="out_part",
        )

    def db_far():
        nonlocal mine
        for bit in head_bits:
            mine = added(chain, mine, swap(mine, "head", bit))

    def residual_back():
        nonlocal gh, pull, dh, d_out, d_gate_raw, sums_a, other
        gh, pull, dh, d_out, d_gate_raw, sums_a = kernel_call(
            residual_back_kernel,
            (
                shaped((rows, model), bf16),
                shaped((half_maps, HEAD_DIM), bf16),
                shaped((rows, model), f32),
                shaped(square, bf16),
                shaped(square, bf16),
                shaped((SUB, model), f32),
            ),
            chain, mine, swap(mine, "head", 1), Free(h), Free(cotangent), fgain_row, Free(w_out), Free(mixed),
            Free(gate_raw), hgain_row, Free(steps),
            scratch=(wide,),
            name="residual_back",
        )
        other = swap(pull, "seq", 1)

    def park_back():
        nonlocal dh, d_out, d_gate_raw, sums_a
        dh, d_out, d_gate_raw, sums_a = park(
            chain, (dh, None), (d_out, None), (d_gate_raw, None), (sums_a, None), name="park_residual"
        )

    def down_one():
        down.step(chain)

    def gate_one():
        gate.step(chain)

    def scan_back():
        nonlocal pull, other, after

        bit = step_bits.pop(0)
        pull, after = kernel_call(
            functools.partial(back_round_kernel, bit),
            (shaped(pull.shape, bf16), shaped(pull.shape, bf16)),
            chain, Free(pack), pull, other, pull if after is None else after,
            name="back_round",
        )
        other = swap(pull, "seq", 2 << bit)

    def scan_rest():
        while step_bits:
            scan_back()

    def up_blocks():
        nonlocal up, up_keep, up_send
        up_keep, up_send = kernel_call(
            functools.partial(emit_kernel, ffn_axis, up_bits),
            (shaped(ffn_half, bf16), shaped(ffn_half, bf16)),
            chain, Held(grad_up),
            name="up_blocks",
        )
        up = Shares(up_keep, up_send, up_bits, ffn_axis)

    def out_core():
        nonlocal out_mine
        out_mine = added(chain, out_keep, swap(out_send, "head", 1))

    def delta_query():
        nonlocal pre, dk_part, gq, q_halo, q_small
        pre, dk_part, gq, q_halo, q_small = kernel_call(
            delta_query_kernel,
            (
                shaped((rows, 2 * head_width), bf16),
                shaped(square, f32),
                stored(square, f32),
                stored((SUB, head_width), f32),
                stored((-(-taps // SUB) * SUB, head_width), f32),
            ),
            chain, taps_in, Free(back), Free(facts), Free(keep_y), Free(d_out),
            scratch=(joined, joined_ids, pltpu.VMEM(square, f32)) + conv_scratch,
            name="delta_query",
        )

    def early_grads():
        nonlocal early
        early_keep, early_send = kernel_call(
            functools.partial(early_grads_kernel, early_bits),
            (shaped((model // 2, width), bf16), shaped((model // 2, width), bf16)),
            chain, gh, Free(keep_y), Free(a), Free(d_gate_raw), Held(gq), Held(q_halo), Held(a_before),
            scratch=(pltpu.VMEM((model, width), bf16),),
            name="early_grads",
        )
        early = Shares(early_keep, early_send, early_bits)

    def down_two():
        down.until(chain, 0)

    def gate_two():
        gate.until(chain, 0)

    def out_far():
        nonlocal out_mine
        for bit in head_bits:
            out_mine = added(chain, out_mine, swap(out_mine, "head", bit))

    def delta_back():
        nonlocal gp, gp_halo, grad_small
        gp, gp_halo, grad_small = kernel_call(
            functools.partial(delta_back_kernel, rounds - 1),
            (
                shaped((rows, 2 * head_width + LANES), f32),
                shaped((SUB, 2 * head_width), f32),
                stored((-(-(2 * taps + 1) // SUB) * SUB, head_width), f32),
            ),
            chain, taps_in, Free(back), Free(facts), Free(steps), Free(keep_y), Free(d_out),
            pre, dk_part, Free(pack), after, other,
            scratch=(joined, joined_ids, pltpu.VMEM((rows, 2 * head_width), f32)) + conv_scratch,
            name="delta_back",
        )

    def input_back():
        nonlocal da, da_edge, head_rows, from_next
        da, da_edge, head_rows = kernel_call(
            input_back_kernel,
            (shaped((rows, model), f32), shaped((SUB, model), f32), shaped((SUB, model), f32)),
            chain, gp, gp_halo, Held(gq), Held(q_halo), Free(d_gate_raw),
            Free(w_query), Free(w_key), Free(w_value), Free(w_gate), Free(w_beta8), Free(block_input),
            gain_row, Free(a_before), Free(sums_a),
            name="input_back",
        )
        from_next = shift(da_edge, "seq", -1)

    def up_one():
        up.step(chain)

    def rows_core():
        nonlocal head_rows
        head_rows = added(chain, head_rows, swap(head_rows, "head", 1))

    def rows_far():
        nonlocal head_rows
        for bit in head_bits:
            head_rows = added(chain, head_rows, swap(head_rows, "head", bit))

    def project_grads():
        nonlocal keep, send, got
        keep, send = kernel_call(
            functools.partial(project_grads_kernel, project_bits, taps),
            (
                shaped((model // 2 + small_extra, 2 * head_width), bf16),
                shaped((model // 2 + small_extra, 2 * head_width), bf16),
            ),
            chain, Free(a), Free(a_before), gp, gp_halo, Free(sums_a), Held(q_small), Free(grad_small), head_rows,
            scratch=(pltpu.VMEM((model, 2 * head_width), bf16), pltpu.VMEM((small_extra, 2 * head_width), f32)),
            name="project_grads",
        )
        got = swap(send, "seq", 1 << project_bits[0])

    def input_split():
        nonlocal da_keep, da_send
        da_keep, da_send = kernel_call(
            input_split_kernel,
            (shaped(half, bf16), shaped(half, bf16)),
            chain, da, from_next,
            scratch=(wide,),
            name="input_split",
        )

    def early_one():
        early.step(chain)

    def up_two():
        up.until(chain, 0)

    def da_core():
        nonlocal mine
        mine = added(chain, da_keep, swap(da_send, "head", 1))

    def da_far():
        nonlocal mine
        for bit in head_bits:
            mine = added(chain, mine, swap(mine, "head", bit))

    def output():
        nonlocal block_output
        (block_output,) = kernel_call(
            output_kernel,
            (final((rows, model), bf16),),
            chain, out_mine, swap(out_mine, "head", 1), Free(h),
            scratch=(wide,),
            name="output",
        )

    def input_grad():
        nonlocal input_grad
        (input_grad,) = kernel_call(
            input_grad_kernel,
            (final((rows, model), f32),),
            chain, mine, swap(mine, "head", 1), Free(block_input), gain_row, Free(dh),
            scratch=(wide,),
            name="input_grad",
        )

    def share_one():
        nonlocal keep, send, got

        shape = ((keep.shape[0] - small_extra) // 2 + small_extra, 2 * head_width)
        keep, send = kernel_call(
            share_small_kernel,
            (shaped(shape, bf16), shaped(shape, bf16)),
            chain, keep, got,
            name="share_small",
        )
        got = swap(send, "seq", 1 << rest_bits.pop(0))

    def share_two():
        while rest_bits:
            share_one()

    def early_two():
        early.until(chain, 0)

    def down_out():
        nonlocal down_share
        (down_share,) = ffn_share(chain, down.pair(chain))

    def up_out():
        nonlocal ffn_up_share
        (ffn_up_share,) = ffn_share(chain, up.pair(chain))

    def gate_out():
        nonlocal ffn_gate_share
        (ffn_gate_share,) = ffn_share(chain, gate.pair(chain))

    def early_out():
        nonlocal out_share, w_gate_share, q_share
        out_share, w_gate_share, q_share = kernel_call(
            early_sum_kernel,
            (
                final((head_width, share), f32),
                final((share, head_width), f32),
                final((share, head_width), f32),
            ),
            chain, *early.pair(chain), name="early_sum",
        )

    parts = (
        db_core,
        out_part,
        db_far,
        residual_back,
        park_back,
        down_one,
        gate_one,
        scan_back,
        up_blocks,
        out_core,
        scan_rest,
        delta_query,
        early_grads,
        down_two,
        gate_two,
        out_far,
        delta_back,
        input_back,
        up_one,
        rows_core,
        input_split,
        rows_far,
        project_grads,
        up_two,
        early_one,
        da_core,
        output,
        down_out,
        share_one,
        early_two,
        up_out,
        da_far,
        input_grad,
        share_two,
        early_out,
        gate_out,
    )
    by_name = {part.__name__: part for part in parts}
    for name in ORDER:
        by_name[name]()
    beta_shape = (heads, model if share % LANES else share)
    (
        k_share, v_share, norm_total, head_gain_total, ffn_gain_total, conv_total, beta_rows,
        bias_total,
    ) = kernel_call(
        functools.partial(project_sum_kernel, taps),
        tuple(final((share, head_width), f32) for _ in range(2))
        + (
            final((1, model), f32),
            final((1, LANES), f32),
            final((1, model), f32),
            final(conv_weight.shape, f32),
            final(beta_shape, f32),
            final((1, heads), f32),
        ),
        chain, keep, got,
        scratch=(
            pltpu.VMEM((small_extra, 2 * head_width), f32),
            pltpu.VMEM((-(-heads * model // LANES // SUB) * SUB, LANES), f32),
        ),
        name="project_sum",
    )
    if share % LANES:
        beta_rows = lax.dynamic_slice(beta_rows, (0, lax.axis_index("seq") * share), (heads, share))
    beta_share = beta_rows.T
    return (
        block_output,
        input_grad,
        norm_total[0],
        q_share,
        k_share,
        v_share,
        w_gate_share,
        beta_share,
        bias_total[0],
        conv_total,
        head_gain_total[0],
        out_share,
        ffn_gain_total[0],
        ffn_gate_share.T,
        ffn_up_share.T,
        down_share,
    )


def solution(mesh):
    return jax.shard_map(
        body,
        mesh=mesh,
        in_specs=(
            P("seq", None), P("seq", None), P("seq"), P(),
            P(None, "head"), P(None, "head"), P(None, "head"), P(None, "head"), P(None, "head"),
            P("head"), P(None, None, "head"), P(), P("head", None), P(),
            P(None, "head"), P(None, "head"), P("head", None),
        ),
        out_specs=(
            P("seq", None), P("seq", None), P(),
            P("seq", "head"), P("seq", "head"), P("seq", "head"), P("seq", "head"), P("seq", "head"),
            P("head"), P(None, None, "head"), P(), P("head", "seq"), P(),
            P("seq", "head"), P("seq", "head"), P("head", "seq"),
        ),
        check_vma=False,
    )
```

```python
import functools
import math

import jax
import jax.numpy as jnp
from jax import lax
from jax.experimental import pallas as pl
from jax.experimental.pallas import tpu as pltpu
from jax.sharding import PartitionSpec as P

HEAD_DIM = 128
CHUNK = 128
LANES = 128
SUB = 8
Q_SCALE = HEAD_DIM ** (-0.5)
VMEM_SLACK = 14 * 1024 * 1024

ORDER = (
    "db_core",
    "db_far",
    "residual_back",
    "out_part",
    "gate_one",
    "down_one",
    "park_back",
    "scan_back",
    "up_blocks",
    "down_two",
    "out_core",
    "scan_rest",
    "delta_query",
    "early_grads",
    "gate_two",
    "delta_back",
    "input_back",
    "rows_core",
    "input_split",
    "out_far",
    "up_one",
    "rows_far",
    "project_grads",
    "up_two",
    "early_one",
    "da_core",
    "output",
    "down_out",
    "share_one",
    "early_two",
    "up_out",
    "da_far",
    "share_two",
    "gate_out",
    "early_out",
    "input_grad",
)
PLANS = {"down": "first", "gate": "last", "up": "first", "early": "first", "project": "first"}

bf16 = jnp.bfloat16
f32 = jnp.float32


def mm(left, right, left_dim=1, right_dim=0):
    return lax.dot_general(
        left.astype(bf16),
        right.astype(bf16),
        (((left_dim,), (right_dim,)), ((), ())),
        preferred_element_type=f32,
    )


def sigmoid(value):
    return 1.0 / (1.0 + jnp.exp(-value))


class Free:
    def __init__(self, value):
        self.value = value


class Held(Free):
    pass


class Far(Free):
    pass


class Place:
    def __getitem__(self, which):
        return lax.axis_index(("seq", "head")[which])


class Direct:
    def __init__(self, shape, dtype):
        self.shape, self.dtype = tuple(shape), dtype


class Chain:
    def __init__(self):
        self.token = None


def kernel_call(body, out_shapes, chain, *args, scratch=(), name, deps=()):
    vmem = pl.BlockSpec(memory_space=pltpu.VMEM)
    anywhere = pl.BlockSpec(memory_space=pl.ANY)
    size_of = lambda a: math.prod(a.shape) * jnp.dtype(a.dtype).itemsize
    held = sum(size_of(s) for s in scratch if hasattr(s, "dtype") and not is_semaphore(s))
    operands, specs = [], []
    for arg in args:
        if isinstance(arg, Free):
            value = arg.value
            if not type(arg) is Free:
                value = pltpu.with_memory_space_constraint(value, pltpu.HBM)
            operands.append(value)
            specs.append(anywhere if isinstance(arg, Far) else vmem)
            if not isinstance(arg, Far):
                held += size_of(value)
        else:
            operands.append(pltpu.with_memory_space_constraint(arg, pltpu.VMEM))
            specs.append(vmem)
    ins, outs = len(args), len(out_shapes)
    waits = (0 if chain.token is None else 1) + len(deps)
    operands += list(deps)
    specs += [anywhere] * len(deps)
    if chain.token is not None:
        operands.append(pltpu.with_memory_space_constraint(chain.token, pltpu.VMEM))
        specs.append(vmem)
    results, result_specs = [], []
    for out in out_shapes:
        if isinstance(out, Direct):
            results.append(pltpu.HBM(out.shape, out.dtype))
            result_specs.append(anywhere)
        else:
            results.append(out)
            result_specs.append(vmem)
            if isinstance(out, jax.ShapeDtypeStruct) or out.memory_space == pltpu.HBM:
                held += size_of(out)
    results.append(shaped((SUB, LANES), f32))
    result_specs.append(vmem)
    here = Place()

    def run(*refs):
        refs[ins + waits + outs][...] = jnp.zeros((SUB, LANES), f32)
        body(here, *refs[:ins], *refs[ins + waits : ins + waits + outs], *refs[ins + waits + outs + 1 :])

    *values, chain.token = pl.pallas_call(
        run,
        out_shape=tuple(results),
        in_specs=specs,
        out_specs=tuple(result_specs),
        scratch_shapes=list(scratch),
        compiler_params=pltpu.CompilerParams(vmem_limit_bytes=int(held) + VMEM_SLACK),
        cost_estimate=pl.CostEstimate(flops=0, bytes_accessed=0, transcendentals=0),
        name=name,
    )(*operands)
    return values


def stored(shape, dtype):
    return pltpu.HBM(tuple(shape), dtype)


def send_out(source, target, sems, index):
    copy = pltpu.make_async_copy(source, target, sems.at[index])
    copy.start()
    return copy


def is_semaphore(scratch):
    return not (
        jnp.issubdtype(scratch.dtype, jnp.floating) or jnp.issubdtype(scratch.dtype, jnp.integer)
    )


def final(shape, dtype):
    return jax.ShapeDtypeStruct(tuple(shape), dtype)


def shaped(shape, dtype):
    return pltpu.VMEM(tuple(shape), dtype)


def swap(value, axis, bit):
    count = lax.axis_size(axis)
    return lax.ppermute(value, axis, [(s, s ^ bit) for s in range(count)])


def shift(value, axis, step):
    count = lax.axis_size(axis)
    return lax.ppermute(
        value, axis, [(s, s + step) for s in range(count) if 0 <= s + step < count]
    )


def bit_of(place_ref, which, bit):
    return lax.rem(lax.shift_right_logical(place_ref[which], bit), 2)


def chosen(flag, when_one, when_zero):
    return jnp.where(flag == 1, when_one, when_zero)


def tri_masks():
    rows = lax.broadcasted_iota(jnp.int32, (CHUNK, CHUNK), 0)
    cols = lax.broadcasted_iota(jnp.int32, (CHUNK, CHUNK), 1)
    return rows, cols


def unit_inverses(lowers):
    rows, cols = tri_masks()
    eye = jnp.where(rows == cols, 1.0, 0.0).astype(f32)
    width = 1
    inverses = None
    while width < CHUNK:
        shift_bits = width.bit_length() - 1
        row_block = lax.shift_right_logical(rows, shift_bits)
        col_block = lax.shift_right_logical(cols, shift_bits)
        within = (
            lax.shift_right_logical(row_block, 1) == lax.shift_right_logical(col_block, 1)
        ) & (row_block != col_block)
        couplings = [jnp.where(within, low, 0.0) for low in lowers]
        if inverses is None:
            inverses = [eye - coupling for coupling in couplings]
        else:
            halves = [mm(inv, coupling) for inv, coupling in zip(inverses, couplings)]
            inverses = [inv - mm(half, inv) for inv, half in zip(inverses, halves)]
        width *= 2
    return inverses


def project_kernel(
    place, x_hbm, wq_hbm, wk_hbm, wv_hbm, wg_hbm, gain_hbm, wb_hbm, bias_hbm, seg_hbm, wo_hbm,
    p_ref, beta_ref, segc_ref, tail_ref, a_hbm, gate_hbm, wb8_hbm, wo_out,
    x_s, weights, gain_s, wb_s, bias_s, seg_s, a_s, gate_s, wb8_s, wo_s, arrived, left,
):
    rows = x_s.shape[0]
    head_width = wq_hbm.shape[1]
    heads = head_width // LANES
    pairs = ((x_hbm, x_s), (gain_hbm, gain_s), (seg_hbm, seg_s), (wb_hbm, wb_s), (bias_hbm, bias_s))
    pairs += ((wo_hbm, wo_s),)
    pairs += tuple(
        (source, weights.at[index]) for index, source in enumerate((wg_hbm, wq_hbm, wk_hbm, wv_hbm))
    )
    copies = [send_out(source, target, arrived, index) for index, (source, target) in enumerate(pairs)]
    for copy in copies[:5]:
        copy.wait()
    wo_copy, *copies = copies[5:]
    segr = seg_s[...].astype(f32)
    wb8_s[...] = jnp.zeros(wb8_s.shape, f32)
    wb8_s[0:heads, :] = wb_s[...].astype(f32)
    leaving = [send_out(wb8_s, wb8_hbm, left, 2)]
    x = x_s[...].astype(f32)
    scale = lax.rsqrt(jnp.mean(x * x, axis=-1, keepdims=True) + 1e-06)
    a = (x * scale * gain_s[...]).astype(bf16)
    a_s[...] = a
    tail_ref[:, 3 * head_width + LANES :] = a.astype(f32)[rows - SUB :, :]
    leaving.append(send_out(a_s, a_hbm, left, 0))
    logits = mm(a, wb8_s[...], 1, 1)
    for head in range(heads):
        column = logits[:, head : head + 1] + bias_s[:, head : head + 1]
        beta_ref[:, head * LANES : (head + 1) * LANES] = sigmoid(
            jnp.broadcast_to(column, (rows, LANES))
        )
    for chunk in range(rows // CHUNK):
        ids = jnp.broadcast_to(segr[chunk : chunk + 1, :], (CHUNK, LANES))
        turned = ids.T
        segc_ref[chunk * CHUNK : (chunk + 1) * CHUNK, :] = turned
        if chunk == rows // CHUNK - 1:
            tail_ref[:, 3 * head_width : 3 * head_width + LANES] = turned[CHUNK - SUB :, :]
    wo_copy.wait()
    leaving.append(send_out(wo_s, wo_out, left, 3))
    copies[0].wait()
    gate_s[...] = mm(a, weights[0])
    leaving.append(send_out(gate_s, gate_hbm, left, 1))
    for part in range(3):
        copies[part + 1].wait()
        value = mm(a, weights[part + 1])
        cols = slice(part * head_width, (part + 1) * head_width)
        low = value.astype(bf16)
        p_ref[:, cols] = low
        tail_ref[:, cols] = low.astype(f32)[rows - SUB :, :]
    for copy in leaving:
        copy.wait()


def lag_masks(joined_ids, lags):
    rows = joined_ids.shape[0] - SUB
    ids = joined_ids[SUB : SUB + rows, :]
    return [None] + [
        jnp.where(joined_ids[SUB - lag : SUB - lag + rows, :] == ids, 1.0, 0.0)
        for lag in range(1, lags + 1)
    ]


def conv_sum(joined, taps_ref, masks, part, head, head_width, rows):
    lags = taps_ref.shape[1] - 1
    col = part * head_width + head * LANES
    tap_cols = slice(head * LANES, (head + 1) * LANES)
    total = taps_ref[part, lags : lags + 1, tap_cols] * joined[SUB : SUB + rows, col : col + LANES]
    for lag in range(1, lags + 1):
        tap = taps_ref[part, lags - lag : lags - lag + 1, tap_cols]
        total = total + tap * joined[SUB - lag : SUB - lag + rows, col : col + LANES] * masks[lag]
    return total


def chunk_flags(joined_ids, chunk):
    start = chunk * CHUNK
    ids = joined_ids[SUB + start : SUB + start + CHUNK, :]
    same = jnp.where(ids == ids.T, 1.0, 0.0)
    before = joined_ids[SUB + start - 1 : SUB + start, :]
    final_id = joined_ids[SUB + start + CHUNK - 1 : SUB + start + CHUNK, :]
    opened = jnp.where(ids == before, 1.0, 0.0)
    closing = jnp.where(ids == final_id, 1.0, 0.0)
    kept = jnp.where(final_id == before, 1.0, 0.0)
    return same, opened, closing, kept


def delta_kernel(
    place, p_ref, tail_ref, taps_ref, segc_ref, beta_ref,
    maps_ref, mix_ref, back_ref, facts_ref, before_ref,
    joined, joined_ids,
):
    rows, width = p_ref.shape
    head_width = width // 3
    heads = head_width // LANES
    chunks = rows // CHUNK
    first = 2 * SUB
    joined[0:SUB, :] = tail_ref[:, :width]
    joined[SUB : SUB + rows, :] = p_ref[...].astype(f32)
    joined_ids[0:SUB, :] = tail_ref[:, width : width + LANES]
    joined_ids[SUB : SUB + rows, :] = segc_ref[...]
    facts_ref[SUB:, 0:head_width] = beta_ref[...]
    facts_ref[0:SUB, 0:head_width] = jnp.zeros((SUB, head_width), f32)
    facts_ref[:, head_width:] = joined_ids[...]
    before_ref[...] = jnp.concatenate(
        [jnp.zeros((SUB, before_ref.shape[1]), f32), tail_ref[:, width + LANES :]], axis=0
    ).astype(bf16)
    back_ref[first:, 0:width] = p_ref[...]
    back_ref[0:first, 0:width] = jnp.concatenate(
        [jnp.zeros((SUB, width), f32), tail_ref[:, :width]], axis=0
    ).astype(bf16)
    back_ref[0:first, width:] = jnp.zeros((first, back_ref.shape[1] - width), bf16)
    masks = lag_masks(joined_ids, taps_ref.shape[1] - 1)
    for part in range(3):
        for head in range(heads):
            total = conv_sum(joined, taps_ref, masks, part, head, head_width, rows)
            z = total * sigmoid(total)
            if part < 2:
                z = z * lax.rsqrt(jnp.sum(z * z, axis=-1, keepdims=True) + 1e-06)
                if part == 0:
                    z = z * Q_SCALE
            col = width + part * head_width + head * LANES
            back_ref[first:, col : col + LANES] = z.astype(bf16)
    row_ids, col_ids = tri_masks()
    flags = [chunk_flags(joined_ids, chunk) for chunk in range(chunks)]
    mix_ref[rows:, :] = jnp.concatenate(
        [jnp.concatenate([flags[min(row, chunks - 1)][3]] * (4 * heads), axis=1) for row in range(2 * SUB)],
        axis=0,
    ).astype(bf16)
    sets = [(head, chunk) for head in range(heads) for chunk in range(chunks)]

    def at_of(head, chunk, part=0):
        col = part * head_width + head * LANES
        return (slice(chunk * CHUNK, (chunk + 1) * CHUNK), slice(col, col + LANES))

    def kept_at(head, chunk, part):
        col = (3 + part) * head_width + head * LANES
        return (slice(first + chunk * CHUNK, first + (chunk + 1) * CHUNK), slice(col, col + LANES))

    lowers = []
    for head, chunk in sets:
        same = flags[chunk][0]
        q, k = back_ref[kept_at(head, chunk, 0)], back_ref[kept_at(head, chunk, 1)]
        inner = mm(jnp.concatenate([q, k], axis=0), k, 1, 1)
        scores = jnp.where(row_ids >= col_ids, inner[:CHUNK] * same, 0.0)
        back_ref[kept_at(head, chunk, 6)] = scores.astype(bf16)
        lowers.append(
            jnp.where(row_ids > col_ids, inner[CHUNK:] * same * beta_ref[at_of(head, chunk)], 0.0)
        )
    inverses = unit_inverses(lowers)
    eye = jnp.where(row_ids == col_ids, 1.0, 0.0).astype(f32)
    maps = [
        jnp.concatenate([eye, jnp.zeros((HEAD_DIM, HEAD_DIM), f32)], axis=1) for _ in range(heads)
    ]
    products = []
    for (head, chunk), inverse in zip(sets, inverses):
        beta = beta_ref[at_of(head, chunk)]
        k = back_ref[kept_at(head, chunk, 1)].astype(f32)
        v = back_ref[kept_at(head, chunk, 2)].astype(f32)
        both = jnp.concatenate([beta * k, beta * v], axis=1)
        products.append(mm(inverse, both))
    steps = {}
    for (head, chunk), inverse, product in zip(sets, inverses, products):
        same, opened, closing, kept = flags[chunk]
        w_rows, u_rows = product[:, :HEAD_DIM], product[:, HEAD_DIM:]
        back_ref[kept_at(head, chunk, 3)] = w_rows.astype(bf16)
        back_ref[kept_at(head, chunk, 4)] = u_rows.astype(bf16)
        back_ref[kept_at(head, chunk, 5)] = inverse.astype(bf16)
        both = jnp.concatenate([opened * w_rows, u_rows], axis=1)
        k = back_ref[kept_at(head, chunk, 1)].astype(f32)
        q = back_ref[kept_at(head, chunk, 0)].astype(f32)
        step = mm(closing * k, both, 0, 0)
        through = mm(back_ref[kept_at(head, chunk, 6)], both)
        mix_ref[at_of(head, chunk, 0)] = (opened * q - through[:, :HEAD_DIM]).astype(bf16)
        mix_ref[at_of(head, chunk, 1)] = step[:, :HEAD_DIM].astype(bf16)
        mix_ref[at_of(head, chunk, 2)] = through[:, HEAD_DIM:].astype(bf16)
        mix_ref[at_of(head, chunk, 3)] = step[:, HEAD_DIM:].astype(bf16)
        steps[head, chunk] = step
    for chunk in range(chunks):
        kept = flags[chunk][3]
        kept_wide = jnp.concatenate([kept, kept], axis=1)
        for head in range(heads):
            step = steps[head, chunk]
            pushed = kept_wide * maps[head] - mm(step[:, :HEAD_DIM], maps[head])
            maps[head] = jnp.concatenate(
                [pushed[:, :HEAD_DIM], pushed[:, HEAD_DIM:] + step[:, HEAD_DIM:]], axis=1
            )
    for head in range(heads):
        maps_ref[head * HEAD_DIM : (head + 1) * HEAD_DIM, :] = maps[head][:, :HEAD_DIM].astype(bf16)
        base = (heads + head) * HEAD_DIM
        maps_ref[base : base + HEAD_DIM, :] = maps[head][:, HEAD_DIM:].astype(bf16)


def park_kernel(count, place, *refs):
    sources, targets, left = refs[:count], refs[count : 2 * count], refs[-1]
    copies = []
    for index, (source, target) in enumerate(zip(sources, targets)):
        if source.shape != target.shape:
            source = source.at[:, 0 : target.shape[1]]
        copies.append(send_out(source, target, left, index))
    for copy in copies:
        copy.wait()


def park(chain, *pairs, name):
    arrays = [value.value if isinstance(value, Free) else value for value, _ in pairs]
    return kernel_call(
        functools.partial(park_kernel, len(pairs)),
        [
            Direct((array.shape[0], array.shape[1] if cols is None else cols), array.dtype)
            for array, (_, cols) in zip(arrays, pairs)
        ],
        chain,
        *[value for value, _ in pairs],
        scratch=(pltpu.SemaphoreType.DMA((len(pairs),)),),
        name=name,
    )


def scan_round_kernel(bit, place, own_ref, other_ref, prefix_ref, pack_ref, total_ref, prefix_out, pack_out):
    upper = bit_of(place, 0, bit)
    half = own_ref.shape[0] // 2
    heads = half // HEAD_DIM
    base = 2 * half * bit
    if bit:
        pack_out[0:base, :] = pack_ref[...]
    for head in range(heads):
        m_at = slice(head * HEAD_DIM, (head + 1) * HEAD_DIM)
        a_at = slice((heads + head) * HEAD_DIM, (heads + head + 1) * HEAD_DIM)
        low_at = slice(base + head * HEAD_DIM, base + (head + 1) * HEAD_DIM)
        suffix_at = slice(base + half + head * HEAD_DIM, base + half + (head + 1) * HEAD_DIM)
        own_m, own_a = own_ref[m_at, :].astype(f32), own_ref[a_at, :].astype(f32)
        other_m, other_a = other_ref[m_at, :].astype(f32), other_ref[a_at, :].astype(f32)
        high_m, high_a = chosen(upper, own_m, other_m), chosen(upper, own_a, other_a)
        low_m, low_a = chosen(upper, other_m, own_m), chosen(upper, other_a, own_a)
        pack_out[low_at, :] = low_m.astype(bf16)
        total = mm(high_m, jnp.concatenate([low_m, low_a], axis=1))
        added_part = (total[:, HEAD_DIM:] + high_a).astype(bf16)
        if total_ref.shape[0] == own_ref.shape[0]:
            total_ref[m_at, :] = total[:, :HEAD_DIM].astype(bf16)
            total_ref[a_at, :] = added_part
        else:
            total_ref[m_at, :] = added_part
        if bit == 0:
            rows, cols = tri_masks()
            eye = jnp.where(rows == cols, 1.0, 0.0).astype(f32)
            prefix_out[m_at, :] = chosen(upper, other_m, eye).astype(bf16)
            prefix_out[a_at, :] = chosen(upper, other_a, jnp.zeros_like(other_a)).astype(bf16)
            pack_out[suffix_at, :] = chosen(upper, eye, other_m.T).astype(bf16)
        else:
            before_m, before_a = prefix_ref[m_at, :].astype(f32), prefix_ref[a_at, :].astype(f32)
            at = base - half + head * HEAD_DIM
            after_m = pack_ref[at : at + HEAD_DIM, :].astype(f32)
            joint = mm(before_m, jnp.concatenate([other_m, other_a], axis=1))
            prefix_out[m_at, :] = chosen(upper, joint[:, :HEAD_DIM], before_m).astype(bf16)
            prefix_out[a_at, :] = chosen(
                upper, joint[:, HEAD_DIM:] + before_a, before_a
            ).astype(bf16)
            pack_out[suffix_at, :] = chosen(upper, after_m, mm(after_m, other_m, 1, 1)).astype(bf16)


def back_round_kernel(bit, place, pack_ref, own_ref, other_ref, after_ref, total_ref, after_out):
    upper = bit_of(place, 0, bit)
    half = own_ref.shape[0]
    base = 2 * half * bit
    for head in range(half // HEAD_DIM):
        at = slice(head * HEAD_DIM, (head + 1) * HEAD_DIM)
        own, other = own_ref[at, :].astype(f32), other_ref[at, :].astype(f32)
        high, low = chosen(upper, own, other), chosen(upper, other, own)
        low_m = pack_ref[base + head * HEAD_DIM : base + (head + 1) * HEAD_DIM, :]
        total_ref[at, :] = (mm(low_m, high, 0, 0) + low).astype(bf16)
        if bit == 0:
            after_out[at, :] = chosen(upper, jnp.zeros_like(other), other).astype(bf16)
        else:
            start = base - half + head * HEAD_DIM
            suffix_m = pack_ref[start : start + HEAD_DIM, :]
            after = after_ref[at, :].astype(f32)
            after_out[at, :] = chosen(upper, after, mm(suffix_m, other) + after).astype(bf16)


def mixer_kernel(
    last_bit, place, prefix_ref, other_a_ref, mix_ref, gate_ref, hgain_ref,
    y_ref, o_ref, keep_ref,
):
    rows, head_width = gate_ref.shape
    heads = head_width // LANES
    upper = bit_of(place, 0, last_bit)
    kept_rows = mix_ref[rows:, 0:LANES].astype(f32)
    for head in range(heads):
        m_at = slice(head * HEAD_DIM, (head + 1) * HEAD_DIM)
        a_at = slice((heads + head) * HEAD_DIM, (heads + head + 1) * HEAD_DIM)
        before_m, before_a = prefix_ref[m_at, :], prefix_ref[a_at, :].astype(f32)
        state = chosen(upper, mm(before_m, other_a_ref[m_at, :]) + before_a, before_a)
        for chunk in range(rows // CHUNK):
            chunk_rows = slice(chunk * CHUNK, (chunk + 1) * CHUNK)
            cols = [
                slice(part * head_width + head * LANES, part * head_width + (head + 1) * LANES)
                for part in range(4)
            ]
            at = (chunk_rows, cols[0])
            low = state.astype(bf16)
            keep_ref[at] = low
            out = mm(mix_ref[at], low) + mix_ref[chunk_rows, cols[2]].astype(f32)
            o_ref[at] = out
            state = (
                kept_rows[chunk : chunk + 1, :] * state
                - mm(mix_ref[chunk_rows, cols[1]], low)
                + mix_ref[chunk_rows, cols[3]].astype(f32)
            )
            gate = gate_ref[at]
            scale = lax.rsqrt(jnp.mean(out * out, axis=-1, keepdims=True) + 1e-05)
            y = (out * scale * hgain_ref[...] * (gate * sigmoid(gate))).astype(bf16)
            y_ref[at] = y
            keep_ref[chunk_rows, cols[1]] = y


def ffn_kernel(
    axis, down_bits, gate_bits, place, x_ref, g_ref, fgain_ref, wg_ref, wu_ref, wd_ref, *rest,
):
    (
        *parts, send_ref, down_send, gate_send, h_hbm, hid_hbm, keep_hbm, down_hbm, gate_hbm, up_hbm,
        h_s, hid_s, keep_s, down_keep, gate_keep, grad_s, up_s, whole, left,
    ) = rest
    y_refs, wo_refs = parts[: len(parts) // 2], parts[len(parts) // 2 :]
    att = None
    for y_ref, wo_ref in zip(y_refs, wo_refs):
        part = mm(y_ref[...], wo_ref[...])
        att = part if att is None else att + part
    h = x_ref[...].astype(f32) + att
    h_s[...] = h
    leaving = [send_out(h_s, h_hbm, left, 0)]
    scale = lax.rsqrt(jnp.mean(h * h, axis=-1, keepdims=True) + 1e-06)
    b = (h * scale * fgain_ref[...]).astype(bf16)
    gate = mm(b, wg_ref[...], 1, 1)
    up = mm(b, wu_ref[...], 1, 1)
    sg = sigmoid(gate)
    act = gate * sg
    hid = (act * up).astype(bf16)
    hid_s[...] = hid
    leaving.append(send_out(hid_s, hid_hbm, left, 2))
    dhid = mm(g_ref[...], wd_ref[...], 1, 1)
    dgate = (dhid * up * (sg * (1.0 + gate * (1.0 - sg)))).astype(bf16)
    dup = (dhid * act).astype(bf16)

    def grad_of(by_units, by_model, out):
        if axis:
            out[...] = mm(by_units, by_model, 0, 0).astype(bf16)
            return
        units = by_units.shape[1]
        if out.shape[1] > units:
            out[:, units:] = jnp.zeros((out.shape[0], out.shape[1] - units), bf16)
        out[:, :units] = mm(by_model, by_units, 0, 0).astype(bf16)

    grad_of(hid, g_ref[...], grad_s)
    emit_shares(place, down_bits, grad_s, down_keep, down_send, axis)
    leaving.append(send_out(down_keep, down_hbm, left, 1))
    grad_of(dgate, b, grad_s)
    emit_shares(place, gate_bits, grad_s, gate_keep, gate_send, axis)
    leaving.append(send_out(gate_keep, gate_hbm, left, 4))
    grad_of(dup, b, up_s)
    leaving.append(send_out(up_s, up_hbm, left, 5))
    whole[...] = mm(dgate, wg_ref[...]) + mm(dup, wu_ref[...])
    split_rows(place, whole, keep_s, send_ref)
    leaving.append(send_out(keep_s, keep_hbm, left, 3))
    for copy in leaving:
        copy.wait()


def split_rows(place, whole, keep_ref, send_ref):
    half = whole.shape[0] // 2
    core = bit_of(place, 1, 0)
    keep_ref[0:half, :] = whole[pl.ds(pl.multiple_of(core * half, half), half), :].astype(bf16)
    send_ref[0:half, :] = whole[pl.ds(pl.multiple_of((1 - core) * half, half), half), :].astype(bf16)


def join_rows(place, mine, theirs, whole):
    half = whole.shape[0] // 2
    core = bit_of(place, 1, 0)
    mine, theirs = mine[:half], theirs[:half]
    whole[pl.ds(pl.multiple_of(core * half, half), half), :] = mine
    whole[pl.ds(pl.multiple_of((1 - core) * half, half), half), :] = theirs


def emit_shares(place, bits, whole, keep_ref, send_ref, axis=0):
    order = [0]
    for bit in reversed(bits[1:]):
        order = order + [relative | (1 << bit) for relative in order]
    block = whole.shape[axis] // (2 * len(order))
    for index, relative in enumerate(order):
        for ref, first in ((keep_ref, 0), (send_ref, 1 << bits[0])):
            owner = lax.bitwise_xor(place[0], jnp.int32(relative | first))
            source = pl.ds(pl.multiple_of(owner * block, block), block)
            target = slice(index * block, (index + 1) * block)
            if axis:
                ref[:, target] = whole[:, source]
            else:
                ref[target, :] = whole[source, :]


def share_round_kernel(axis, place, keep_ref, got_ref, keep_out, send_out):
    half = keep_out.shape[axis]
    for at, ref in ((slice(0, half), keep_out), (slice(half, 2 * half), send_out)):
        if axis:
            ref[...] = keep_ref[:, at] + got_ref[:, at]
        else:
            ref[...] = keep_ref[at] + got_ref[at]


def out_part_kernel(place, hid_ref, wd_ref, keep_ref, send_ref, whole):
    whole[...] = mm(hid_ref[...], wd_ref[...])
    split_rows(place, whole, keep_ref, send_ref)


def emit_kernel(axis, bits, place, whole, keep_ref, send_ref):
    emit_shares(place, bits, whole, keep_ref, send_ref, axis)


def early_grads_kernel(
    bits, place, gh_ref, y_ref, a_ref, dgr_ref, gq_ref, halo_ref, before_ref,
    keep_ref, send_ref, whole,
):
    width = dgr_ref.shape[1]
    whole[:, :width] = mm(gh_ref[...], y_ref[:, width:], 0, 0).astype(bf16)
    whole[:, width : 2 * width] = mm(a_ref[...], dgr_ref[...], 0, 0).astype(bf16)
    edge = jnp.concatenate([jnp.zeros((SUB, width), f32), halo_ref[...]], axis=0)
    whole[:, 2 * width :] = (
        mm(a_ref[...], gq_ref[...], 0, 0) + mm(before_ref[...], edge, 0, 0)
    ).astype(bf16)
    emit_shares(place, bits, whole, keep_ref, send_ref)


def early_sum_kernel(place, keep_ref, got_ref, turned_ref, gate_ref, query_ref):
    total = keep_ref[...].astype(f32) + got_ref[...].astype(f32)
    width = gate_ref.shape[1]
    turned_ref[...] = total[:, :width].T
    gate_ref[...] = total[:, width : 2 * width]
    query_ref[...] = total[:, 2 * width :]


def ffn_share_kernel(axis, place, keep_ref, got_ref, out_ref):
    total = keep_ref[...].astype(f32) + got_ref[...].astype(f32)
    out_ref[...] = total if axis else total.T[: out_ref.shape[0], :]


def residual_back_kernel(
    place, mine, theirs, h_ref, g_ref, fgain_ref, wo_ref, o_ref,
    gate_ref, hgain_ref, steps_ref,
    gh_ref, pull_ref, dh_ref, do_ref, dgr_ref, sums_ref, whole,
):
    rows, head_width = o_ref.shape
    heads = head_width // LANES
    join_rows(place, mine[...].astype(f32), theirs[...].astype(f32), whole)
    h = h_ref[...]
    db = whole[...]
    scale = lax.rsqrt(jnp.mean(h * h, axis=-1, keepdims=True) + 1e-06)
    hat = h * scale
    prod = db * hat
    sums_ref[...] = jnp.zeros(sums_ref.shape, f32)
    sums_ref[0:1, :] = jnp.sum(prod, axis=0, keepdims=True)
    inner = jnp.mean(prod * fgain_ref[...], axis=-1, keepdims=True)
    dh = g_ref[...].astype(f32) + scale * (db * fgain_ref[...] - hat * inner)
    dh_ref[...] = dh
    gh = dh.astype(bf16)
    gh_ref[...] = gh
    dy_all = mm(gh, wo_ref[...], 1, 1)
    hg_sum = jnp.zeros((1, LANES), f32)
    for head in range(heads):
        cols = slice(head * LANES, (head + 1) * LANES)
        out, gate, dy = o_ref[:, cols], gate_ref[:, cols], dy_all[:, cols]
        norm = lax.rsqrt(jnp.mean(out * out, axis=-1, keepdims=True) + 1e-05)
        hat_o = out * norm
        sg = sigmoid(gate)
        act = gate * sg
        hg_sum = hg_sum + jnp.sum(dy * hat_o * act, axis=0, keepdims=True)
        dgain = dy * hgain_ref[...]
        dgr_ref[:, cols] = (dgain * hat_o * (sg * (1.0 + gate * (1.0 - sg)))).astype(bf16)
        e = dgain * act
        do_ref[:, cols] = (norm * (e - hat_o * jnp.mean(e * hat_o, axis=-1, keepdims=True))).astype(bf16)
    sums_ref[1:2, 0:LANES] = hg_sum
    chunks = rows // CHUNK
    kept_rows = steps_ref[rows:, 0:LANES].astype(f32)
    pulls = [None] * heads
    for chunk in range(chunks - 1, -1, -1):
        chunk_rows = slice(chunk * CHUNK, (chunk + 1) * CHUNK)
        for head in range(heads):
            cols = slice(head * LANES, (head + 1) * LANES)
            map_cols = slice(head_width + head * LANES, head_width + (head + 1) * LANES)
            local = mm(steps_ref[chunk_rows, cols], do_ref[chunk_rows, cols], 0, 0)
            if pulls[head] is not None:
                local = (
                    local
                    + kept_rows[chunk : chunk + 1, :] * pulls[head]
                    - mm(steps_ref[chunk_rows, map_cols], pulls[head], 0, 0)
                )
            pulls[head] = local
    for head in range(heads):
        pull_ref[head * HEAD_DIM : (head + 1) * HEAD_DIM, :] = pulls[head].astype(bf16)


def back_places(head_width):
    def at_of(head, chunk, part=0):
        col = part * head_width + head * LANES
        return (slice(chunk * CHUNK, (chunk + 1) * CHUNK), slice(col, col + LANES))

    def kept_at(head, chunk, part):
        col = (3 + part) * head_width + head * LANES
        start = 2 * SUB + chunk * CHUNK
        return (slice(start, start + CHUNK), slice(col, col + LANES))

    return at_of, kept_at


def fill_joined(back_ref, facts_ref, joined, joined_ids, head_width):
    width = 3 * head_width
    joined[0:SUB, :] = back_ref[0 : 2 * SUB, :width].astype(f32)[SUB:, :]
    joined[SUB:, :] = back_ref[2 * SUB :, :width].astype(f32)
    joined_ids[...] = facts_ref[:, head_width : head_width + LANES]


def fill_lag_masks(masks, mask_s, du_s):
    rows = mask_s.shape[1] - 2 * SUB
    du_s[0:SUB, :] = jnp.zeros((SUB, LANES), f32)
    du_s[SUB + rows :, :] = jnp.zeros((SUB, LANES), f32)
    for lag in range(1, len(masks)):
        mask_s[lag - 1, 0:SUB, :] = jnp.zeros((SUB, LANES), f32)
        mask_s[lag - 1, SUB : SUB + rows, :] = masks[lag]
        mask_s[lag - 1, SUB + rows :, :] = jnp.zeros((SUB, LANES), f32)


def conv_back(taps_ref, joined, masks, mask_s, du_s, part, head, head_width, rows, grad):
    lags = len(masks) - 1
    col = part * head_width + head * LANES
    cols = slice(col, col + LANES)
    tap_cols = slice(head * LANES, (head + 1) * LANES)
    total = conv_sum(joined, taps_ref, masks, part, head, head_width, rows)
    sg = sigmoid(total)
    if part < 2:
        z = total * sg
        norm = lax.rsqrt(jnp.sum(z * z, axis=-1, keepdims=True) + 1e-06)
        hat = z * norm
        grad = norm * (grad - hat * jnp.sum(grad * hat, axis=-1, keepdims=True))
        if part == 0:
            grad = grad * Q_SCALE
    grad = grad * (sg * (1.0 + total * (1.0 - sg)))
    du_s[SUB : SUB + rows, :] = grad
    before = taps_ref[part, lags : lags + 1, tap_cols] * grad
    halo = jnp.zeros((SUB, LANES), f32)
    tap_grads = [None] * (lags + 1)
    tap_grads[lags] = jnp.sum(grad * joined[SUB : SUB + rows, cols], axis=0, keepdims=True)
    for lag in range(1, lags + 1):
        tap = taps_ref[part, lags - lag : lags - lag + 1, tap_cols]
        tap_grads[lags - lag] = jnp.sum(
            grad * joined[SUB - lag : SUB - lag + rows, cols] * masks[lag], axis=0, keepdims=True
        )
        moved = du_s[SUB + lag : SUB + lag + rows, :]
        before = before + tap * moved * mask_s[lag - 1, SUB + lag : SUB + lag + rows, :]
        halo = halo + tap * du_s[lag : lag + SUB, :] * mask_s[lag - 1, lag : lag + SUB, :]
    return before, halo, tap_grads


def delta_query_kernel(
    place, taps_ref, back_ref, facts_ref, keep_ref, do_ref,
    pre_ref, dk_ref, gq_ref, halo_ref, small_ref,
    joined, joined_ids, dq_s, du_s, mask_s,
):
    rows, head_width = do_ref.shape
    heads = head_width // LANES
    chunks = rows // CHUNK
    fill_joined(back_ref, facts_ref, joined, joined_ids, head_width)
    masks = lag_masks(joined_ids, taps_ref.shape[1] - 1)
    row_ids, col_ids = tri_masks()
    flags = [chunk_flags(joined_ids, chunk) for chunk in range(chunks)]
    at_of, kept_at = back_places(head_width)
    for head in range(heads):
        for chunk in range(chunks):
            same, opened, closing, kept = flags[chunk]
            at = at_of(head, chunk)
            q, k, w_rows, u_rows, scores = (
                back_ref[kept_at(head, chunk, part)] for part in (0, 1, 3, 4, 6)
            )
            state, do = keep_ref[at], do_ref[at]
            fresh = (u_rows.astype(f32) - opened * mm(w_rows, state)).astype(bf16)
            pre_ref[at] = fresh
            pre_ref[at_of(head, chunk, 1)] = mm(scores, do, 0, 0).astype(bf16)
            dscore = jnp.where(row_ids >= col_ids, mm(do, fresh, 1, 1) * same, 0.0).astype(bf16)
            dq_s[at] = opened * mm(do, state, 1, 1) + mm(dscore, k)
            dk_ref[at] = mm(dscore, q, 0, 0)
    fill_lag_masks(masks, mask_s, du_s)
    small_ref[...] = jnp.zeros(small_ref.shape, f32)
    for head in range(heads):
        cols = slice(head * LANES, (head + 1) * LANES)
        gq_ref[:, cols], halo_ref[:, cols], tap_grads = conv_back(
            taps_ref, joined, masks, mask_s, du_s, 0, head, head_width, rows, dq_s[:, cols]
        )
        for row, tap_grad in enumerate(tap_grads):
            small_ref[row : row + 1, cols] = tap_grad


def delta_back_kernel(
    last_bit, place, taps_ref, back_ref, facts_ref, steps_ref, keep_ref, do_ref, pre_ref, dk_ref,
    pack_ref, after_ref, other_ref,
    gp_ref, halo_ref, small_ref,
    joined, joined_ids, dk_s, du_s, mask_s,
):
    rows, head_width = do_ref.shape
    width = 2 * head_width
    heads = head_width // LANES
    chunks = rows // CHUNK
    fill_joined(back_ref, facts_ref, joined, joined_ids, head_width)
    masks = lag_masks(joined_ids, taps_ref.shape[1] - 1)
    row_ids, col_ids = tri_masks()
    flags = [chunk_flags(joined_ids, chunk) for chunk in range(chunks)]
    upper = bit_of(place, 0, last_bit)
    sets = [(head, chunk) for head in range(heads) for chunk in range(chunks)]
    at_of, kept_at = back_places(head_width)
    state_grads = {}
    for head in range(heads):
        at = slice(head * HEAD_DIM, (head + 1) * HEAD_DIM)
        after = after_ref[at, :].astype(f32)
        start = pack_ref.shape[0] - after_ref.shape[0] + head * HEAD_DIM
        suffix_m = pack_ref[start : start + HEAD_DIM, :]
        grad = chosen(upper, after, mm(suffix_m, other_ref[at, :]) + after)
        for chunk in range(chunks - 1, -1, -1):
            state_grads[head, chunk] = grad
            if chunk:
                low = grad.astype(bf16)
                grad = (
                    flags[chunk][3] * grad
                    - mm(steps_ref[at_of(head, chunk, 1)], low, 0, 0)
                    + mm(steps_ref[at_of(head, chunk)], do_ref[at_of(head, chunk)], 0, 0)
                )
    lane_ids = lax.broadcasted_iota(jnp.int32, (CHUNK, LANES), 1)
    gb_cols = [jnp.zeros((CHUNK, LANES), f32) for _ in range(chunks)]
    for head, chunk in sets:
        same, opened, closing, kept = flags[chunk]
        at = at_of(head, chunk)
        k, v, w_rows, u_rows, inverse = (
            back_ref[kept_at(head, chunk, part)] for part in (1, 2, 3, 4, 5)
        )
        kf, vf = k.astype(f32), v.astype(f32)
        beta = facts_ref[
            SUB + chunk * CHUNK : SUB + (chunk + 1) * CHUNK, head * LANES : (head + 1) * LANES
        ]
        state = keep_ref[at]
        sgrad = state_grads[head, chunk].astype(bf16)
        fresh = pre_ref[at]
        dfresh = pre_ref[at_of(head, chunk, 1)].astype(f32) + mm(closing * kf, sgrad)
        dw = -(opened * mm(dfresh, state, 1, 1))
        dx = mm(inverse, jnp.concatenate([dfresh, dw], axis=1), 0, 0)
        dxv, dxk = dx[:, :HEAD_DIM], dx[:, HEAD_DIM:]
        dlow = mm(dx, jnp.concatenate([u_rows, w_rows], axis=1), 1, 1)
        dlow = jnp.where(row_ids > col_ids, -dlow * same, 0.0)
        inner = mm(k, k, 1, 1)
        dbeta = jnp.sum(dxv * vf + dxk * kf + dlow * inner, axis=-1, keepdims=True)
        glow = (dlow * beta).astype(bf16)
        dk_s[at_of(head, chunk, 0)] = (
            beta * dxk
            + dk_ref[at]
            + closing * mm(fresh, sgrad, 1, 1)
            + mm(glow, k)
            + mm(glow, k, 0, 0)
        )
        dk_s[at_of(head, chunk, 1)] = beta * dxv
        raw = jnp.broadcast_to(dbeta, (CHUNK, LANES)) * beta * (1.0 - beta)
        gb_cols[chunk] = jnp.where(lane_ids == head, raw, gb_cols[chunk])
    bias_sum = jnp.zeros((1, LANES), f32)
    for chunk in range(chunks):
        gp_ref[chunk * CHUNK : (chunk + 1) * CHUNK, width:] = gb_cols[chunk]
        bias_sum = bias_sum + jnp.sum(gb_cols[chunk], axis=0, keepdims=True)
    small_ref[...] = jnp.zeros(small_ref.shape, f32)
    tap_count = len(masks)
    small_ref[2 * tap_count : 2 * tap_count + 1, 0:LANES] = bias_sum
    fill_lag_masks(masks, mask_s, du_s)
    for part in (1, 2):
        for head in range(heads):
            col = (part - 1) * head_width + head * LANES
            cols = slice(col, col + LANES)
            gp_ref[:, cols], halo_ref[:, cols], tap_grads = conv_back(
                taps_ref, joined, masks, mask_s, du_s, part, head, head_width, rows, dk_s[:, cols]
            )
            for tap, tap_grad in enumerate(tap_grads):
                row = (part - 1) * tap_count + tap
                small_ref[row : row + 1, head * LANES : (head + 1) * LANES] = tap_grad


def input_back_kernel(
    place, gp_ref, halo_ref, gq_ref, qhalo_ref, dgr_ref, wq_ref, wk_ref, wv_ref, wg_ref, wb_ref,
    x_ref, gain_ref, before_ref, sums_ref, whole, edge_ref, rows_ref,
):
    width = halo_ref.shape[1]
    head_width = width // 2
    zeros = jnp.zeros((SUB, head_width), f32)
    total = mm(dgr_ref[...], wg_ref[...], 1, 1) + mm(gp_ref[:, width : width + SUB], wb_ref[...])
    edge = None
    first, second = slice(0, head_width), slice(head_width, width)
    for grads, halo, w_ref in (
        (gq_ref[...], qhalo_ref[...], wq_ref),
        (gp_ref[:, first], halo_ref[:, first], wk_ref),
        (gp_ref[:, second], halo_ref[:, second], wv_ref),
    ):
        total = total + mm(grads, w_ref[...], 1, 1)
        piece = mm(jnp.concatenate([zeros, halo], axis=0), w_ref[...], 1, 1)
        edge = piece if edge is None else edge + piece
    whole[...] = total
    edge_ref[...] = edge[SUB:, :]
    x = x_ref[...].astype(f32)
    scale = lax.rsqrt(jnp.mean(x * x, axis=-1, keepdims=True) + 1e-06)
    hat_before = before_ref[...].astype(f32) / gain_ref[...]
    rows_ref[...] = jnp.zeros(rows_ref.shape, f32)
    rows_ref[0:1, :] = jnp.sum(total * (x * scale), axis=0, keepdims=True) + jnp.sum(
        edge * hat_before, axis=0, keepdims=True
    )
    rows_ref[1:2, :] = sums_ref[1:2, :]


def input_split_kernel(place, whole_ref, next_ref, keep_ref, send_ref, whole):
    rows = whole.shape[0]
    whole[...] = whole_ref[...]
    whole[rows - SUB :, :] = whole[rows - SUB :, :] + next_ref[...]
    split_rows(place, whole, keep_ref, send_ref)


def small_places(model, taps, heads, width):
    sizes = [model, LANES, model, 3 * taps * heads * LANES, heads * model, LANES]
    starts = [0]
    for size in sizes:
        starts.append(starts[-1] + size // LANES)
    across = width // LANES
    rows = -(-starts[-1] // across)
    return starts[:-1], -(-rows // (2 * SUB)) * 2 * SUB


def piece_at(index, width):
    across = width // LANES
    col = index % across * LANES
    return (slice(index // across, index // across + 1), slice(col, col + LANES))


def project_grads_kernel(
    bits, taps, place, a_ref, before_ref, gp_ref, halo_ref, sums_a, qsmall_ref, gsmall_ref, head_rows,
    keep_ref, send_ref, whole, small,
):
    a = a_ref[...]
    model = a.shape[1]
    width = whole.shape[1]
    heads = width // (2 * LANES)
    starts, _ = small_places(model, taps, heads, width)
    small[...] = jnp.zeros(small.shape, f32)
    beta_rows = mm(gp_ref[:, width:], a, 0, 0)
    pieces = model // LANES
    for piece in range(pieces):
        cols = slice(piece * LANES, (piece + 1) * LANES)
        small[piece_at(starts[0] + piece, width)] = head_rows[0:1, cols]
        small[piece_at(starts[2] + piece, width)] = sums_a[0:1, cols]
        for head in range(heads):
            small[piece_at(starts[4] + head * pieces + piece, width)] = beta_rows[head : head + 1, cols]
    for row in range(3 * taps):
        ref, at = (qsmall_ref, row) if row < taps else (gsmall_ref, row - taps)
        for head in range(heads):
            small[piece_at(starts[3] + row * heads + head, width)] = ref[
                at : at + 1, head * LANES : (head + 1) * LANES
            ]
    small[piece_at(starts[1], width)] = head_rows[1:2, 0:LANES]
    small[piece_at(starts[5], width)] = gsmall_ref[2 * taps : 2 * taps + 1, 0:LANES]
    edge = jnp.concatenate([jnp.zeros((SUB, width), f32), halo_ref[...]], axis=0)
    whole[...] = (mm(a, gp_ref[:, :width], 0, 0) + mm(before_ref[...], edge, 0, 0)).astype(bf16)
    emit_shares(place, bits, whole, keep_ref, send_ref)
    keep_ref[model // 2 :, :] = small[...].astype(bf16)
    send_ref[model // 2 :, :] = small[...].astype(bf16)


def share_small_kernel(place, keep_ref, got_ref, keep_out, send_out_ref):
    extra = 2 * keep_out.shape[0] - keep_ref.shape[0]
    half = keep_out.shape[0] - extra
    small = keep_ref[2 * half :, :] + got_ref[2 * half :, :]
    keep_out[0:half, :] = keep_ref[0:half, :] + got_ref[0:half, :]
    send_out_ref[0:half, :] = keep_ref[half : 2 * half, :] + got_ref[half : 2 * half, :]
    keep_out[half:, :] = small
    send_out_ref[half:, :] = small


def project_sum_kernel(
    taps, place, keep_ref, got_ref, k_ref, v_ref,
    norm_ref, hgain_ref, fgain_ref, taps_ref, beta_ref, bias_ref, small, rows_s,
):
    share, head_width = k_ref.shape
    width = 2 * head_width
    heads = head_width // LANES
    total = keep_ref[...].astype(f32) + got_ref[...].astype(f32)
    for index, out_ref in enumerate((k_ref, v_ref)):
        out_ref[...] = total[:share, index * head_width : (index + 1) * head_width]
    small[...] = total[share:, :]
    model = norm_ref.shape[1]
    starts, _ = small_places(model, taps, heads, width)
    pieces = model // LANES
    for piece in range(pieces):
        cols = slice(piece * LANES, (piece + 1) * LANES)
        norm_ref[0:1, cols] = small[piece_at(starts[0] + piece, width)]
        fgain_ref[0:1, cols] = small[piece_at(starts[2] + piece, width)]
        for head in range(heads):
            row = small[piece_at(starts[4] + head * pieces + piece, width)]
            rows_s[head * pieces + piece : head * pieces + piece + 1, :] = row
    hgain_ref[...] = small[piece_at(starts[1], width)]
    for part in range(3):
        for tap in range(taps):
            for head in range(heads):
                taps_ref[part, tap : tap + 1, head * LANES : (head + 1) * LANES] = small[
                    piece_at(starts[3] + (part * taps + tap) * heads + head, width)
                ]
    bias_ref[...] = small[piece_at(starts[5], width)][:, : bias_ref.shape[1]]
    if share % LANES:
        for head in range(heads):
            for piece in range(pieces):
                at = head * pieces + piece
                beta_ref[head : head + 1, piece * LANES : (piece + 1) * LANES] = rows_s[at : at + 1, :]
    else:
        for head in range(heads):
            for piece in range(share // LANES):
                at = head * pieces + place[0] * (share // LANES) + piece
                beta_ref[head : head + 1, piece * LANES : (piece + 1) * LANES] = rows_s[pl.ds(at, 1), :]


def input_grad_kernel(place, mine, theirs, x_ref, gain_ref, dh_ref, out_ref, whole):
    join_rows(place, mine[...].astype(f32), theirs[...].astype(f32), whole)
    x = x_ref[...].astype(f32)
    scale = lax.rsqrt(jnp.mean(x * x, axis=-1, keepdims=True) + 1e-06)
    hat = x * scale
    grad = whole[...] * gain_ref[...]
    inner = jnp.mean(grad * hat, axis=-1, keepdims=True)
    out_ref[...] = dh_ref[...] + scale * (grad - hat * inner)


def output_kernel(place, mine, theirs, h_ref, out_ref, whole):
    join_rows(place, mine[...].astype(f32), theirs[...].astype(f32), whole)
    out_ref[...] = (h_ref[...] + whole[...]).astype(bf16)


def add_kernel(place, left_ref, right_ref, out_ref):
    out_ref[...] = (left_ref[...].astype(f32) + right_ref[...].astype(f32)).astype(out_ref.dtype)


def added(chain, left, right):
    shape = left.value.shape if isinstance(left, Free) else left.shape
    (out,) = kernel_call(
        add_kernel, (shaped(shape, right.dtype),), chain, left, right, name="added"
    )
    return out


def gathered(value):
    count = lax.axis_size("head")
    blocks = [value]
    bit = 2
    while bit < count:
        blocks = blocks + [swap(block, "head", bit) for block in blocks]
        bit *= 2
    return blocks + [swap(block, "head", 1) for block in blocks]


class Shares:
    def __init__(self, keep, send, bits, axis=0):
        self.keep, self.bits, self.axis = keep, list(bits), axis
        self.got = swap(send, "seq", 1 << self.bits.pop(0))

    def step(self, chain):
        half = list(self.got.shape)
        half[self.axis] //= 2
        self.keep, send = kernel_call(
            functools.partial(share_round_kernel, self.axis),
            (shaped(half, bf16), shaped(half, bf16)),
            chain, self.keep, self.got, name="share_round",
        )
        self.got = swap(send, "seq", 1 << self.bits.pop(0))

    def until(self, chain, left):
        while len(self.bits) > left:
            self.step(chain)

    def pair(self, chain):
        self.until(chain, 0)
        return self.keep, self.got


def head_rounds(chain, value):
    count = lax.axis_size("head")
    bit = 1
    while bit < count:
        value = added(chain, value, swap(value, "head", bit))
        bit *= 2
    return value


def body(
    block_input, cotangent, segment_ids, norm_gain, w_query, w_key, w_value, w_gate, w_beta,
    beta_bias, conv_weight, head_gain, w_out, ffn_gain, w_ffn_gate, w_ffn_up, w_ffn_down,
):
    rows, model = block_input.shape
    heads = w_beta.shape[1]
    head_width = w_query.shape[1]
    ffn_width = w_ffn_gate.shape[1]
    taps = conv_weight.shape[1]
    seq_count = lax.axis_size("seq")
    rounds = seq_count.bit_length() - 1
    share = model // seq_count
    width = 3 * head_width
    chunks = rows // CHUNK
    y_first = list(range(rounds))
    y_last = y_first[1:] + y_first[:1]
    y_next = y_first[1:2] + y_first[:1] + y_first[2:]
    by_plan = {"first": y_first, "last": y_last, "next": y_next}
    down_bits, gate_bits, up_bits, early_bits, project_bits = (
        by_plan[PLANS[key]] for key in ("down", "gate", "up", "early", "project")
    )

    chain = Chain()

    def ffn_share(chain, pair):
        return kernel_call(
            functools.partial(ffn_share_kernel, ffn_axis),
            (final((ffn_width, share), f32),), chain, *pair, name="ffn_share",
        )

    bias_in = beta_bias[None] if heads > 1 else jnp.broadcast_to(beta_bias[None], (1, 2))
    gain_row, fgain_row, hgain_row = Free(norm_gain[None]), Free(ffn_gain[None]), Free(head_gain[None])
    taps_in = Free(conv_weight)

    square = (rows, head_width)
    p, beta, seg_cols, tail, a, gate_raw, w_beta8, w_out_copy = kernel_call(
        project_kernel,
        (
            shaped((rows, width), bf16),
            shaped(square, f32),
            shaped((rows, LANES), f32),
            shaped((SUB, width + LANES + model), f32),
            Direct((rows, model), bf16),
            Direct(square, f32),
            Direct((SUB, model), f32),
            Direct(w_out.shape, bf16),
        ),
        chain, Far(block_input), Far(w_query), Far(w_key), Far(w_value), Far(w_gate),
        Far(norm_gain[None]), Far(w_beta.T), Far(bias_in),
        Far(segment_ids.reshape(chunks, LANES)), Far(w_out),
        scratch=(
            pltpu.VMEM((rows, model), bf16),
            pltpu.VMEM((4, model, head_width), bf16),
            pltpu.VMEM((1, model), f32),
            pltpu.VMEM((heads, model), bf16),
            pltpu.VMEM(bias_in.shape, f32),
            pltpu.VMEM((chunks, LANES), jnp.int32),
            pltpu.VMEM((rows, model), bf16),
            pltpu.VMEM(square, f32),
            pltpu.VMEM((SUB, model), f32),
            pltpu.VMEM(w_out.shape, bf16),
            pltpu.SemaphoreType.DMA((10,)),
            pltpu.SemaphoreType.DMA((4,)),
        ),
        name="project",
    )
    halo = shift(tail, "seq", 1)
    joined = pltpu.VMEM((rows + SUB, width), f32)
    joined_ids = pltpu.VMEM((rows + SUB, LANES), f32)
    maps, mix, back, facts, a_before = kernel_call(
        delta_kernel,
        (
            shaped((2 * heads * HEAD_DIM, HEAD_DIM), bf16),
            shaped((rows + 2 * SUB, 4 * head_width), bf16),
            shaped((rows + 2 * SUB, 2 * width + 4 * head_width), bf16),
            shaped((rows + SUB, head_width + LANES), f32),
            shaped((2 * SUB, model), bf16),
        ),
        chain, p, halo, Held(conv_weight), seg_cols, beta,
        scratch=(joined, joined_ids),
        name="delta",
    )
    half_maps = heads * HEAD_DIM
    w_out_all = gathered(w_out_copy)
    prefix = pack = maps
    for bit in range(rounds - 1):
        other = swap(maps, "seq", 1 << bit)
        if bit == 0:
            back, facts, steps, a_before = park(
                chain, (back, None), (facts, None), (mix, 2 * head_width), (a_before, None), name="park_delta"
            )
        maps, prefix, pack = kernel_call(
            functools.partial(scan_round_kernel, bit),
            (
                shaped((half_maps if bit == rounds - 2 else 2 * half_maps, HEAD_DIM), bf16),
                shaped((2 * half_maps, HEAD_DIM), bf16),
                shaped((2 * half_maps * (bit + 1), HEAD_DIM), bf16),
            ),
            chain, maps, other, prefix, pack,
            name="scan_round",
            )
    other_a = swap(maps, "seq", 1 << (rounds - 1))
    y, mixed, keep_y = kernel_call(
        functools.partial(mixer_kernel, rounds - 1),
        (shaped(square, bf16), shaped(square, f32), shaped((rows, 2 * head_width), bf16)),
        chain, prefix, other_a, mix, Free(gate_raw), hgain_row,
        name="mixer",
    )
    mixed, keep_y, pack = park(
        chain, (mixed, None), (keep_y, None), (pack, None), name="park_mixer"
    )
    y_all = gathered(y)
    half = (rows // 2, model)
    wide = pltpu.VMEM((rows, model), f32)
    ffn_wide = -(-ffn_width // LANES) * LANES
    ffn_axis = 0 if share % LANES else 1
    ffn_whole = (ffn_width, model) if ffn_axis else (model, ffn_wide)
    ffn_half = (ffn_width, model // 2) if ffn_axis else (model // 2, ffn_wide)
    (
        db_send, down_send, gate_send, h, hidden, db_keep, down_keep, gate_keep, grad_up,
    ) = kernel_call(
        functools.partial(ffn_kernel, ffn_axis, down_bits, gate_bits),
        (
            shaped(half, bf16),
            shaped(ffn_half, bf16),
            shaped(ffn_half, bf16),
            Direct((rows, model), f32),
            Direct((rows, ffn_width), bf16),
            Direct(half, bf16),
            Direct(ffn_half, bf16),
            Direct(ffn_half, bf16),
            Direct(ffn_whole, bf16),
        ),
        chain, Free(block_input), Free(cotangent), fgain_row,
        Free(w_ffn_gate.T), Free(w_ffn_up.T), Free(w_ffn_down),
        *y_all, Free(w_out_all[0]), *w_out_all[1:],
        scratch=(
            wide,
            pltpu.VMEM((rows, ffn_width), bf16),
            pltpu.VMEM(half, bf16),
            pltpu.VMEM(ffn_half, bf16),
            pltpu.VMEM(ffn_half, bf16),
            pltpu.VMEM(ffn_whole, bf16),
            pltpu.VMEM(ffn_whole, bf16),
            wide,
            pltpu.SemaphoreType.DMA((6,)),
        ),
        name="ffn",
    )
    down = Shares(Free(down_keep), down_send, down_bits, ffn_axis)
    gate = Shares(Free(gate_keep), gate_send, gate_bits, ffn_axis)
    head_bits = [1 << bit for bit in range(1, lax.axis_size("head").bit_length() - 1)]
    pre = dk_part = gq = q_halo = q_small = q_share = None
    conv_scratch = (
        pltpu.VMEM((rows + 2 * SUB, LANES), f32),
        pltpu.VMEM((taps - 1, rows + 2 * SUB, LANES), f32),
    )
    step_bits = list(range(rounds - 1))
    rest_bits = list(project_bits[1:])
    _, small_extra = small_places(model, taps, heads, 2 * head_width)
    mine = out_keep = out_send = gh = pull = dh = d_out = d_gate_raw = sums_a = other = after = up = up_keep = up_send = out_mine = early = early_keep = early_send = gp = gp_halo = grad_small = da = da_edge = head_rows = from_next = keep = send = got = da_keep = da_send = block_output = input_grad = out_share = w_gate_share = down_share = ffn_gate_share = ffn_up_share = None

    def db_core():
        nonlocal mine
        mine = added(chain, Held(db_keep), swap(db_send, "head", 1))

    def out_part():
        nonlocal out_keep, out_send
        out_keep, out_send = kernel_call(
            out_part_kernel,
            (shaped(half, bf16), shaped(half, bf16)),
            chain, Held(hidden), Held(w_ffn_down),
            scratch=(wide,),
            name="out_part",
        )

    def db_far():
        nonlocal mine
        for bit in head_bits:
            mine = added(chain, mine, swap(mine, "head", bit))

    def residual_back():
        nonlocal gh, pull, dh, d_out, d_gate_raw, sums_a, other
        gh, pull, dh, d_out, d_gate_raw, sums_a = kernel_call(
            residual_back_kernel,
            (
                shaped((rows, model), bf16),
                shaped((half_maps, HEAD_DIM), bf16),
                shaped((rows, model), f32),
                shaped(square, bf16),
                shaped(square, bf16),
                shaped((SUB, model), f32),
            ),
            chain, mine, swap(mine, "head", 1), Free(h), Free(cotangent), fgain_row, Free(w_out), Free(mixed),
            Free(gate_raw), hgain_row, Free(steps),
            scratch=(wide,),
            name="residual_back",
        )
        other = swap(pull, "seq", 1)

    def park_back():
        nonlocal dh, d_out, d_gate_raw, sums_a
        dh, d_out, d_gate_raw, sums_a = park(
            chain, (dh, None), (d_out, None), (d_gate_raw, None), (sums_a, None), name="park_residual"
        )

    def down_one():
        down.step(chain)

    def gate_one():
        gate.step(chain)

    def scan_back():
        nonlocal pull, other, after

        bit = step_bits.pop(0)
        pull, after = kernel_call(
            functools.partial(back_round_kernel, bit),
            (shaped(pull.shape, bf16), shaped(pull.shape, bf16)),
            chain, Free(pack), pull, other, pull if after is None else after,
            name="back_round",
        )
        other = swap(pull, "seq", 2 << bit)

    def scan_rest():
        while step_bits:
            scan_back()

    def up_blocks():
        nonlocal up, up_keep, up_send
        up_keep, up_send = kernel_call(
            functools.partial(emit_kernel, ffn_axis, up_bits),
            (shaped(ffn_half, bf16), shaped(ffn_half, bf16)),
            chain, Free(grad_up),
            name="up_blocks",
        )
        up = Shares(up_keep, up_send, up_bits, ffn_axis)

    def out_core():
        nonlocal out_mine
        out_mine = added(chain, out_keep, swap(out_send, "head", 1))

    def delta_query():
        nonlocal pre, dk_part, gq, q_halo, q_small
        pre, dk_part, gq, q_halo, q_small = kernel_call(
            delta_query_kernel,
            (
                shaped((rows, 2 * head_width), bf16),
                shaped(square, f32),
                stored(square, f32),
                stored((SUB, head_width), f32),
                stored((-(-taps // SUB) * SUB, head_width), f32),
            ),
            chain, taps_in, Free(back), Free(facts), Free(keep_y), Free(d_out),
            scratch=(joined, joined_ids, pltpu.VMEM(square, f32)) + conv_scratch,
            name="delta_query",
        )

    def early_grads():
        nonlocal early
        early_keep, early_send = kernel_call(
            functools.partial(early_grads_kernel, early_bits),
            (shaped((model // 2, width), bf16), shaped((model // 2, width), bf16)),
            chain, gh, Free(keep_y), Free(a), Free(d_gate_raw), Held(gq), Held(q_halo), Held(a_before),
            scratch=(pltpu.VMEM((model, width), bf16),),
            name="early_grads",
        )
        early = Shares(early_keep, early_send, early_bits)

    def down_two():
        down.until(chain, 0)

    def gate_two():
        gate.until(chain, 0)

    def out_far():
        nonlocal out_mine
        for bit in head_bits:
            out_mine = added(chain, out_mine, swap(out_mine, "head", bit))

    def delta_back():
        nonlocal gp, gp_halo, grad_small
        gp, gp_halo, grad_small = kernel_call(
            functools.partial(delta_back_kernel, rounds - 1),
            (
                shaped((rows, 2 * head_width + LANES), f32),
                shaped((SUB, 2 * head_width), f32),
                stored((-(-(2 * taps + 1) // SUB) * SUB, head_width), f32),
            ),
            chain, taps_in, Free(back), Free(facts), Free(steps), Free(keep_y), Free(d_out),
            pre, dk_part, Free(pack), after, other,
            scratch=(joined, joined_ids, pltpu.VMEM((rows, 2 * head_width), f32)) + conv_scratch,
            name="delta_back",
        )

    def input_back():
        nonlocal da, da_edge, head_rows, from_next
        da, da_edge, head_rows = kernel_call(
            input_back_kernel,
            (shaped((rows, model), f32), shaped((SUB, model), f32), shaped((SUB, model), f32)),
            chain, gp, gp_halo, Free(gq), Free(q_halo), Free(d_gate_raw),
            Free(w_query), Free(w_key), Free(w_value), Free(w_gate), Free(w_beta8), Free(block_input),
            gain_row, Free(a_before), Free(sums_a),
            name="input_back",
        )
        from_next = shift(da_edge, "seq", -1)

    def up_one():
        up.step(chain)

    def rows_core():
        nonlocal head_rows
        head_rows = added(chain, head_rows, swap(head_rows, "head", 1))

    def rows_far():
        nonlocal head_rows
        for bit in head_bits:
            head_rows = added(chain, head_rows, swap(head_rows, "head", bit))

    def project_grads():
        nonlocal keep, send, got
        keep, send = kernel_call(
            functools.partial(project_grads_kernel, project_bits, taps),
            (
                shaped((model // 2 + small_extra, 2 * head_width), bf16),
                shaped((model // 2 + small_extra, 2 * head_width), bf16),
            ),
            chain, Free(a), Free(a_before), gp, gp_halo, Free(sums_a), Held(q_small), Free(grad_small), head_rows,
            scratch=(pltpu.VMEM((model, 2 * head_width), bf16), pltpu.VMEM((small_extra, 2 * head_width), f32)),
            name="project_grads",
        )
        got = swap(send, "seq", 1 << project_bits[0])

    def input_split():
        nonlocal da_keep, da_send
        da_keep, da_send = kernel_call(
            input_split_kernel,
            (shaped(half, bf16), shaped(half, bf16)),
            chain, da, from_next,
            scratch=(wide,),
            name="input_split",
        )

    def early_one():
        early.step(chain)

    def up_two():
        up.until(chain, 0)

    def da_core():
        nonlocal mine
        mine = added(chain, da_keep, swap(da_send, "head", 1))

    def da_far():
        nonlocal mine
        for bit in head_bits:
            mine = added(chain, mine, swap(mine, "head", bit))

    def output():
        nonlocal block_output
        (block_output,) = kernel_call(
            output_kernel,
            (final((rows, model), bf16),),
            chain, out_mine, swap(out_mine, "head", 1), Free(h),
            scratch=(wide,),
            name="output",
        )

    def input_grad():
        nonlocal input_grad
        (input_grad,) = kernel_call(
            input_grad_kernel,
            (final((rows, model), f32),),
            chain, mine, swap(mine, "head", 1), Free(block_input), gain_row, Free(dh),
            scratch=(wide,),
            name="input_grad",
        )

    def share_one():
        nonlocal keep, send, got

        shape = ((keep.shape[0] - small_extra) // 2 + small_extra, 2 * head_width)
        keep, send = kernel_call(
            share_small_kernel,
            (shaped(shape, bf16), shaped(shape, bf16)),
            chain, keep, got,
            name="share_small",
        )
        got = swap(send, "seq", 1 << rest_bits.pop(0))

    def share_two():
        while rest_bits:
            share_one()

    def early_two():
        early.until(chain, 0)

    def down_out():
        nonlocal down_share
        (down_share,) = ffn_share(chain, down.pair(chain))

    def up_out():
        nonlocal ffn_up_share
        (ffn_up_share,) = ffn_share(chain, up.pair(chain))

    def gate_out():
        nonlocal ffn_gate_share
        (ffn_gate_share,) = ffn_share(chain, gate.pair(chain))

    def early_out():
        nonlocal out_share, w_gate_share, q_share
        out_share, w_gate_share, q_share = kernel_call(
            early_sum_kernel,
            (
                final((head_width, share), f32),
                final((share, head_width), f32),
                final((share, head_width), f32),
            ),
            chain, *early.pair(chain), name="early_sum",
        )

    parts = (
        db_core,
        out_part,
        db_far,
        residual_back,
        park_back,
        down_one,
        gate_one,
        scan_back,
        up_blocks,
        out_core,
        scan_rest,
        delta_query,
        early_grads,
        down_two,
        gate_two,
        out_far,
        delta_back,
        input_back,
        up_one,
        rows_core,
        input_split,
        rows_far,
        project_grads,
        up_two,
        early_one,
        da_core,
        output,
        down_out,
        share_one,
        early_two,
        up_out,
        da_far,
        input_grad,
        share_two,
        early_out,
        gate_out,
    )
    by_name = {part.__name__: part for part in parts}
    for name in ORDER:
        by_name[name]()
    beta_shape = (heads, model if share % LANES else share)
    (
        k_share, v_share, norm_total, head_gain_total, ffn_gain_total, conv_total, beta_rows,
        bias_total,
    ) = kernel_call(
        functools.partial(project_sum_kernel, taps),
        tuple(final((share, head_width), f32) for _ in range(2))
        + (
            final((1, model), f32),
            final((1, LANES), f32),
            final((1, model), f32),
            final(conv_weight.shape, f32),
            final(beta_shape, f32),
            final((1, heads), f32),
        ),
        chain, keep, got,
        scratch=(
            pltpu.VMEM((small_extra, 2 * head_width), f32),
            pltpu.VMEM((-(-heads * model // LANES // SUB) * SUB, LANES), f32),
        ),
        name="project_sum",
    )
    if share % LANES:
        beta_rows = lax.dynamic_slice(beta_rows, (0, lax.axis_index("seq") * share), (heads, share))
    beta_share = beta_rows.T
    return (
        block_output,
        input_grad,
        norm_total[0],
        q_share,
        k_share,
        v_share,
        w_gate_share,
        beta_share,
        bias_total[0],
        conv_total,
        head_gain_total[0],
        out_share,
        ffn_gain_total[0],
        ffn_gate_share.T,
        ffn_up_share.T,
        down_share,
    )


def solution(mesh):
    return jax.shard_map(
        body,
        mesh=mesh,
        in_specs=(
            P("seq", None), P("seq", None), P("seq"), P(),
            P(None, "head"), P(None, "head"), P(None, "head"), P(None, "head"), P(None, "head"),
            P("head"), P(None, None, "head"), P(), P("head", None), P(),
            P(None, "head"), P(None, "head"), P("head", None),
        ),
        out_specs=(
            P("seq", None), P("seq", None), P(),
            P("seq", "head"), P("seq", "head"), P("seq", "head"), P("seq", "head"), P("seq", "head"),
            P("head"), P(None, None, "head"), P(), P("head", "seq"), P(),
            P("seq", "head"), P("seq", "head"), P("head", "seq"),
        ),
        check_vma=False,
    )
```

```python
import functools
import math

import jax
import jax.numpy as jnp
from jax import lax
from jax.experimental import pallas as pl
from jax.experimental.pallas import tpu as pltpu
from jax.sharding import PartitionSpec as P

HEAD_DIM = 128
CHUNK = 128
LANES = 128
SUB = 8
Q_SCALE = HEAD_DIM ** (-0.5)
VMEM_SLACK = 7 * 1024 * 1024

ORDER = (
    "db_core",
    "db_far",
    "residual_back",
    "out_part",
    "gate_one",
    "down_one",
    "park_back",
    "scan_back",
    "up_blocks",
    "down_two",
    "out_core",
    "scan_rest",
    "delta_query",
    "early_grads",
    "gate_two",
    "delta_back",
    "input_back",
    "rows_core",
    "out_far",
    "input_split",
    "up_one",
    "rows_far",
    "project_grads",
    "up_two",
    "early_one",
    "da_core",
    "output",
    "down_out",
    "share_one",
    "early_two",
    "up_out",
    "da_far",
    "share_two",
    "gate_out",
    "early_out",
    "input_grad",
)
PLANS = {"down": "first", "gate": "last", "up": "first", "early": "first", "project": "first"}

bf16 = jnp.bfloat16
f32 = jnp.float32


def mm(left, right, left_dim=1, right_dim=0):
    return lax.dot_general(
        left.astype(bf16),
        right.astype(bf16),
        (((left_dim,), (right_dim,)), ((), ())),
        preferred_element_type=f32,
    )


def sigmoid(value):
    return 1.0 / (1.0 + jnp.exp(-value))


class Free:
    def __init__(self, value):
        self.value = value


class Held(Free):
    pass


class Far(Free):
    pass


class Place:
    def __getitem__(self, which):
        return lax.axis_index(("seq", "head")[which])


class Direct:
    def __init__(self, shape, dtype):
        self.shape, self.dtype = tuple(shape), dtype


class Chain:
    def __init__(self):
        self.token = None


def kernel_call(body, out_shapes, chain, *args, scratch=(), name, deps=()):
    vmem = pl.BlockSpec(memory_space=pltpu.VMEM)
    anywhere = pl.BlockSpec(memory_space=pl.ANY)
    size_of = lambda a: math.prod(a.shape) * jnp.dtype(a.dtype).itemsize
    held = sum(size_of(s) for s in scratch if hasattr(s, "dtype") and not is_semaphore(s))
    operands, specs = [], []
    for arg in args:
        if isinstance(arg, Free):
            value = arg.value
            if not type(arg) is Free:
                value = pltpu.with_memory_space_constraint(value, pltpu.HBM)
            operands.append(value)
            specs.append(anywhere if isinstance(arg, Far) else vmem)
            if not isinstance(arg, Far):
                held += size_of(value)
        else:
            operands.append(pltpu.with_memory_space_constraint(arg, pltpu.VMEM))
            specs.append(vmem)
    ins, outs = len(args), len(out_shapes)
    waits = (0 if chain.token is None else 1) + len(deps)
    operands += list(deps)
    specs += [anywhere] * len(deps)
    if chain.token is not None:
        operands.append(pltpu.with_memory_space_constraint(chain.token, pltpu.VMEM))
        specs.append(vmem)
    results, result_specs = [], []
    for out in out_shapes:
        if isinstance(out, Direct):
            results.append(pltpu.HBM(out.shape, out.dtype))
            result_specs.append(anywhere)
        else:
            results.append(out)
            result_specs.append(vmem)
            if isinstance(out, jax.ShapeDtypeStruct) or out.memory_space == pltpu.HBM:
                held += size_of(out)
    results.append(shaped((SUB, LANES), f32))
    result_specs.append(vmem)
    here = Place()

    def run(*refs):
        refs[ins + waits + outs][...] = jnp.zeros((SUB, LANES), f32)
        body(here, *refs[:ins], *refs[ins + waits : ins + waits + outs], *refs[ins + waits + outs + 1 :])

    *values, chain.token = pl.pallas_call(
        run,
        out_shape=tuple(results),
        in_specs=specs,
        out_specs=tuple(result_specs),
        scratch_shapes=list(scratch),
        compiler_params=pltpu.CompilerParams(vmem_limit_bytes=int(held) + VMEM_SLACK),
        cost_estimate=pl.CostEstimate(flops=0, bytes_accessed=0, transcendentals=0),
        name=name,
    )(*operands)
    return values


def stored(shape, dtype):
    return pltpu.HBM(tuple(shape), dtype)


def send_out(source, target, sems, index):
    copy = pltpu.make_async_copy(source, target, sems.at[index])
    copy.start()
    return copy


def is_semaphore(scratch):
    return not (
        jnp.issubdtype(scratch.dtype, jnp.floating) or jnp.issubdtype(scratch.dtype, jnp.integer)
    )


def final(shape, dtype):
    return jax.ShapeDtypeStruct(tuple(shape), dtype)


def shaped(shape, dtype):
    return pltpu.VMEM(tuple(shape), dtype)


def swap(value, axis, bit):
    count = lax.axis_size(axis)
    return lax.ppermute(value, axis, [(s, s ^ bit) for s in range(count)])


def shift(value, axis, step):
    count = lax.axis_size(axis)
    return lax.ppermute(
        value, axis, [(s, s + step) for s in range(count) if 0 <= s + step < count]
    )


def bit_of(place_ref, which, bit):
    return lax.rem(lax.shift_right_logical(place_ref[which], bit), 2)


def chosen(flag, when_one, when_zero):
    return jnp.where(flag == 1, when_one, when_zero)


def tri_masks():
    rows = lax.broadcasted_iota(jnp.int32, (CHUNK, CHUNK), 0)
    cols = lax.broadcasted_iota(jnp.int32, (CHUNK, CHUNK), 1)
    return rows, cols


def unit_inverses(lowers):
    rows, cols = tri_masks()
    eye = jnp.where(rows == cols, 1.0, 0.0).astype(f32)
    width = 1
    inverses = None
    while width < CHUNK:
        shift_bits = width.bit_length() - 1
        row_block = lax.shift_right_logical(rows, shift_bits)
        col_block = lax.shift_right_logical(cols, shift_bits)
        within = (
            lax.shift_right_logical(row_block, 1) == lax.shift_right_logical(col_block, 1)
        ) & (row_block != col_block)
        couplings = [jnp.where(within, low, 0.0) for low in lowers]
        if inverses is None:
            inverses = [eye - coupling for coupling in couplings]
        else:
            halves = [mm(inv, coupling) for inv, coupling in zip(inverses, couplings)]
            inverses = [inv - mm(half, inv) for inv, half in zip(inverses, halves)]
        width *= 2
    return inverses


def project_kernel(
    place, x_hbm, wq_hbm, wk_hbm, wv_hbm, wg_hbm, gain_hbm, wb_hbm, bias_hbm, seg_hbm, wo_hbm,
    p_ref, beta_ref, segc_ref, tail_ref, a_hbm, gate_hbm, wb8_hbm, wo_out,
    x_s, weights, gain_s, wb_s, bias_s, seg_s, a_s, gate_s, wb8_s, wo_s, arrived, left,
):
    rows = x_s.shape[0]
    head_width = wq_hbm.shape[1]
    heads = head_width // LANES
    pairs = ((x_hbm, x_s), (gain_hbm, gain_s), (seg_hbm, seg_s), (wb_hbm, wb_s), (bias_hbm, bias_s))
    pairs += ((wo_hbm, wo_s),)
    pairs += tuple(
        (source, weights.at[index]) for index, source in enumerate((wg_hbm, wq_hbm, wk_hbm, wv_hbm))
    )
    copies = [send_out(source, target, arrived, index) for index, (source, target) in enumerate(pairs)]
    for copy in copies[:5]:
        copy.wait()
    wo_copy, *copies = copies[5:]
    segr = seg_s[...].astype(f32)
    wb8_s[...] = jnp.zeros(wb8_s.shape, f32)
    wb8_s[0:heads, :] = wb_s[...].astype(f32)
    leaving = [send_out(wb8_s, wb8_hbm, left, 2)]
    x = x_s[...].astype(f32)
    scale = lax.rsqrt(jnp.mean(x * x, axis=-1, keepdims=True) + 1e-06)
    a = (x * scale * gain_s[...]).astype(bf16)
    a_s[...] = a
    tail_ref[:, 3 * head_width + LANES :] = a.astype(f32)[rows - SUB :, :]
    leaving.append(send_out(a_s, a_hbm, left, 0))
    logits = mm(a, wb8_s[...], 1, 1)
    for head in range(heads):
        column = logits[:, head : head + 1] + bias_s[:, head : head + 1]
        beta_ref[:, head * LANES : (head + 1) * LANES] = sigmoid(
            jnp.broadcast_to(column, (rows, LANES))
        )
    for chunk in range(rows // CHUNK):
        ids = jnp.broadcast_to(segr[chunk : chunk + 1, :], (CHUNK, LANES))
        turned = ids.T
        segc_ref[chunk * CHUNK : (chunk + 1) * CHUNK, :] = turned
        if chunk == rows // CHUNK - 1:
            tail_ref[:, 3 * head_width : 3 * head_width + LANES] = turned[CHUNK - SUB :, :]
    wo_copy.wait()
    leaving.append(send_out(wo_s, wo_out, left, 3))
    copies[0].wait()
    gate_s[...] = mm(a, weights[0])
    leaving.append(send_out(gate_s, gate_hbm, left, 1))
    for part in range(3):
        copies[part + 1].wait()
        value = mm(a, weights[part + 1])
        cols = slice(part * head_width, (part + 1) * head_width)
        low = value.astype(bf16)
        p_ref[:, cols] = low
        tail_ref[:, cols] = low.astype(f32)[rows - SUB :, :]
    for copy in leaving:
        copy.wait()


def lag_masks(joined_ids, lags):
    rows = joined_ids.shape[0] - SUB
    ids = joined_ids[SUB : SUB + rows, :]
    return [None] + [
        jnp.where(joined_ids[SUB - lag : SUB - lag + rows, :] == ids, 1.0, 0.0)
        for lag in range(1, lags + 1)
    ]


def conv_sum(joined, taps_ref, masks, part, head, head_width, rows):
    lags = taps_ref.shape[1] - 1
    col = part * head_width + head * LANES
    tap_cols = slice(head * LANES, (head + 1) * LANES)
    total = taps_ref[part, lags : lags + 1, tap_cols] * joined[SUB : SUB + rows, col : col + LANES]
    for lag in range(1, lags + 1):
        tap = taps_ref[part, lags - lag : lags - lag + 1, tap_cols]
        total = total + tap * joined[SUB - lag : SUB - lag + rows, col : col + LANES] * masks[lag]
    return total


def chunk_flags(joined_ids, chunk):
    start = chunk * CHUNK
    ids = joined_ids[SUB + start : SUB + start + CHUNK, :]
    same = jnp.where(ids == ids.T, 1.0, 0.0)
    before = joined_ids[SUB + start - 1 : SUB + start, :]
    final_id = joined_ids[SUB + start + CHUNK - 1 : SUB + start + CHUNK, :]
    opened = jnp.where(ids == before, 1.0, 0.0)
    closing = jnp.where(ids == final_id, 1.0, 0.0)
    kept = jnp.where(final_id == before, 1.0, 0.0)
    return same, opened, closing, kept


def delta_kernel(
    place, p_ref, tail_ref, taps_ref, segc_ref, beta_ref,
    maps_ref, mix_ref, back_ref, facts_ref, before_ref,
    joined, joined_ids,
):
    rows, width = p_ref.shape
    head_width = width // 3
    heads = head_width // LANES
    chunks = rows // CHUNK
    first = 2 * SUB
    joined[0:SUB, :] = tail_ref[:, :width]
    joined[SUB : SUB + rows, :] = p_ref[...].astype(f32)
    joined_ids[0:SUB, :] = tail_ref[:, width : width + LANES]
    joined_ids[SUB : SUB + rows, :] = segc_ref[...]
    facts_ref[SUB:, 0:head_width] = beta_ref[...]
    facts_ref[0:SUB, 0:head_width] = jnp.zeros((SUB, head_width), f32)
    facts_ref[:, head_width:] = joined_ids[...]
    before_ref[...] = jnp.concatenate(
        [jnp.zeros((SUB, before_ref.shape[1]), f32), tail_ref[:, width + LANES :]], axis=0
    ).astype(bf16)
    back_ref[first:, 0:width] = p_ref[...]
    back_ref[0:first, 0:width] = jnp.concatenate(
        [jnp.zeros((SUB, width), f32), tail_ref[:, :width]], axis=0
    ).astype(bf16)
    back_ref[0:first, width:] = jnp.zeros((first, back_ref.shape[1] - width), bf16)
    masks = lag_masks(joined_ids, taps_ref.shape[1] - 1)
    for part in range(3):
        for head in range(heads):
            total = conv_sum(joined, taps_ref, masks, part, head, head_width, rows)
            z = total * sigmoid(total)
            if part < 2:
                z = z * lax.rsqrt(jnp.sum(z * z, axis=-1, keepdims=True) + 1e-06)
                if part == 0:
                    z = z * Q_SCALE
            col = width + part * head_width + head * LANES
            back_ref[first:, col : col + LANES] = z.astype(bf16)
    row_ids, col_ids = tri_masks()
    flags = [chunk_flags(joined_ids, chunk) for chunk in range(chunks)]
    mix_ref[rows:, :] = jnp.concatenate(
        [jnp.concatenate([flags[min(row, chunks - 1)][3]] * (4 * heads), axis=1) for row in range(2 * SUB)],
        axis=0,
    ).astype(bf16)
    sets = [(head, chunk) for head in range(heads) for chunk in range(chunks)]

    def at_of(head, chunk, part=0):
        col = part * head_width + head * LANES
        return (slice(chunk * CHUNK, (chunk + 1) * CHUNK), slice(col, col + LANES))

    def kept_at(head, chunk, part):
        col = (3 + part) * head_width + head * LANES
        return (slice(first + chunk * CHUNK, first + (chunk + 1) * CHUNK), slice(col, col + LANES))

    lowers = []
    for head, chunk in sets:
        same = flags[chunk][0]
        q, k = back_ref[kept_at(head, chunk, 0)], back_ref[kept_at(head, chunk, 1)]
        inner = mm(jnp.concatenate([q, k], axis=0), k, 1, 1)
        scores = jnp.where(row_ids >= col_ids, inner[:CHUNK] * same, 0.0)
        back_ref[kept_at(head, chunk, 6)] = scores.astype(bf16)
        lowers.append(
            jnp.where(row_ids > col_ids, inner[CHUNK:] * same * beta_ref[at_of(head, chunk)], 0.0)
        )
    inverses = unit_inverses(lowers)
    eye = jnp.where(row_ids == col_ids, 1.0, 0.0).astype(f32)
    maps = [
        jnp.concatenate([eye, jnp.zeros((HEAD_DIM, HEAD_DIM), f32)], axis=1) for _ in range(heads)
    ]
    products = []
    for (head, chunk), inverse in zip(sets, inverses):
        beta = beta_ref[at_of(head, chunk)]
        k = back_ref[kept_at(head, chunk, 1)].astype(f32)
        v = back_ref[kept_at(head, chunk, 2)].astype(f32)
        both = jnp.concatenate([beta * k, beta * v], axis=1)
        products.append(mm(inverse, both))
    steps = {}
    for (head, chunk), inverse, product in zip(sets, inverses, products):
        same, opened, closing, kept = flags[chunk]
        w_rows, u_rows = product[:, :HEAD_DIM], product[:, HEAD_DIM:]
        back_ref[kept_at(head, chunk, 3)] = w_rows.astype(bf16)
        back_ref[kept_at(head, chunk, 4)] = u_rows.astype(bf16)
        back_ref[kept_at(head, chunk, 5)] = inverse.astype(bf16)
        both = jnp.concatenate([opened * w_rows, u_rows], axis=1)
        k = back_ref[kept_at(head, chunk, 1)].astype(f32)
        q = back_ref[kept_at(head, chunk, 0)].astype(f32)
        step = mm(closing * k, both, 0, 0)
        through = mm(back_ref[kept_at(head, chunk, 6)], both)
        mix_ref[at_of(head, chunk, 0)] = (opened * q - through[:, :HEAD_DIM]).astype(bf16)
        mix_ref[at_of(head, chunk, 1)] = step[:, :HEAD_DIM].astype(bf16)
        mix_ref[at_of(head, chunk, 2)] = through[:, HEAD_DIM:].astype(bf16)
        mix_ref[at_of(head, chunk, 3)] = step[:, HEAD_DIM:].astype(bf16)
        steps[head, chunk] = step
    for chunk in range(chunks):
        kept = flags[chunk][3]
        kept_wide = jnp.concatenate([kept, kept], axis=1)
        for head in range(heads):
            step = steps[head, chunk]
            pushed = kept_wide * maps[head] - mm(step[:, :HEAD_DIM], maps[head])
            maps[head] = jnp.concatenate(
                [pushed[:, :HEAD_DIM], pushed[:, HEAD_DIM:] + step[:, HEAD_DIM:]], axis=1
            )
    for head in range(heads):
        maps_ref[head * HEAD_DIM : (head + 1) * HEAD_DIM, :] = maps[head][:, :HEAD_DIM].astype(bf16)
        base = (heads + head) * HEAD_DIM
        maps_ref[base : base + HEAD_DIM, :] = maps[head][:, HEAD_DIM:].astype(bf16)


def park_kernel(count, place, *refs):
    sources, targets, left = refs[:count], refs[count : 2 * count], refs[-1]
    copies = []
    for index, (source, target) in enumerate(zip(sources, targets)):
        if source.shape != target.shape:
            source = source.at[:, 0 : target.shape[1]]
        copies.append(send_out(source, target, left, index))
    for copy in copies:
        copy.wait()


def park(chain, *pairs, name):
    arrays = [value.value if isinstance(value, Free) else value for value, _ in pairs]
    return kernel_call(
        functools.partial(park_kernel, len(pairs)),
        [
            Direct((array.shape[0], array.shape[1] if cols is None else cols), array.dtype)
            for array, (_, cols) in zip(arrays, pairs)
        ],
        chain,
        *[value for value, _ in pairs],
        scratch=(pltpu.SemaphoreType.DMA((len(pairs),)),),
        name=name,
    )


def scan_round_kernel(bit, place, own_ref, other_ref, prefix_ref, pack_ref, total_ref, prefix_out, pack_out):
    upper = bit_of(place, 0, bit)
    half = own_ref.shape[0] // 2
    heads = half // HEAD_DIM
    base = 2 * half * bit
    if bit:
        pack_out[0:base, :] = pack_ref[...]
    for head in range(heads):
        m_at = slice(head * HEAD_DIM, (head + 1) * HEAD_DIM)
        a_at = slice((heads + head) * HEAD_DIM, (heads + head + 1) * HEAD_DIM)
        low_at = slice(base + head * HEAD_DIM, base + (head + 1) * HEAD_DIM)
        suffix_at = slice(base + half + head * HEAD_DIM, base + half + (head + 1) * HEAD_DIM)
        own_m, own_a = own_ref[m_at, :].astype(f32), own_ref[a_at, :].astype(f32)
        other_m, other_a = other_ref[m_at, :].astype(f32), other_ref[a_at, :].astype(f32)
        high_m, high_a = chosen(upper, own_m, other_m), chosen(upper, own_a, other_a)
        low_m, low_a = chosen(upper, other_m, own_m), chosen(upper, other_a, own_a)
        pack_out[low_at, :] = low_m.astype(bf16)
        total = mm(high_m, jnp.concatenate([low_m, low_a], axis=1))
        added_part = (total[:, HEAD_DIM:] + high_a).astype(bf16)
        if total_ref.shape[0] == own_ref.shape[0]:
            total_ref[m_at, :] = total[:, :HEAD_DIM].astype(bf16)
            total_ref[a_at, :] = added_part
        else:
            total_ref[m_at, :] = added_part
        if bit == 0:
            rows, cols = tri_masks()
            eye = jnp.where(rows == cols, 1.0, 0.0).astype(f32)
            prefix_out[m_at, :] = chosen(upper, other_m, eye).astype(bf16)
            prefix_out[a_at, :] = chosen(upper, other_a, jnp.zeros_like(other_a)).astype(bf16)
            pack_out[suffix_at, :] = chosen(upper, eye, other_m.T).astype(bf16)
        else:
            before_m, before_a = prefix_ref[m_at, :].astype(f32), prefix_ref[a_at, :].astype(f32)
            at = base - half + head * HEAD_DIM
            after_m = pack_ref[at : at + HEAD_DIM, :].astype(f32)
            joint = mm(before_m, jnp.concatenate([other_m, other_a], axis=1))
            prefix_out[m_at, :] = chosen(upper, joint[:, :HEAD_DIM], before_m).astype(bf16)
            prefix_out[a_at, :] = chosen(
                upper, joint[:, HEAD_DIM:] + before_a, before_a
            ).astype(bf16)
            pack_out[suffix_at, :] = chosen(upper, after_m, mm(after_m, other_m, 1, 1)).astype(bf16)


def back_round_kernel(bit, place, pack_ref, own_ref, other_ref, after_ref, total_ref, after_out):
    upper = bit_of(place, 0, bit)
    half = own_ref.shape[0]
    base = 2 * half * bit
    for head in range(half // HEAD_DIM):
        at = slice(head * HEAD_DIM, (head + 1) * HEAD_DIM)
        own, other = own_ref[at, :].astype(f32), other_ref[at, :].astype(f32)
        high, low = chosen(upper, own, other), chosen(upper, other, own)
        low_m = pack_ref[base + head * HEAD_DIM : base + (head + 1) * HEAD_DIM, :]
        total_ref[at, :] = (mm(low_m, high, 0, 0) + low).astype(bf16)
        if bit == 0:
            after_out[at, :] = chosen(upper, jnp.zeros_like(other), other).astype(bf16)
        else:
            start = base - half + head * HEAD_DIM
            suffix_m = pack_ref[start : start + HEAD_DIM, :]
            after = after_ref[at, :].astype(f32)
            after_out[at, :] = chosen(upper, after, mm(suffix_m, other) + after).astype(bf16)


def mixer_kernel(
    last_bit, place, prefix_ref, other_a_ref, mix_ref, gate_ref, hgain_ref,
    y_ref, o_ref, keep_ref,
):
    rows, head_width = gate_ref.shape
    heads = head_width // LANES
    upper = bit_of(place, 0, last_bit)
    kept_rows = mix_ref[rows:, 0:LANES].astype(f32)
    for head in range(heads):
        m_at = slice(head * HEAD_DIM, (head + 1) * HEAD_DIM)
        a_at = slice((heads + head) * HEAD_DIM, (heads + head + 1) * HEAD_DIM)
        before_m, before_a = prefix_ref[m_at, :], prefix_ref[a_at, :].astype(f32)
        state = chosen(upper, mm(before_m, other_a_ref[m_at, :]) + before_a, before_a)
        for chunk in range(rows // CHUNK):
            chunk_rows = slice(chunk * CHUNK, (chunk + 1) * CHUNK)
            cols = [
                slice(part * head_width + head * LANES, part * head_width + (head + 1) * LANES)
                for part in range(4)
            ]
            at = (chunk_rows, cols[0])
            low = state.astype(bf16)
            keep_ref[at] = low
            out = mm(mix_ref[at], low) + mix_ref[chunk_rows, cols[2]].astype(f32)
            o_ref[at] = out
            state = (
                kept_rows[chunk : chunk + 1, :] * state
                - mm(mix_ref[chunk_rows, cols[1]], low)
                + mix_ref[chunk_rows, cols[3]].astype(f32)
            )
            gate = gate_ref[at]
            scale = lax.rsqrt(jnp.mean(out * out, axis=-1, keepdims=True) + 1e-05)
            y = (out * scale * hgain_ref[...] * (gate * sigmoid(gate))).astype(bf16)
            y_ref[at] = y
            keep_ref[chunk_rows, cols[1]] = y


def ffn_kernel(
    axis, down_bits, gate_bits, place, x_ref, g_ref, fgain_ref, wg_ref, wu_ref, wd_ref, *rest,
):
    (
        *parts, send_ref, down_send, gate_send, h_hbm, hid_hbm, keep_hbm, down_hbm, gate_hbm, up_hbm,
        h_s, hid_s, keep_s, down_keep, gate_keep, grad_s, up_s, whole, left,
    ) = rest
    y_refs, wo_refs = parts[: len(parts) // 2], parts[len(parts) // 2 :]
    att = None
    for y_ref, wo_ref in zip(y_refs, wo_refs):
        part = mm(y_ref[...], wo_ref[...])
        att = part if att is None else att + part
    h = x_ref[...].astype(f32) + att
    h_s[...] = h
    leaving = [send_out(h_s, h_hbm, left, 0)]
    scale = lax.rsqrt(jnp.mean(h * h, axis=-1, keepdims=True) + 1e-06)
    b = (h * scale * fgain_ref[...]).astype(bf16)
    gate = mm(b, wg_ref[...], 1, 1)
    up = mm(b, wu_ref[...], 1, 1)
    sg = sigmoid(gate)
    act = gate * sg
    hid = (act * up).astype(bf16)
    hid_s[...] = hid
    leaving.append(send_out(hid_s, hid_hbm, left, 2))
    dhid = mm(g_ref[...], wd_ref[...], 1, 1)
    dgate = (dhid * up * (sg * (1.0 + gate * (1.0 - sg)))).astype(bf16)
    dup = (dhid * act).astype(bf16)

    def grad_of(by_units, by_model, out):
        if axis:
            out[...] = mm(by_units, by_model, 0, 0).astype(bf16)
            return
        units = by_units.shape[1]
        if out.shape[1] > units:
            out[:, units:] = jnp.zeros((out.shape[0], out.shape[1] - units), bf16)
        out[:, :units] = mm(by_model, by_units, 0, 0).astype(bf16)

    grad_of(hid, g_ref[...], grad_s)
    emit_shares(place, down_bits, grad_s, down_keep, down_send, axis)
    leaving.append(send_out(down_keep, down_hbm, left, 1))
    grad_of(dgate, b, grad_s)
    emit_shares(place, gate_bits, grad_s, gate_keep, gate_send, axis)
    leaving.append(send_out(gate_keep, gate_hbm, left, 4))
    grad_of(dup, b, up_s)
    leaving.append(send_out(up_s, up_hbm, left, 5))
    whole[...] = mm(dgate, wg_ref[...]) + mm(dup, wu_ref[...])
    split_rows(place, whole, keep_s, send_ref)
    leaving.append(send_out(keep_s, keep_hbm, left, 3))
    for copy in leaving:
        copy.wait()


def split_rows(place, whole, keep_ref, send_ref):
    half = whole.shape[0] // 2
    core = bit_of(place, 1, 0)
    keep_ref[0:half, :] = whole[pl.ds(pl.multiple_of(core * half, half), half), :].astype(bf16)
    send_ref[0:half, :] = whole[pl.ds(pl.multiple_of((1 - core) * half, half), half), :].astype(bf16)


def join_rows(place, mine, theirs, whole):
    half = whole.shape[0] // 2
    core = bit_of(place, 1, 0)
    mine, theirs = mine[:half], theirs[:half]
    whole[pl.ds(pl.multiple_of(core * half, half), half), :] = mine
    whole[pl.ds(pl.multiple_of((1 - core) * half, half), half), :] = theirs


def emit_shares(place, bits, whole, keep_ref, send_ref, axis=0):
    order = [0]
    for bit in reversed(bits[1:]):
        order = order + [relative | (1 << bit) for relative in order]
    block = whole.shape[axis] // (2 * len(order))
    for index, relative in enumerate(order):
        for ref, first in ((keep_ref, 0), (send_ref, 1 << bits[0])):
            owner = lax.bitwise_xor(place[0], jnp.int32(relative | first))
            source = pl.ds(pl.multiple_of(owner * block, block), block)
            target = slice(index * block, (index + 1) * block)
            if axis:
                ref[:, target] = whole[:, source]
            else:
                ref[target, :] = whole[source, :]


def share_round_kernel(axis, place, keep_ref, got_ref, keep_out, send_out):
    half = keep_out.shape[axis]
    for at, ref in ((slice(0, half), keep_out), (slice(half, 2 * half), send_out)):
        if axis:
            ref[...] = keep_ref[:, at] + got_ref[:, at]
        else:
            ref[...] = keep_ref[at] + got_ref[at]


def out_part_kernel(place, hid_ref, wd_ref, keep_ref, send_ref, whole):
    whole[...] = mm(hid_ref[...], wd_ref[...])
    split_rows(place, whole, keep_ref, send_ref)


def emit_kernel(axis, bits, place, whole, keep_ref, send_ref):
    emit_shares(place, bits, whole, keep_ref, send_ref, axis)


def early_grads_kernel(
    bits, place, gh_ref, y_ref, a_ref, dgr_ref, gq_ref, halo_ref, before_ref,
    keep_ref, send_ref, whole,
):
    width = dgr_ref.shape[1]
    whole[:, :width] = mm(gh_ref[...], y_ref[:, width:], 0, 0).astype(bf16)
    whole[:, width : 2 * width] = mm(a_ref[...], dgr_ref[...], 0, 0).astype(bf16)
    edge = jnp.concatenate([jnp.zeros((SUB, width), f32), halo_ref[...]], axis=0)
    whole[:, 2 * width :] = (
        mm(a_ref[...], gq_ref[...], 0, 0) + mm(before_ref[...], edge, 0, 0)
    ).astype(bf16)
    emit_shares(place, bits, whole, keep_ref, send_ref)


def early_sum_kernel(place, keep_ref, got_ref, turned_ref, gate_ref, query_ref):
    total = keep_ref[...].astype(f32) + got_ref[...].astype(f32)
    width = gate_ref.shape[1]
    turned_ref[...] = total[:, :width].T
    gate_ref[...] = total[:, width : 2 * width]
    query_ref[...] = total[:, 2 * width :]


def ffn_share_kernel(axis, place, keep_ref, got_ref, out_ref):
    total = keep_ref[...].astype(f32) + got_ref[...].astype(f32)
    out_ref[...] = total if axis else total.T[: out_ref.shape[0], :]


def residual_back_kernel(
    place, mine, theirs, h_ref, g_ref, fgain_ref, wo_ref, o_ref,
    gate_ref, hgain_ref, steps_ref,
    gh_ref, pull_ref, dh_ref, do_ref, dgr_ref, sums_ref, whole,
):
    rows, head_width = o_ref.shape
    heads = head_width // LANES
    join_rows(place, mine[...].astype(f32), theirs[...].astype(f32), whole)
    h = h_ref[...]
    db = whole[...]
    scale = lax.rsqrt(jnp.mean(h * h, axis=-1, keepdims=True) + 1e-06)
    hat = h * scale
    prod = db * hat
    sums_ref[...] = jnp.zeros(sums_ref.shape, f32)
    sums_ref[0:1, :] = jnp.sum(prod, axis=0, keepdims=True)
    inner = jnp.mean(prod * fgain_ref[...], axis=-1, keepdims=True)
    dh = g_ref[...].astype(f32) + scale * (db * fgain_ref[...] - hat * inner)
    dh_ref[...] = dh
    gh = dh.astype(bf16)
    gh_ref[...] = gh
    dy_all = mm(gh, wo_ref[...], 1, 1)
    hg_sum = jnp.zeros((1, LANES), f32)
    for head in range(heads):
        cols = slice(head * LANES, (head + 1) * LANES)
        out, gate, dy = o_ref[:, cols], gate_ref[:, cols], dy_all[:, cols]
        norm = lax.rsqrt(jnp.mean(out * out, axis=-1, keepdims=True) + 1e-05)
        hat_o = out * norm
        sg = sigmoid(gate)
        act = gate * sg
        hg_sum = hg_sum + jnp.sum(dy * hat_o * act, axis=0, keepdims=True)
        dgain = dy * hgain_ref[...]
        dgr_ref[:, cols] = (dgain * hat_o * (sg * (1.0 + gate * (1.0 - sg)))).astype(bf16)
        e = dgain * act
        do_ref[:, cols] = (norm * (e - hat_o * jnp.mean(e * hat_o, axis=-1, keepdims=True))).astype(bf16)
    sums_ref[1:2, 0:LANES] = hg_sum
    chunks = rows // CHUNK
    kept_rows = steps_ref[rows:, 0:LANES].astype(f32)
    pulls = [None] * heads
    for chunk in range(chunks - 1, -1, -1):
        chunk_rows = slice(chunk * CHUNK, (chunk + 1) * CHUNK)
        for head in range(heads):
            cols = slice(head * LANES, (head + 1) * LANES)
            map_cols = slice(head_width + head * LANES, head_width + (head + 1) * LANES)
            local = mm(steps_ref[chunk_rows, cols], do_ref[chunk_rows, cols], 0, 0)
            if pulls[head] is not None:
                local = (
                    local
                    + kept_rows[chunk : chunk + 1, :] * pulls[head]
                    - mm(steps_ref[chunk_rows, map_cols], pulls[head], 0, 0)
                )
            pulls[head] = local
    for head in range(heads):
        pull_ref[head * HEAD_DIM : (head + 1) * HEAD_DIM, :] = pulls[head].astype(bf16)


def back_places(head_width):
    def at_of(head, chunk, part=0):
        col = part * head_width + head * LANES
        return (slice(chunk * CHUNK, (chunk + 1) * CHUNK), slice(col, col + LANES))

    def kept_at(head, chunk, part):
        col = (3 + part) * head_width + head * LANES
        start = 2 * SUB + chunk * CHUNK
        return (slice(start, start + CHUNK), slice(col, col + LANES))

    return at_of, kept_at


def fill_joined(back_ref, facts_ref, joined, joined_ids, head_width):
    width = 3 * head_width
    joined[0:SUB, :] = back_ref[0 : 2 * SUB, :width].astype(f32)[SUB:, :]
    joined[SUB:, :] = back_ref[2 * SUB :, :width].astype(f32)
    joined_ids[...] = facts_ref[:, head_width : head_width + LANES]


def fill_lag_masks(masks, mask_s, du_s):
    rows = mask_s.shape[1] - 2 * SUB
    du_s[0:SUB, :] = jnp.zeros((SUB, LANES), f32)
    du_s[SUB + rows :, :] = jnp.zeros((SUB, LANES), f32)
    for lag in range(1, len(masks)):
        mask_s[lag - 1, 0:SUB, :] = jnp.zeros((SUB, LANES), f32)
        mask_s[lag - 1, SUB : SUB + rows, :] = masks[lag]
        mask_s[lag - 1, SUB + rows :, :] = jnp.zeros((SUB, LANES), f32)


def conv_back(taps_ref, joined, masks, mask_s, du_s, part, head, head_width, rows, grad):
    lags = len(masks) - 1
    col = part * head_width + head * LANES
    cols = slice(col, col + LANES)
    tap_cols = slice(head * LANES, (head + 1) * LANES)
    total = conv_sum(joined, taps_ref, masks, part, head, head_width, rows)
    sg = sigmoid(total)
    if part < 2:
        z = total * sg
        norm = lax.rsqrt(jnp.sum(z * z, axis=-1, keepdims=True) + 1e-06)
        hat = z * norm
        grad = norm * (grad - hat * jnp.sum(grad * hat, axis=-1, keepdims=True))
        if part == 0:
            grad = grad * Q_SCALE
    grad = grad * (sg * (1.0 + total * (1.0 - sg)))
    du_s[SUB : SUB + rows, :] = grad
    before = taps_ref[part, lags : lags + 1, tap_cols] * grad
    halo = jnp.zeros((SUB, LANES), f32)
    tap_grads = [None] * (lags + 1)
    tap_grads[lags] = jnp.sum(grad * joined[SUB : SUB + rows, cols], axis=0, keepdims=True)
    for lag in range(1, lags + 1):
        tap = taps_ref[part, lags - lag : lags - lag + 1, tap_cols]
        tap_grads[lags - lag] = jnp.sum(
            grad * joined[SUB - lag : SUB - lag + rows, cols] * masks[lag], axis=0, keepdims=True
        )
        moved = du_s[SUB + lag : SUB + lag + rows, :]
        before = before + tap * moved * mask_s[lag - 1, SUB + lag : SUB + lag + rows, :]
        halo = halo + tap * du_s[lag : lag + SUB, :] * mask_s[lag - 1, lag : lag + SUB, :]
    return before, halo, tap_grads


def delta_query_kernel(
    place, taps_ref, back_ref, facts_ref, keep_ref, do_ref,
    pre_ref, dk_ref, gq_ref, halo_ref, small_ref,
    joined, joined_ids, dq_s, du_s, mask_s,
):
    rows, head_width = do_ref.shape
    heads = head_width // LANES
    chunks = rows // CHUNK
    fill_joined(back_ref, facts_ref, joined, joined_ids, head_width)
    masks = lag_masks(joined_ids, taps_ref.shape[1] - 1)
    row_ids, col_ids = tri_masks()
    flags = [chunk_flags(joined_ids, chunk) for chunk in range(chunks)]
    at_of, kept_at = back_places(head_width)
    for head in range(heads):
        for chunk in range(chunks):
            same, opened, closing, kept = flags[chunk]
            at = at_of(head, chunk)
            q, k, w_rows, u_rows, scores = (
                back_ref[kept_at(head, chunk, part)] for part in (0, 1, 3, 4, 6)
            )
            state, do = keep_ref[at], do_ref[at]
            fresh = (u_rows.astype(f32) - opened * mm(w_rows, state)).astype(bf16)
            pre_ref[at] = fresh
            pre_ref[at_of(head, chunk, 1)] = mm(scores, do, 0, 0).astype(bf16)
            dscore = jnp.where(row_ids >= col_ids, mm(do, fresh, 1, 1) * same, 0.0).astype(bf16)
            dq_s[at] = opened * mm(do, state, 1, 1) + mm(dscore, k)
            dk_ref[at] = mm(dscore, q, 0, 0)
    fill_lag_masks(masks, mask_s, du_s)
    small_ref[...] = jnp.zeros(small_ref.shape, f32)
    for head in range(heads):
        cols = slice(head * LANES, (head + 1) * LANES)
        gq_ref[:, cols], halo_ref[:, cols], tap_grads = conv_back(
            taps_ref, joined, masks, mask_s, du_s, 0, head, head_width, rows, dq_s[:, cols]
        )
        for row, tap_grad in enumerate(tap_grads):
            small_ref[row : row + 1, cols] = tap_grad


def delta_back_kernel(
    last_bit, place, taps_ref, back_ref, facts_ref, steps_ref, keep_ref, do_ref, pre_ref, dk_ref,
    pack_ref, after_ref, other_ref,
    gp_ref, halo_ref, small_ref,
    joined, joined_ids, dk_s, du_s, mask_s,
):
    rows, head_width = do_ref.shape
    width = 2 * head_width
    heads = head_width // LANES
    chunks = rows // CHUNK
    fill_joined(back_ref, facts_ref, joined, joined_ids, head_width)
    masks = lag_masks(joined_ids, taps_ref.shape[1] - 1)
    row_ids, col_ids = tri_masks()
    flags = [chunk_flags(joined_ids, chunk) for chunk in range(chunks)]
    upper = bit_of(place, 0, last_bit)
    sets = [(head, chunk) for head in range(heads) for chunk in range(chunks)]
    at_of, kept_at = back_places(head_width)
    state_grads = {}
    for head in range(heads):
        at = slice(head * HEAD_DIM, (head + 1) * HEAD_DIM)
        after = after_ref[at, :].astype(f32)
        start = pack_ref.shape[0] - after_ref.shape[0] + head * HEAD_DIM
        suffix_m = pack_ref[start : start + HEAD_DIM, :]
        grad = chosen(upper, after, mm(suffix_m, other_ref[at, :]) + after)
        for chunk in range(chunks - 1, -1, -1):
            state_grads[head, chunk] = grad
            if chunk:
                low = grad.astype(bf16)
                grad = (
                    flags[chunk][3] * grad
                    - mm(steps_ref[at_of(head, chunk, 1)], low, 0, 0)
                    + mm(steps_ref[at_of(head, chunk)], do_ref[at_of(head, chunk)], 0, 0)
                )
    lane_ids = lax.broadcasted_iota(jnp.int32, (CHUNK, LANES), 1)
    gb_cols = [jnp.zeros((CHUNK, LANES), f32) for _ in range(chunks)]
    for head, chunk in sets:
        same, opened, closing, kept = flags[chunk]
        at = at_of(head, chunk)
        k, v, w_rows, u_rows, inverse = (
            back_ref[kept_at(head, chunk, part)] for part in (1, 2, 3, 4, 5)
        )
        kf, vf = k.astype(f32), v.astype(f32)
        beta = facts_ref[
            SUB + chunk * CHUNK : SUB + (chunk + 1) * CHUNK, head * LANES : (head + 1) * LANES
        ]
        state = keep_ref[at]
        sgrad = state_grads[head, chunk].astype(bf16)
        fresh = pre_ref[at]
        dfresh = pre_ref[at_of(head, chunk, 1)].astype(f32) + mm(closing * kf, sgrad)
        dw = -(opened * mm(dfresh, state, 1, 1))
        dx = mm(inverse, jnp.concatenate([dfresh, dw], axis=1), 0, 0)
        dxv, dxk = dx[:, :HEAD_DIM], dx[:, HEAD_DIM:]
        dlow = mm(dx, jnp.concatenate([u_rows, w_rows], axis=1), 1, 1)
        dlow = jnp.where(row_ids > col_ids, -dlow * same, 0.0)
        inner = mm(k, k, 1, 1)
        dbeta = jnp.sum(dxv * vf + dxk * kf + dlow * inner, axis=-1, keepdims=True)
        glow = (dlow * beta).astype(bf16)
        dk_s[at_of(head, chunk, 0)] = (
            beta * dxk
            + dk_ref[at]
            + closing * mm(fresh, sgrad, 1, 1)
            + mm(glow, k)
            + mm(glow, k, 0, 0)
        )
        dk_s[at_of(head, chunk, 1)] = beta * dxv
        raw = jnp.broadcast_to(dbeta, (CHUNK, LANES)) * beta * (1.0 - beta)
        gb_cols[chunk] = jnp.where(lane_ids == head, raw, gb_cols[chunk])
    bias_sum = jnp.zeros((1, LANES), f32)
    for chunk in range(chunks):
        gp_ref[chunk * CHUNK : (chunk + 1) * CHUNK, width:] = gb_cols[chunk]
        bias_sum = bias_sum + jnp.sum(gb_cols[chunk], axis=0, keepdims=True)
    small_ref[...] = jnp.zeros(small_ref.shape, f32)
    tap_count = len(masks)
    small_ref[2 * tap_count : 2 * tap_count + 1, 0:LANES] = bias_sum
    fill_lag_masks(masks, mask_s, du_s)
    for part in (1, 2):
        for head in range(heads):
            col = (part - 1) * head_width + head * LANES
            cols = slice(col, col + LANES)
            gp_ref[:, cols], halo_ref[:, cols], tap_grads = conv_back(
                taps_ref, joined, masks, mask_s, du_s, part, head, head_width, rows, dk_s[:, cols]
            )
            for tap, tap_grad in enumerate(tap_grads):
                row = (part - 1) * tap_count + tap
                small_ref[row : row + 1, head * LANES : (head + 1) * LANES] = tap_grad


def input_back_kernel(
    place, gp_ref, halo_ref, gq_ref, qhalo_ref, dgr_ref, wq_ref, wk_ref, wv_ref, wg_ref, wb_ref,
    x_ref, gain_ref, before_ref, sums_ref, whole, edge_ref, rows_ref,
):
    width = halo_ref.shape[1]
    head_width = width // 2
    zeros = jnp.zeros((SUB, head_width), f32)
    total = mm(dgr_ref[...], wg_ref[...], 1, 1) + mm(gp_ref[:, width : width + SUB], wb_ref[...])
    edge = None
    first, second = slice(0, head_width), slice(head_width, width)
    for grads, halo, w_ref in (
        (gq_ref[...], qhalo_ref[...], wq_ref),
        (gp_ref[:, first], halo_ref[:, first], wk_ref),
        (gp_ref[:, second], halo_ref[:, second], wv_ref),
    ):
        total = total + mm(grads, w_ref[...], 1, 1)
        piece = mm(jnp.concatenate([zeros, halo], axis=0), w_ref[...], 1, 1)
        edge = piece if edge is None else edge + piece
    whole[...] = total
    edge_ref[...] = edge[SUB:, :]
    x = x_ref[...].astype(f32)
    scale = lax.rsqrt(jnp.mean(x * x, axis=-1, keepdims=True) + 1e-06)
    hat_before = before_ref[...].astype(f32) / gain_ref[...]
    rows_ref[...] = jnp.zeros(rows_ref.shape, f32)
    rows_ref[0:1, :] = jnp.sum(total * (x * scale), axis=0, keepdims=True) + jnp.sum(
        edge * hat_before, axis=0, keepdims=True
    )
    rows_ref[1:2, :] = sums_ref[1:2, :]


def input_split_kernel(place, whole_ref, next_ref, keep_ref, send_ref, whole):
    rows = whole.shape[0]
    whole[...] = whole_ref[...]
    whole[rows - SUB :, :] = whole[rows - SUB :, :] + next_ref[...]
    split_rows(place, whole, keep_ref, send_ref)


def small_places(model, taps, heads, width):
    sizes = [model, LANES, model, 3 * taps * heads * LANES, heads * model, LANES]
    starts = [0]
    for size in sizes:
        starts.append(starts[-1] + size // LANES)
    across = width // LANES
    rows = -(-starts[-1] // across)
    return starts[:-1], -(-rows // (2 * SUB)) * 2 * SUB


def piece_at(index, width):
    across = width // LANES
    col = index % across * LANES
    return (slice(index // across, index // across + 1), slice(col, col + LANES))


def project_grads_kernel(
    bits, taps, place, a_ref, before_ref, gp_ref, halo_ref, sums_a, qsmall_ref, gsmall_ref, head_rows,
    keep_ref, send_ref, whole, small,
):
    a = a_ref[...]
    model = a.shape[1]
    width = whole.shape[1]
    heads = width // (2 * LANES)
    starts, _ = small_places(model, taps, heads, width)
    small[...] = jnp.zeros(small.shape, f32)
    beta_rows = mm(gp_ref[:, width:], a, 0, 0)
    pieces = model // LANES
    for piece in range(pieces):
        cols = slice(piece * LANES, (piece + 1) * LANES)
        small[piece_at(starts[0] + piece, width)] = head_rows[0:1, cols]
        small[piece_at(starts[2] + piece, width)] = sums_a[0:1, cols]
        for head in range(heads):
            small[piece_at(starts[4] + head * pieces + piece, width)] = beta_rows[head : head + 1, cols]
    for row in range(3 * taps):
        ref, at = (qsmall_ref, row) if row < taps else (gsmall_ref, row - taps)
        for head in range(heads):
            small[piece_at(starts[3] + row * heads + head, width)] = ref[
                at : at + 1, head * LANES : (head + 1) * LANES
            ]
    small[piece_at(starts[1], width)] = head_rows[1:2, 0:LANES]
    small[piece_at(starts[5], width)] = gsmall_ref[2 * taps : 2 * taps + 1, 0:LANES]
    edge = jnp.concatenate([jnp.zeros((SUB, width), f32), halo_ref[...]], axis=0)
    whole[...] = (mm(a, gp_ref[:, :width], 0, 0) + mm(before_ref[...], edge, 0, 0)).astype(bf16)
    emit_shares(place, bits, whole, keep_ref, send_ref)
    keep_ref[model // 2 :, :] = small[...].astype(bf16)
    send_ref[model // 2 :, :] = small[...].astype(bf16)


def share_small_kernel(place, keep_ref, got_ref, keep_out, send_out_ref):
    extra = 2 * keep_out.shape[0] - keep_ref.shape[0]
    half = keep_out.shape[0] - extra
    small = keep_ref[2 * half :, :] + got_ref[2 * half :, :]
    keep_out[0:half, :] = keep_ref[0:half, :] + got_ref[0:half, :]
    send_out_ref[0:half, :] = keep_ref[half : 2 * half, :] + got_ref[half : 2 * half, :]
    keep_out[half:, :] = small
    send_out_ref[half:, :] = small


def project_sum_kernel(
    taps, place, keep_ref, got_ref, k_ref, v_ref,
    norm_ref, hgain_ref, fgain_ref, taps_ref, beta_ref, bias_ref, small, rows_s,
):
    share, head_width = k_ref.shape
    width = 2 * head_width
    heads = head_width // LANES
    total = keep_ref[...].astype(f32) + got_ref[...].astype(f32)
    for index, out_ref in enumerate((k_ref, v_ref)):
        out_ref[...] = total[:share, index * head_width : (index + 1) * head_width]
    small[...] = total[share:, :]
    model = norm_ref.shape[1]
    starts, _ = small_places(model, taps, heads, width)
    pieces = model // LANES
    for piece in range(pieces):
        cols = slice(piece * LANES, (piece + 1) * LANES)
        norm_ref[0:1, cols] = small[piece_at(starts[0] + piece, width)]
        fgain_ref[0:1, cols] = small[piece_at(starts[2] + piece, width)]
        for head in range(heads):
            row = small[piece_at(starts[4] + head * pieces + piece, width)]
            rows_s[head * pieces + piece : head * pieces + piece + 1, :] = row
    hgain_ref[...] = small[piece_at(starts[1], width)]
    for part in range(3):
        for tap in range(taps):
            for head in range(heads):
                taps_ref[part, tap : tap + 1, head * LANES : (head + 1) * LANES] = small[
                    piece_at(starts[3] + (part * taps + tap) * heads + head, width)
                ]
    bias_ref[...] = small[piece_at(starts[5], width)][:, : bias_ref.shape[1]]
    if share % LANES:
        for head in range(heads):
            for piece in range(pieces):
                at = head * pieces + piece
                beta_ref[head : head + 1, piece * LANES : (piece + 1) * LANES] = rows_s[at : at + 1, :]
    else:
        for head in range(heads):
            for piece in range(share // LANES):
                at = head * pieces + place[0] * (share // LANES) + piece
                beta_ref[head : head + 1, piece * LANES : (piece + 1) * LANES] = rows_s[pl.ds(at, 1), :]


def input_grad_kernel(place, mine, theirs, x_ref, gain_ref, dh_ref, out_ref, whole):
    join_rows(place, mine[...].astype(f32), theirs[...].astype(f32), whole)
    x = x_ref[...].astype(f32)
    scale = lax.rsqrt(jnp.mean(x * x, axis=-1, keepdims=True) + 1e-06)
    hat = x * scale
    grad = whole[...] * gain_ref[...]
    inner = jnp.mean(grad * hat, axis=-1, keepdims=True)
    out_ref[...] = dh_ref[...] + scale * (grad - hat * inner)


def output_kernel(place, mine, theirs, h_ref, out_ref, whole):
    join_rows(place, mine[...].astype(f32), theirs[...].astype(f32), whole)
    out_ref[...] = (h_ref[...] + whole[...]).astype(bf16)


def add_kernel(place, left_ref, right_ref, out_ref):
    out_ref[...] = (left_ref[...].astype(f32) + right_ref[...].astype(f32)).astype(out_ref.dtype)


def added(chain, left, right):
    shape = left.value.shape if isinstance(left, Free) else left.shape
    (out,) = kernel_call(
        add_kernel, (shaped(shape, right.dtype),), chain, left, right, name="added"
    )
    return out


def gathered(value):
    count = lax.axis_size("head")
    blocks = [value]
    bit = 2
    while bit < count:
        blocks = blocks + [swap(block, "head", bit) for block in blocks]
        bit *= 2
    return blocks + [swap(block, "head", 1) for block in blocks]


class Shares:
    def __init__(self, keep, send, bits, axis=0):
        self.keep, self.bits, self.axis = keep, list(bits), axis
        self.got = swap(send, "seq", 1 << self.bits.pop(0))

    def step(self, chain):
        half = list(self.got.shape)
        half[self.axis] //= 2
        self.keep, send = kernel_call(
            functools.partial(share_round_kernel, self.axis),
            (shaped(half, bf16), shaped(half, bf16)),
            chain, self.keep, self.got, name="share_round",
        )
        self.got = swap(send, "seq", 1 << self.bits.pop(0))

    def until(self, chain, left):
        while len(self.bits) > left:
            self.step(chain)

    def pair(self, chain):
        self.until(chain, 0)
        return self.keep, self.got


def head_rounds(chain, value):
    count = lax.axis_size("head")
    bit = 1
    while bit < count:
        value = added(chain, value, swap(value, "head", bit))
        bit *= 2
    return value


def body(
    block_input, cotangent, segment_ids, norm_gain, w_query, w_key, w_value, w_gate, w_beta,
    beta_bias, conv_weight, head_gain, w_out, ffn_gain, w_ffn_gate, w_ffn_up, w_ffn_down,
):
    rows, model = block_input.shape
    heads = w_beta.shape[1]
    head_width = w_query.shape[1]
    ffn_width = w_ffn_gate.shape[1]
    taps = conv_weight.shape[1]
    seq_count = lax.axis_size("seq")
    rounds = seq_count.bit_length() - 1
    share = model // seq_count
    width = 3 * head_width
    chunks = rows // CHUNK
    y_first = list(range(rounds))
    y_last = y_first[1:] + y_first[:1]
    y_next = y_first[1:2] + y_first[:1] + y_first[2:]
    by_plan = {"first": y_first, "last": y_last, "next": y_next}
    down_bits, gate_bits, up_bits, early_bits, project_bits = (
        by_plan[PLANS[key]] for key in ("down", "gate", "up", "early", "project")
    )

    chain = Chain()

    def ffn_share(chain, pair):
        return kernel_call(
            functools.partial(ffn_share_kernel, ffn_axis),
            (final((ffn_width, share), f32),), chain, *pair, name="ffn_share",
        )

    bias_in = beta_bias[None] if heads > 1 else jnp.broadcast_to(beta_bias[None], (1, 2))
    gain_row, fgain_row, hgain_row = Free(norm_gain[None]), Free(ffn_gain[None]), Free(head_gain[None])
    taps_in = Free(conv_weight)

    square = (rows, head_width)
    p, beta, seg_cols, tail, a, gate_raw, w_beta8, w_out_copy = kernel_call(
        project_kernel,
        (
            shaped((rows, width), bf16),
            shaped(square, f32),
            shaped((rows, LANES), f32),
            shaped((SUB, width + LANES + model), f32),
            Direct((rows, model), bf16),
            Direct(square, f32),
            Direct((SUB, model), f32),
            Direct(w_out.shape, bf16),
        ),
        chain, Far(block_input), Far(w_query), Far(w_key), Far(w_value), Far(w_gate),
        Far(norm_gain[None]), Far(w_beta.T), Far(bias_in),
        Far(segment_ids.reshape(chunks, LANES)), Far(w_out),
        scratch=(
            pltpu.VMEM((rows, model), bf16),
            pltpu.VMEM((4, model, head_width), bf16),
            pltpu.VMEM((1, model), f32),
            pltpu.VMEM((heads, model), bf16),
            pltpu.VMEM(bias_in.shape, f32),
            pltpu.VMEM((chunks, LANES), jnp.int32),
            pltpu.VMEM((rows, model), bf16),
            pltpu.VMEM(square, f32),
            pltpu.VMEM((SUB, model), f32),
            pltpu.VMEM(w_out.shape, bf16),
            pltpu.SemaphoreType.DMA((10,)),
            pltpu.SemaphoreType.DMA((4,)),
        ),
        name="project",
    )
    halo = shift(tail, "seq", 1)
    joined = pltpu.VMEM((rows + SUB, width), f32)
    joined_ids = pltpu.VMEM((rows + SUB, LANES), f32)
    maps, mix, back, facts, a_before = kernel_call(
        delta_kernel,
        (
            shaped((2 * heads * HEAD_DIM, HEAD_DIM), bf16),
            shaped((rows + 2 * SUB, 4 * head_width), bf16),
            shaped((rows + 2 * SUB, 2 * width + 4 * head_width), bf16),
            shaped((rows + SUB, head_width + LANES), f32),
            shaped((2 * SUB, model), bf16),
        ),
        chain, p, halo, Held(conv_weight), seg_cols, beta,
        scratch=(joined, joined_ids),
        name="delta",
    )
    half_maps = heads * HEAD_DIM
    w_out_all = gathered(w_out_copy)
    prefix = pack = maps
    for bit in range(rounds - 1):
        other = swap(maps, "seq", 1 << bit)
        if bit == 0:
            back, facts, steps, a_before = park(
                chain, (back, None), (facts, None), (mix, 2 * head_width), (a_before, None), name="park_delta"
            )
        maps, prefix, pack = kernel_call(
            functools.partial(scan_round_kernel, bit),
            (
                shaped((half_maps if bit == rounds - 2 else 2 * half_maps, HEAD_DIM), bf16),
                shaped((2 * half_maps, HEAD_DIM), bf16),
                shaped((2 * half_maps * (bit + 1), HEAD_DIM), bf16),
            ),
            chain, maps, other, prefix, pack,
            name="scan_round",
            )
    other_a = swap(maps, "seq", 1 << (rounds - 1))
    y, mixed, keep_y = kernel_call(
        functools.partial(mixer_kernel, rounds - 1),
        (shaped(square, bf16), shaped(square, f32), shaped((rows, 2 * head_width), bf16)),
        chain, prefix, other_a, mix, Free(gate_raw), hgain_row,
        name="mixer",
    )
    mixed, keep_y, pack = park(
        chain, (mixed, None), (keep_y, None), (pack, None), name="park_mixer"
    )
    y_all = gathered(y)
    half = (rows // 2, model)
    wide = pltpu.VMEM((rows, model), f32)
    ffn_wide = -(-ffn_width // LANES) * LANES
    ffn_axis = 0 if share % LANES else 1
    ffn_whole = (ffn_width, model) if ffn_axis else (model, ffn_wide)
    ffn_half = (ffn_width, model // 2) if ffn_axis else (model // 2, ffn_wide)
    (
        db_send, down_send, gate_send, h, hidden, db_keep, down_keep, gate_keep, grad_up,
    ) = kernel_call(
        functools.partial(ffn_kernel, ffn_axis, down_bits, gate_bits),
        (
            shaped(half, bf16),
            shaped(ffn_half, bf16),
            shaped(ffn_half, bf16),
            Direct((rows, model), f32),
            Direct((rows, ffn_width), bf16),
            Direct(half, bf16),
            Direct(ffn_half, bf16),
            Direct(ffn_half, bf16),
            Direct(ffn_whole, bf16),
        ),
        chain, Free(block_input), Free(cotangent), fgain_row,
        Free(w_ffn_gate.T), Free(w_ffn_up.T), Free(w_ffn_down),
        *y_all, Free(w_out_all[0]), *w_out_all[1:],
        scratch=(
            wide,
            pltpu.VMEM((rows, ffn_width), bf16),
            pltpu.VMEM(half, bf16),
            pltpu.VMEM(ffn_half, bf16),
            pltpu.VMEM(ffn_half, bf16),
            pltpu.VMEM(ffn_whole, bf16),
            pltpu.VMEM(ffn_whole, bf16),
            wide,
            pltpu.SemaphoreType.DMA((6,)),
        ),
        name="ffn",
    )
    down = Shares(Free(down_keep), down_send, down_bits, ffn_axis)
    gate = Shares(Free(gate_keep), gate_send, gate_bits, ffn_axis)
    head_bits = [1 << bit for bit in range(1, lax.axis_size("head").bit_length() - 1)]
    pre = dk_part = gq = q_halo = q_small = q_share = None
    conv_scratch = (
        pltpu.VMEM((rows + 2 * SUB, LANES), f32),
        pltpu.VMEM((taps - 1, rows + 2 * SUB, LANES), f32),
    )
    step_bits = list(range(rounds - 1))
    rest_bits = list(project_bits[1:])
    _, small_extra = small_places(model, taps, heads, 2 * head_width)
    mine = out_keep = out_send = gh = pull = dh = d_out = d_gate_raw = sums_a = other = after = up = up_keep = up_send = out_mine = early = early_keep = early_send = gp = gp_halo = grad_small = da = da_edge = head_rows = from_next = keep = send = got = da_keep = da_send = block_output = input_grad = out_share = w_gate_share = down_share = ffn_gate_share = ffn_up_share = None

    def db_core():
        nonlocal mine
        mine = added(chain, Held(db_keep), swap(db_send, "head", 1))

    def out_part():
        nonlocal out_keep, out_send
        out_keep, out_send = kernel_call(
            out_part_kernel,
            (shaped(half, bf16), shaped(half, bf16)),
            chain, Held(hidden), Held(w_ffn_down),
            scratch=(wide,),
            name="out_part",
        )

    def db_far():
        nonlocal mine
        for bit in head_bits:
            mine = added(chain, mine, swap(mine, "head", bit))

    def residual_back():
        nonlocal gh, pull, dh, d_out, d_gate_raw, sums_a, other
        gh, pull, dh, d_out, d_gate_raw, sums_a = kernel_call(
            residual_back_kernel,
            (
                shaped((rows, model), bf16),
                shaped((half_maps, HEAD_DIM), bf16),
                shaped((rows, model), f32),
                shaped(square, bf16),
                shaped(square, bf16),
                shaped((SUB, model), f32),
            ),
            chain, mine, swap(mine, "head", 1), Free(h), Free(cotangent), fgain_row, Free(w_out), Free(mixed),
            Free(gate_raw), hgain_row, Free(steps),
            scratch=(wide,),
            name="residual_back",
        )
        other = swap(pull, "seq", 1)

    def park_back():
        nonlocal dh, d_out, d_gate_raw, sums_a
        dh, d_out, d_gate_raw, sums_a = park(
            chain, (dh, None), (d_out, None), (d_gate_raw, None), (sums_a, None), name="park_residual"
        )

    def down_one():
        down.step(chain)

    def gate_one():
        gate.step(chain)

    def scan_back():
        nonlocal pull, other, after

        bit = step_bits.pop(0)
        pull, after = kernel_call(
            functools.partial(back_round_kernel, bit),
            (shaped(pull.shape, bf16), shaped(pull.shape, bf16)),
            chain, Free(pack), pull, other, pull if after is None else after,
            name="back_round",
        )
        other = swap(pull, "seq", 2 << bit)

    def scan_rest():
        while step_bits:
            scan_back()

    def up_blocks():
        nonlocal up, up_keep, up_send
        up_keep, up_send = kernel_call(
            functools.partial(emit_kernel, ffn_axis, up_bits),
            (shaped(ffn_half, bf16), shaped(ffn_half, bf16)),
            chain, Free(grad_up),
            name="up_blocks",
        )
        up = Shares(up_keep, up_send, up_bits, ffn_axis)

    def out_core():
        nonlocal out_mine
        out_mine = added(chain, out_keep, swap(out_send, "head", 1))

    def delta_query():
        nonlocal pre, dk_part, gq, q_halo, q_small
        pre, dk_part, gq, q_halo, q_small = kernel_call(
            delta_query_kernel,
            (
                shaped((rows, 2 * head_width), bf16),
                shaped(square, f32),
                stored(square, f32),
                stored((SUB, head_width), f32),
                stored((-(-taps // SUB) * SUB, head_width), f32),
            ),
            chain, taps_in, Free(back), Free(facts), Free(keep_y), Free(d_out),
            scratch=(joined, joined_ids, pltpu.VMEM(square, f32)) + conv_scratch,
            name="delta_query",
        )

    def early_grads():
        nonlocal early
        early_keep, early_send = kernel_call(
            functools.partial(early_grads_kernel, early_bits),
            (shaped((model // 2, width), bf16), shaped((model // 2, width), bf16)),
            chain, gh, Free(keep_y), Free(a), Free(d_gate_raw), Held(gq), Held(q_halo), Held(a_before),
            scratch=(pltpu.VMEM((model, width), bf16),),
            name="early_grads",
        )
        early = Shares(early_keep, early_send, early_bits)

    def down_two():
        down.until(chain, 0)

    def gate_two():
        gate.until(chain, 0)

    def out_far():
        nonlocal out_mine
        for bit in head_bits:
            out_mine = added(chain, out_mine, swap(out_mine, "head", bit))

    def delta_back():
        nonlocal gp, gp_halo, grad_small
        gp, gp_halo, grad_small = kernel_call(
            functools.partial(delta_back_kernel, rounds - 1),
            (
                shaped((rows, 2 * head_width + LANES), f32),
                shaped((SUB, 2 * head_width), f32),
                stored((-(-(2 * taps + 1) // SUB) * SUB, head_width), f32),
            ),
            chain, taps_in, Free(back), Free(facts), Free(steps), Free(keep_y), Free(d_out),
            pre, dk_part, Free(pack), after, other,
            scratch=(joined, joined_ids, pltpu.VMEM((rows, 2 * head_width), f32)) + conv_scratch,
            name="delta_back",
        )

    def input_back():
        nonlocal da, da_edge, head_rows, from_next
        da, da_edge, head_rows = kernel_call(
            input_back_kernel,
            (shaped((rows, model), f32), shaped((SUB, model), f32), shaped((SUB, model), f32)),
            chain, gp, gp_halo, Free(gq), Free(q_halo), Free(d_gate_raw),
            Free(w_query), Free(w_key), Free(w_value), Free(w_gate), Free(w_beta8), Free(block_input),
            gain_row, Free(a_before), Free(sums_a),
            name="input_back",
        )
        from_next = shift(da_edge, "seq", -1)

    def up_one():
        up.step(chain)

    def rows_core():
        nonlocal head_rows
        head_rows = added(chain, head_rows, swap(head_rows, "head", 1))

    def rows_far():
        nonlocal head_rows
        for bit in head_bits:
            head_rows = added(chain, head_rows, swap(head_rows, "head", bit))

    def project_grads():
        nonlocal keep, send, got
        keep, send = kernel_call(
            functools.partial(project_grads_kernel, project_bits, taps),
            (
                shaped((model // 2 + small_extra, 2 * head_width), bf16),
                shaped((model // 2 + small_extra, 2 * head_width), bf16),
            ),
            chain, Free(a), Free(a_before), gp, gp_halo, Free(sums_a), Held(q_small), Free(grad_small), head_rows,
            scratch=(pltpu.VMEM((model, 2 * head_width), bf16), pltpu.VMEM((small_extra, 2 * head_width), f32)),
            name="project_grads",
        )
        got = swap(send, "seq", 1 << project_bits[0])

    def input_split():
        nonlocal da_keep, da_send
        da_keep, da_send = kernel_call(
            input_split_kernel,
            (shaped(half, bf16), shaped(half, bf16)),
            chain, da, from_next,
            scratch=(wide,),
            name="input_split",
        )

    def early_one():
        early.step(chain)

    def up_two():
        up.until(chain, 0)

    def da_core():
        nonlocal mine
        mine = added(chain, da_keep, swap(da_send, "head", 1))

    def da_far():
        nonlocal mine
        for bit in head_bits:
            mine = added(chain, mine, swap(mine, "head", bit))

    def output():
        nonlocal block_output
        (block_output,) = kernel_call(
            output_kernel,
            (final((rows, model), bf16),),
            chain, out_mine, swap(out_mine, "head", 1), Free(h),
            scratch=(wide,),
            name="output",
        )

    def input_grad():
        nonlocal input_grad
        (input_grad,) = kernel_call(
            input_grad_kernel,
            (final((rows, model), f32),),
            chain, mine, swap(mine, "head", 1), Free(block_input), gain_row, Free(dh),
            scratch=(wide,),
            name="input_grad",
        )

    def share_one():
        nonlocal keep, send, got

        shape = ((keep.shape[0] - small_extra) // 2 + small_extra, 2 * head_width)
        keep, send = kernel_call(
            share_small_kernel,
            (shaped(shape, bf16), shaped(shape, bf16)),
            chain, keep, got,
            name="share_small",
        )
        got = swap(send, "seq", 1 << rest_bits.pop(0))

    def share_two():
        while rest_bits:
            share_one()

    def early_two():
        early.until(chain, 0)

    def down_out():
        nonlocal down_share
        (down_share,) = ffn_share(chain, down.pair(chain))

    def up_out():
        nonlocal ffn_up_share
        (ffn_up_share,) = ffn_share(chain, up.pair(chain))

    def gate_out():
        nonlocal ffn_gate_share
        (ffn_gate_share,) = ffn_share(chain, gate.pair(chain))

    def early_out():
        nonlocal out_share, w_gate_share, q_share
        out_share, w_gate_share, q_share = kernel_call(
            early_sum_kernel,
            (
                final((head_width, share), f32),
                final((share, head_width), f32),
                final((share, head_width), f32),
            ),
            chain, *early.pair(chain), name="early_sum",
        )

    parts = (
        db_core,
        out_part,
        db_far,
        residual_back,
        park_back,
        down_one,
        gate_one,
        scan_back,
        up_blocks,
        out_core,
        scan_rest,
        delta_query,
        early_grads,
        down_two,
        gate_two,
        out_far,
        delta_back,
        input_back,
        up_one,
        rows_core,
        input_split,
        rows_far,
        project_grads,
        up_two,
        early_one,
        da_core,
        output,
        down_out,
        share_one,
        early_two,
        up_out,
        da_far,
        input_grad,
        share_two,
        early_out,
        gate_out,
    )
    by_name = {part.__name__: part for part in parts}
    for name in ORDER:
        by_name[name]()
    beta_shape = (heads, model if share % LANES else share)
    (
        k_share, v_share, norm_total, head_gain_total, ffn_gain_total, conv_total, beta_rows,
        bias_total,
    ) = kernel_call(
        functools.partial(project_sum_kernel, taps),
        tuple(final((share, head_width), f32) for _ in range(2))
        + (
            final((1, model), f32),
            final((1, LANES), f32),
            final((1, model), f32),
            final(conv_weight.shape, f32),
            final(beta_shape, f32),
            final((1, heads), f32),
        ),
        chain, keep, got,
        scratch=(
            pltpu.VMEM((small_extra, 2 * head_width), f32),
            pltpu.VMEM((-(-heads * model // LANES // SUB) * SUB, LANES), f32),
        ),
        name="project_sum",
    )
    if share % LANES:
        beta_rows = lax.dynamic_slice(beta_rows, (0, lax.axis_index("seq") * share), (heads, share))
    beta_share = beta_rows.T
    return (
        block_output,
        input_grad,
        norm_total[0],
        q_share,
        k_share,
        v_share,
        w_gate_share,
        beta_share,
        bias_total[0],
        conv_total,
        head_gain_total[0],
        out_share,
        ffn_gain_total[0],
        ffn_gate_share.T,
        ffn_up_share.T,
        down_share,
    )


def solution(mesh):
    return jax.shard_map(
        body,
        mesh=mesh,
        in_specs=(
            P("seq", None), P("seq", None), P("seq"), P(),
            P(None, "head"), P(None, "head"), P(None, "head"), P(None, "head"), P(None, "head"),
            P("head"), P(None, None, "head"), P(), P("head", None), P(),
            P(None, "head"), P(None, "head"), P("head", None),
        ),
        out_specs=(
            P("seq", None), P("seq", None), P(),
            P("seq", "head"), P("seq", "head"), P("seq", "head"), P("seq", "head"), P("seq", "head"),
            P("head"), P(None, None, "head"), P(), P("head", "seq"), P(),
            P("seq", "head"), P("seq", "head"), P("head", "seq"),
        ),
        check_vma=False,
    )
```
